32 devices in a mesh: dp: 8 (over z, y), mp: 4 (over x, core).
Axes of the slice: x: 2, y: 2, z: 4, core: 2. Of those that a mesh axis runs over, the one named last changes fastest.
Arguments:
- feats: bfloat16 [19456, 384], P('dp'), may hold values from -6 to 6
- centres: float32 [3, 19456], P(None, 'dp'), may hold values from -5 to 5
- counts: int32 [512], P('dp'), may hold values from 13 to 38, as said below
- cotangent: bfloat16 [19456, 384], P('dp'), may hold values from -6 to 6
- qkv_weight: float32 [3, 384, 512], P(None, 'dp', 'mp'), may hold values from -0.3125 to 0.3125
- out_weight: float32 [512, 384], P('mp', 'dp'), may hold values from -1.5 to 1.5
- up_weight: float32 [384, 1536], P('dp', 'mp'), may hold values from -0.3125 to 0.3125
- up_bias: float32 [1536], P('mp'), may hold values from -1 to 1
- down_weight: float32 [1536, 384], P('mp', 'dp'), may hold values from -0.15625 to 0.15625
- norm_vectors: float32 [7, 384], replicated, may hold values from -1 to 1.5, as said below
- pos_hidden: float32 [4, 128], replicated, may hold values from -3.5 to 3.5
- pos_proj: float32 [128, 384], replicated, may hold values from -0.5 to 0.5
- qkv_moment: float32 [3, 384, 512], P(None, 'dp', 'mp'), may hold values from -0.00390625 to 0.00390625
- out_moment: float32 [512, 384], P('mp', 'dp'), may hold values from -0.00390625 to 0.00390625
- up_moment: float32 [384, 1536], P('dp', 'mp'), may hold values from -0.00390625 to 0.00390625
- bias_moment: float32 [1536], P('mp'), may hold values from -0.00390625 to 0.00390625
- down_moment: float32 [1536, 384], P('mp', 'dp'), may hold values from -0.00390625 to 0.00390625
- vector_moment: float32 [7, 384], replicated, may hold values from -0.00390625 to 0.00390625
- hidden_moment: float32 [4, 128], replicated, may hold values from -0.00390625 to 0.00390625
- proj_moment: float32 [128, 384], replicated, may hold values from -0.00390625 to 0.00390625
- qkv_second: float32 [3, 384, 512], P(None, 'dp', 'mp'), may hold values from 4.9505735e-07 to 1.9802294e-06
- out_second: float32 [512, 384], P('mp', 'dp'), may hold values from 4.9505735e-07 to 1.9802294e-06
- up_second: float32 [384, 1536], P('dp', 'mp'), may hold values from 4.9505735e-07 to 1.9802294e-06
- bias_second: float32 [1536], P('mp'), may hold values from 4.9505735e-07 to 1.9802294e-06
- down_second: float32 [1536, 384], P('mp', 'dp'), may hold values from 4.9505735e-07 to 1.9802294e-06
- vector_second: float32 [7, 384], replicated, may hold values from 4.9505735e-07 to 1.9802294e-06
- hidden_second: float32 [4, 128], replicated, may hold values from 4.9505735e-07 to 1.9802294e-06
- proj_second: float32 [128, 384], replicated, may hold values from 4.9505735e-07 to 1.9802294e-06
Outputs:
- block_out: bfloat16 [19456, 384], P(('dp', 'mp'))
- feats_grad: float32 [19456, 384], P(('dp', 'mp'))
- clip_norm: float32 [], replicated
- trust_norms: float32 [2, 14], replicated
- qkv_weight_grad: float32 [3, 384, 512], P(None, 'dp', 'mp')
- qkv_weight_new: float32 [3, 384, 512], P(None, 'dp', 'mp')
- qkv_moment_new: float32 [3, 384, 512], P(None, 'dp', 'mp')
- qkv_second_new: float32 [3, 384, 512], P(None, 'dp', 'mp')
- qkv_weight_copy: bfloat16 [3, 384, 512], P(None, 'dp', 'mp')
- out_weight_grad: float32 [512, 384], P('mp', 'dp')
- out_weight_new: float32 [512, 384], P('mp', 'dp')
- out_moment_new: float32 [512, 384], P('mp', 'dp')
- out_second_new: float32 [512, 384], P('mp', 'dp')
- out_weight_copy: bfloat16 [512, 384], P('mp', 'dp')
- up_weight_grad: float32 [384, 1536], P('dp', 'mp')
- up_weight_new: float32 [384, 1536], P('dp', 'mp')
- up_moment_new: float32 [384, 1536], P('dp', 'mp')
- up_second_new: float32 [384, 1536], P('dp', 'mp')
- up_weight_copy: bfloat16 [384, 1536], P('dp', 'mp')
- up_bias_grad: float32 [1536], P('mp')
- up_bias_new: float32 [1536], P('mp')
- bias_moment_new: float32 [1536], P('mp')
- bias_second_new: float32 [1536], P('mp')
- up_bias_copy: bfloat16 [1536], P('mp')
- down_weight_grad: float32 [1536, 384], P('mp', 'dp')
- down_weight_new: float32 [1536, 384], P('mp', 'dp')
- down_moment_new: float32 [1536, 384], P('mp', 'dp')
- down_second_new: float32 [1536, 384], P('mp', 'dp')
- down_weight_copy: bfloat16 [1536, 384], P('mp', 'dp')
- norm_vectors_grad: float32 [7, 384], replicated
- norm_vectors_new: float32 [7, 384], replicated
- vector_moment_new: float32 [7, 384], replicated
- vector_second_new: float32 [7, 384], replicated
- norm_vectors_copy: bfloat16 [7, 384], replicated
- pos_hidden_grad: float32 [4, 128], replicated
- pos_hidden_new: float32 [4, 128], replicated
- hidden_moment_new: float32 [4, 128], replicated
- hidden_second_new: float32 [4, 128], replicated
- pos_hidden_copy: bfloat16 [4, 128], replicated
- pos_proj_grad: float32 [128, 384], replicated
- pos_proj_new: float32 [128, 384], replicated
- proj_moment_new: float32 [128, 384], replicated
- proj_second_new: float32 [128, 384], replicated
- pos_proj_copy: bfloat16 [128, 384], replicated
The draws below stay inside these ranges and needn't reach their ends.
Inputs may be any that keep to these rules, and one draw needn't show every extreme that they name: `counts`: among the clouds of each index of dp, one has exactly 38 visible patches and another exactly 13. `norm_vectors`: gains of the two norms and the biases of the layer.
All inputs are finite; a program needn't handle non-finite values.
Results may differ from the reference program's by a relative error of at most 0.011.
Values may be sent and summed in bfloat16 or wider, within the bound.
A program may use at most 128 MiB of HBM per device.

```python
import math
import jax
import jax.numpy as jnp
from jax import lax

D = 384
HD = 64
FF = 1536
PH = 128
HEAD_SLOTS = 8
PAD = 38
VIS_MIN = 13
BLOCK_CLOUDS = 16
C_DEV = 64
SLOTW = 512
CLOUDS = 512
TOKENS = 19456
PARAMS = 2019968
N_MP = 4


def draw_counts(key, part):
    groups = CLOUDS // C_DEV
    base = jax.random.randint(jax.random.fold_in(key, 11), (groups, C_DEV), VIS_MIN, PAD + 1)
    highest_pick = jax.random.randint(jax.random.fold_in(key, 12), (groups, 1), 0, C_DEV)
    offset = jax.random.randint(jax.random.fold_in(key, 13), (groups, 1), 1, C_DEV)
    lowest_pick = (highest_pick + offset) % C_DEV
    column = jnp.arange(C_DEV)[None, :]
    table = jnp.where(column == highest_pick, PAD, jnp.where(column == lowest_pick, VIS_MIN, base))
    return table.reshape(CLOUDS).astype(jnp.int32)


def draw_norm_vectors(key, part):
    noise = jnp.clip(jax.random.normal(key, (7, D), jnp.float32), -5.0, 5.0)
    row_ids = jnp.arange(7)[:, None]
    return jnp.where(row_ids < 2, 1.0 + 0.1 * noise, 0.2 * noise).astype(jnp.float32)


def shard_levels(own_key, extent, cuts, least, largest):
    factor_of, own = 1.0, jax.random.fold_in(own_key, 6)
    for dim, shards_of in cuts:
        heights = jnp.exp(jax.random.uniform(jax.random.fold_in(own, dim), (shards_of,), jnp.float32, least / len(cuts), largest / len(cuts)))
        factor_of = factor_of * jnp.repeat(heights, extent[dim] // shards_of).reshape([-1 if axis == dim else 1 for axis in range(len(extent))])
    return factor_of


def bell_draw(key, shape, width, bound, shards=(), kind=jnp.bfloat16):
    entries = width * jax.random.normal(key, shape, jnp.float32)
    if shards:
        entries = entries * shard_levels(key, shape, shards, -0.22, 0.18)
    return jnp.clip(entries, -bound, bound).astype(kind)


def setup_inputs(seed: int = 0) -> dict:
    arg_keys = jax.random.split(jax.random.key(seed), 29)
    return {
        "feats": bell_draw(arg_keys[0], (TOKENS, D), 1.0, 6.0, ((0, 8),)),
        "centres": bell_draw(arg_keys[1], (3, TOKENS), 1.0, 5.0, ((1, 8),), jnp.float32),
        "counts": draw_counts(jax.random.fold_in(arg_keys[28], 71), 0),
        "cotangent": bell_draw(arg_keys[3], (TOKENS, D), 1.0, 6.0, ((0, 8),)),
        "qkv_weight": bell_draw(arg_keys[4], (3, D, SLOTW), D ** -0.5, 0.3125, ((1, 8), (2, 4)), jnp.float32),
        "out_weight": bell_draw(arg_keys[5], (SLOTW, D), (HEAD_SLOTS * HD // 32) ** -0.5, 1.5, ((0, 4), (1, 8)), jnp.float32),
        "up_weight": bell_draw(arg_keys[6], (D, FF), D ** -0.5, 0.3125, ((0, 8), (1, 4)), jnp.float32),
        "up_bias": bell_draw(arg_keys[7], (FF,), 0.2, 1.0, ((0, 4),), jnp.float32),
        "down_weight": bell_draw(arg_keys[8], (FF, D), FF ** -0.5, 0.15625, ((0, 4), (1, 8)), jnp.float32),
        "norm_vectors": draw_norm_vectors(jax.random.fold_in(arg_keys[28], 71), 0),
        "pos_hidden": bell_draw(arg_keys[10], (4, PH), 3 ** -0.5, 3.5, (), jnp.float32),
        "pos_proj": bell_draw(arg_keys[11], (PH, D), PH ** -0.5, 0.5, (), jnp.float32),
        "qkv_moment": bell_draw(arg_keys[12], (3, D, SLOTW), (PARAMS ** -0.5), 0.00390625, ((1, 8), (2, 4)), jnp.float32),
        "out_moment": bell_draw(arg_keys[13], (SLOTW, D), (PARAMS ** -0.5), 0.00390625, ((0, 4), (1, 8)), jnp.float32),
        "up_moment": bell_draw(arg_keys[14], (D, FF), (PARAMS ** -0.5), 0.00390625, ((0, 8), (1, 4)), jnp.float32),
        "bias_moment": bell_draw(arg_keys[15], (FF,), (PARAMS ** -0.5), 0.00390625, ((0, 4),), jnp.float32),
        "down_moment": bell_draw(arg_keys[16], (FF, D), (PARAMS ** -0.5), 0.00390625, ((0, 4), (1, 8)), jnp.float32),
        "vector_moment": bell_draw(arg_keys[17], (7, D), (PARAMS ** -0.5), 0.00390625, (), jnp.float32),
        "hidden_moment": bell_draw(arg_keys[18], (4, PH), (PARAMS ** -0.5), 0.00390625, (), jnp.float32),
        "proj_moment": bell_draw(arg_keys[19], (PH, D), (PARAMS ** -0.5), 0.00390625, (), jnp.float32),
        "qkv_second": jnp.clip(jnp.exp(math.log(1.9802293991233455e-06) - 1.3862944 * jax.random.uniform(arg_keys[20], (3, D, SLOTW), jnp.float32) ** shard_levels(arg_keys[20], (3, D, SLOTW), ((1, 8), (2, 4)), -0.2, 0.2)), 4.950573497808364e-07, 1.9802293991233455e-06),
        "out_second": jnp.clip(jnp.exp(math.log(1.9802293991233455e-06) - 1.3862944 * jax.random.uniform(arg_keys[21], (SLOTW, D), jnp.float32) ** shard_levels(arg_keys[21], (SLOTW, D), ((0, 4), (1, 8)), -0.2, 0.2)), 4.950573497808364e-07, 1.9802293991233455e-06),
        "up_second": jnp.clip(jnp.exp(math.log(1.9802293991233455e-06) - 1.3862944 * jax.random.uniform(arg_keys[22], (D, FF), jnp.float32) ** shard_levels(arg_keys[22], (D, FF), ((0, 8), (1, 4)), -0.2, 0.2)), 4.950573497808364e-07, 1.9802293991233455e-06),
        "bias_second": jnp.clip(jnp.exp(math.log(1.9802293991233455e-06) - 1.3862944 * jax.random.uniform(arg_keys[23], (FF,), jnp.float32) ** shard_levels(arg_keys[23], (FF,), ((0, 4),), -0.2, 0.2)), 4.950573497808364e-07, 1.9802293991233455e-06),
        "down_second": jnp.clip(jnp.exp(math.log(1.9802293991233455e-06) - 1.3862944 * jax.random.uniform(arg_keys[24], (FF, D), jnp.float32) ** shard_levels(arg_keys[24], (FF, D), ((0, 4), (1, 8)), -0.2, 0.2)), 4.950573497808364e-07, 1.9802293991233455e-06),
        "vector_second": jnp.clip(jnp.exp(jax.random.uniform(arg_keys[25], (7, D), jnp.float32, math.log(4.950573497808364e-07), math.log(1.9802293991233455e-06))), 4.950573497808364e-07, 1.9802293991233455e-06),
        "hidden_second": jnp.clip(jnp.exp(jax.random.uniform(arg_keys[26], (4, PH), jnp.float32, math.log(4.950573497808364e-07), math.log(1.9802293991233455e-06))), 4.950573497808364e-07, 1.9802293991233455e-06),
        "proj_second": jnp.clip(jnp.exp(jax.random.uniform(arg_keys[27], (PH, D), jnp.float32, math.log(4.950573497808364e-07), math.log(1.9802293991233455e-06))), 4.950573497808364e-07, 1.9802293991233455e-06),
    }


@jax.custom_vjp
def low(v):
    return lax.optimization_barrier(v.astype(jnp.bfloat16)).astype(jnp.float32)

@jax.custom_vjp
def low_back(v):
    return v

def low_keep(v):
    return (low(v), None)

def low_pass(kept, grad):
    return (grad,)

def back_keep(v):
    return (v, None)

def back_low(kept, grad):
    return (low(grad),)
low.defvjp(low_keep, low_pass)
low_back.defvjp(back_keep, back_low)
norm_eps = 1e-05
beta_one = 0.5
beta_two = 0.5
adam_eps = 1e-06
decay_rate = 0.01
learn_rate = 0.3
clip_max = 1.0
step_count = 3.0
neg_fill = -1e+30
highest = lax.Precision.HIGHEST

def layer_norm(values, gain, shift):
    centre = values - lax.optimization_barrier(jnp.mean(values, axis=-1, keepdims=True))
    spread = lax.optimization_barrier(jnp.mean(centre * centre, axis=-1, keepdims=True))
    return centre * lax.rsqrt(spread + norm_eps) * gain + shift

def gelu_exact(values):
    return 0.5 * values * (1.0 + lax.erf(values * 0.7071067811865476))

def piece_squares(array, tensor_index):
    if tensor_index == 5:
        return lax.optimization_barrier(jnp.sum(array * array, axis=1))
    return jnp.sum(array * array)[None]

def piece_ratio(trust_ratio, tensor_index):
    if tensor_index < 5:
        return trust_ratio[tensor_index]
    if tensor_index == 5:
        return trust_ratio[5:12][:, None]
    return trust_ratio[tensor_index + 6]

def reference(feats, centres, counts, cotangent, qkv_weight, out_weight, up_weight, up_bias, down_weight, norm_vectors, pos_hidden, pos_proj, qkv_moment, out_moment, up_moment, bias_moment, down_moment, vector_moment, hidden_moment, proj_moment, qkv_second, out_second, up_second, bias_second, down_second, vector_second, hidden_second, proj_second):
    keep_rows = (jnp.arange(PAD)[None, :] < counts[:, None]).reshape(-1).astype(jnp.float32)
    slot_ids = jnp.arange(HEAD_SLOTS)
    live = ((slot_ids % 2 == 0) | (slot_ids // 2 < N_MP // 2)).astype(jnp.float32)
    col_keep = jnp.repeat(live, HD)
    row_total = keep_rows.shape[0]
    block_rows = BLOCK_CLOUDS * PAD
    block_count = row_total // block_rows
    score_scale = 1.0 / math.sqrt(HD)
    cloud_ids = jnp.arange(block_rows) // PAD
    same_cloud = cloud_ids[:, None] == cloud_ids[None, :]

    @jax.checkpoint
    def attend(parts):
        query, keys, values, keep = parts
        raw = jnp.einsum('qsd,ksd->sqk', query, keys, precision=highest)
        scores = low_back(raw * score_scale)
        allowed = same_cloud & (keep[None, :] > 0.5)
        scores = jnp.where(allowed[None], scores, neg_fill)
        top = lax.optimization_barrier(jnp.max(scores, axis=-1, keepdims=True))
        expo = jnp.exp(scores - top)
        probs = expo / lax.optimization_barrier(jnp.sum(expo, axis=-1, keepdims=True))
        return jnp.einsum('sqk,ksd->qsd', low(probs), values, precision=highest)

    def forward(feat_full, qkv_full, out_full, up_full, bias_full, down_full, vector_full, hidden_full, proj_full):
        pre_pos = jnp.dot(centres.T, hidden_full[:3], precision=highest) + hidden_full[3]
        hidden_pos = low(gelu_exact(pre_pos))
        stream_in = feat_full + (low_back(jnp.dot(hidden_pos, low(proj_full), precision=highest)) + vector_full[6])
        normed_one = low(layer_norm(stream_in, vector_full[0], vector_full[2]))
        qkv_low = low(qkv_full) * col_keep
        projected = low_back(low(jnp.einsum('rd,tdc->trc', normed_one, qkv_low, precision=highest)))
        heads_view = projected.reshape(3, block_count, block_rows, HEAD_SLOTS, HD)
        mixed = lax.map(attend, (heads_view[0], heads_view[1], heads_view[2], keep_rows.reshape(block_count, block_rows)))
        attn_low = low_back(low(mixed.reshape(row_total, HEAD_SLOTS * HD)))
        middle = stream_in + low_back(jnp.dot(attn_low, low(out_full), precision=highest)) + vector_full[4]
        normed_two = low(layer_norm(middle, vector_full[1], vector_full[3]))
        pre_up = low_back(jnp.dot(normed_two, low(up_full), precision=highest) + bias_full)
        activated = low(gelu_exact(pre_up))
        top_out = middle + jnp.dot(activated, low(down_full), precision=highest) + vector_full[5]
        return top_out * keep_rows[:, None]
    weights = [qkv_weight, out_weight, up_weight, up_bias, down_weight, norm_vectors, pos_hidden, pos_proj]
    moments = [qkv_moment, out_moment, up_moment, bias_moment, down_moment, vector_moment, hidden_moment, proj_moment]
    seconds = [qkv_second, out_second, up_second, bias_second, down_second, vector_second, hidden_second, proj_second]
    primal = tuple([feats.astype(jnp.float32)] + weights)
    result, pullback = jax.vjp(forward, *primal)
    grads_all = pullback(cotangent.astype(jnp.float32))
    feats_grad = grads_all[0]
    grads = list(grads_all[1:])
    grad_total = jnp.zeros((), jnp.float32)
    for tensor_index in range(8):
        grad_total = grad_total + jnp.sum(grads[tensor_index] * grads[tensor_index])
    clip_norm = jnp.sqrt(grad_total)
    factor = jnp.minimum(1.0, clip_max / (clip_norm + 1e-06))
    clipped_list = []
    moment_list = []
    second_list = []
    direction_list = []
    weight_square = []
    update_square = []
    for tensor_index in range(8):
        clipped = grads[tensor_index] * factor
        moment_new = beta_one * moments[tensor_index] + (1.0 - beta_one) * clipped
        second_new = beta_two * seconds[tensor_index] + (1.0 - beta_two) * clipped * clipped
        direction = moment_new / (1.0 - beta_one ** step_count) / (jnp.sqrt(second_new / (1.0 - beta_two ** step_count)) + adam_eps) + decay_rate * weights[tensor_index]
        clipped_list.append(clipped)
        moment_list.append(moment_new)
        second_list.append(second_new)
        direction_list.append(direction)
        weight_square.append(piece_squares(weights[tensor_index], tensor_index))
        update_square.append(piece_squares(direction, tensor_index))
    weight_norm = jnp.sqrt(jnp.concatenate(weight_square))
    update_norm = jnp.sqrt(jnp.concatenate(update_square))
    trust_ratio = weight_norm / (update_norm + 1e-06)
    trust_norms = jnp.stack((weight_norm, update_norm))
    outputs = [result.astype(jnp.bfloat16), feats_grad, clip_norm, trust_norms]
    for tensor_index in range(8):
        new_weight = weights[tensor_index] - learn_rate * piece_ratio(trust_ratio, tensor_index) * direction_list[tensor_index]
        outputs.append(clipped_list[tensor_index])
        outputs.append(new_weight)
        outputs.append(moment_list[tensor_index])
        outputs.append(second_list[tensor_index])
        outputs.append(new_weight.astype(jnp.bfloat16))
    return tuple(outputs)
```

```python
import functools
import math

import jax
import jax.numpy as jnp
from jax import lax
from jax.experimental import pallas as pl
from jax.experimental.pallas import tpu as pltpu
from jax.sharding import PartitionSpec as P

HD = 64
PAD = 38
SLOT = 40
GROUP = 4

norm_eps = 1e-05
beta_one = 0.5
beta_two = 0.5
adam_eps = 1e-06
decay_rate = 0.01
learn_rate = 0.3
clip_max = 1.0
step_count = 3.0
neg_fill = -1e30
highest = lax.Precision.HIGHEST
f32 = jnp.float32
bf16 = jnp.bfloat16

NN = (((1,), (0,)), ((), ()))
NT = (((1,), (1,)), ((), ()))
TN = (((0,), (0,)), ((), ()))


def dot(a, b, dims=NN, precision=None):
    return lax.dot_general(a, b, dims, precision=precision, preferred_element_type=f32)


def gelu_pair(v):
    cdf = 0.5 * (1.0 + lax.erf(v * 0.7071067811865476))
    return v * cdf, cdf + v * jnp.exp(-0.5 * v * v) * 0.3989422804014327


def piece_squares(array, tensor_index):
    if tensor_index == 5:
        return jnp.sum(array * array, axis=1)
    return jnp.sum(array * array)[None]


def piece_ratio(trust_ratio, tensor_index):
    if tensor_index < 5:
        return trust_ratio[tensor_index]
    if tensor_index == 5:
        return trust_ratio[5:12][:, None]
    return trust_ratio[tensor_index + 6]


class Layer:
    def __init__(self, refs, mp, clouds, width, inner):
        self.__dict__.update(refs)
        self.mp = mp
        self.clouds = clouds
        self.width = width
        self.inner = inner
        self.rows = clouds * SLOT
        self.block = GROUP * SLOT
        self.blocks = clouds // GROUP
        self.tile = self.rows // 2 if self.rows % 32 == 0 else self.rows
        self.hid = self.proj_low.shape[0]

    def live(self, j):
        return [h for h in range(2) if (2 * j + h) % 2 == 0 or j < self.mp // 2]

    def spread_rows(self):
        zeros = jnp.zeros((SLOT - PAD, self.width), f32)
        self.stage[...] = self.feats[...].astype(f32)
        for c in range(self.clouds):
            self.stream[pl.ds(SLOT * c, PAD), :] = self.stage[pl.ds(PAD * c, PAD), :]
            self.stream[pl.ds(SLOT * c + PAD, SLOT - PAD), :] = zeros
        self.stage[...] = self.cotangent[...].astype(f32)
        for c in range(self.clouds):
            self.middle_grad[pl.ds(SLOT * c, PAD), :] = self.stage[pl.ds(PAD * c, PAD), :]
            self.middle_grad[pl.ds(SLOT * c + PAD, SLOT - PAD), :] = zeros

    def keep_block(self, b, shape, dim):
        place = lax.broadcasted_iota(jnp.int32, shape, dim)
        bound = jnp.zeros(shape, jnp.int32)
        for i in range(GROUP):
            limit = self.counts[b * GROUP + i] + SLOT * i
            inside = (place >= SLOT * i) & (place < limit)
            bound = jnp.where(inside, 1, bound)
        return bound > 0

    def masks(self):
        n = self.block

        def step(b, carry):
            keys = lax.broadcasted_iota(jnp.int32, (n, n), 0)
            query = lax.broadcasted_iota(jnp.int32, (n, n), 1)
            fill = jnp.full((n, n), neg_fill, f32)
            for i in range(GROUP):
                limit = self.counts[b * GROUP + i] + SLOT * i
                inside = (keys >= SLOT * i) & (keys < limit)
                mine = (query >= SLOT * i) & (query < SLOT * (i + 1))
                fill = jnp.where(inside & mine, 0.0, fill)
            self.mask[b] = fill
            self.keep[pl.ds(b * n, n), :] = jnp.where(self.keep_block(b, (n, 128), 0), 1.0, 0.0)
            return carry

        lax.fori_loop(0, self.blocks, step, 0)

    def norm(self, x):
        centre = x - jnp.mean(x, axis=-1, keepdims=True)
        spread = jnp.mean(centre * centre, axis=-1, keepdims=True)
        rate = lax.rsqrt(spread + norm_eps)
        return centre * rate, rate

    def norm_back(self, grad, hat, rate, gain):
        scaled = grad * gain
        first = jnp.mean(scaled, axis=-1, keepdims=True)
        second = jnp.mean(scaled * hat, axis=-1, keepdims=True)
        return rate * (scaled - first - hat * second)

    def entry(self):
        t = self.tile

        def step(i, carry):
            rows = pl.ds(i * t, t)
            pre = dot(self.points[rows, :], self.pos_hidden[...], NN, highest)
            value, slope = gelu_pair(pre)
            hidden = value.astype(bf16)
            self.pos_slope[rows, :] = slope
            self.hidden[rows, :] = hidden
            term = dot(hidden, self.proj_low[...]) + self.vec[6:7, :]
            x = self.stream[rows, :] + term
            hat, rate = self.norm(x)
            self.stream[rows, :] = x
            self.hat_one[rows, :] = hat
            self.rate_one[rows, :] = jnp.broadcast_to(rate, (t, 128))
            self.normed_one[rows, :] = (hat * self.vec[0:1, :] + self.vec[2:3, :]).astype(bf16)
            return carry

        lax.fori_loop(0, self.rows // t, step, 0)

    def project(self, j):
        w = self.width
        t = self.tile

        def step(i, carry):
            rows = pl.ds(i * t, t)
            self.qkv[j, rows, :] = dot(self.normed_one[rows, :], self.w_qkv(j)).astype(bf16)
            return carry

        lax.fori_loop(0, self.rows // t, step, 0)

    def lanes(self, h, n):
        lane = lax.broadcasted_iota(jnp.int32, (n, 128), 1)
        return (lane < HD) if h == 0 else (lane >= HD)

    def attend(self, j, first):
        n = self.block

        def step(b, carry):
            rows = pl.ds(b * n, n)
            query = self.qkv[j, rows, 0:128] * jnp.asarray(1.0 / math.sqrt(HD), bf16)
            keys = self.qkv[j, rows, 128:256]
            values = self.qkv[j, rows, 256:384]
            zero = jnp.zeros_like(query)
            mixed = jnp.zeros((n, 128), f32)
            for place, h in enumerate(self.live(j)):
                own = self.lanes(h, n)
                scores = dot(keys, jnp.where(own, query, zero), NT) + self.mask[b]
                top = jnp.max(scores, axis=0, keepdims=True)
                expo = jnp.exp(scores - top)
                total = jnp.sum(expo, axis=0, keepdims=True)
                probs = expo / total
                self.probs[first + place, b] = probs
                mixed = jnp.where(own, dot(probs.astype(bf16), values, TN), mixed)
            self.attn_low[j, rows, :] = mixed.astype(bf16)
            return carry

        lax.fori_loop(0, self.blocks, step, 0)

    def middle(self):
        t = self.tile

        def step(i, carry):
            rows = pl.ds(i * t, t)
            x = self.stream[rows, :] + self.vec[4:5, :]
            for j in range(self.mp):
                x = x + dot(self.attn_low[j, rows, :], self.w_out(j), NT)
            hat, rate = self.norm(x)
            self.stream[rows, :] = x
            self.hat_two[rows, :] = hat
            self.rate_two[rows, :] = jnp.broadcast_to(rate, (t, 128))
            self.normed_two[rows, :] = (hat * self.vec[1:2, :] + self.vec[3:4, :]).astype(bf16)
            return carry

        lax.fori_loop(0, self.rows // t, step, 0)

    def feed(self, j):
        t = self.tile

        def step(i, carry):
            rows = pl.ds(i * t, t)
            pre = dot(self.normed_two[rows, :], self.w_up(j)) + self.up_bias[j, 0:1, :]
            value, slope = gelu_pair(pre)
            low = value.astype(bf16)
            self.activated[j, rows, :] = low
            self.slope[j, rows, :] = slope
            self.stream[rows, :] += dot(low, self.w_down(j), NT)
            return carry

        lax.fori_loop(0, self.rows // t, step, 0)

    def top(self):
        t = self.tile

        def step(i, carry):
            rows = pl.ds(i * t, t)
            keep = jnp.concatenate([self.keep[rows, :]] * (self.width // 128), axis=1)
            self.stream[rows, :] = (self.stream[rows, :] + self.vec[5:6, :]) * keep
            grad = self.middle_grad[rows, :] * keep
            self.middle_grad[rows, :] = grad
            self.grad_top[rows, :] = grad.astype(bf16)
            self.vec_grad[5:6, :] += jnp.sum(grad, axis=0, keepdims=True)
            return carry

        self.vec_grad[...] = jnp.zeros_like(self.vec_grad)
        self.up_bias_grad[...] = jnp.zeros_like(self.up_bias_grad)
        lax.fori_loop(0, self.rows // t, step, 0)

    def feed_back(self, j):
        t = self.tile

        def step(i, carry):
            rows = pl.ds(i * t, t)
            grad = dot(self.grad_top[rows, :], self.w_down(j)) * self.slope[j, rows, :]
            low = grad.astype(bf16)
            self.grad_pre[j, rows, :] = low
            self.up_bias_grad[j, 0:1, :] += jnp.sum(low.astype(f32), axis=0, keepdims=True)
            term = dot(low, self.w_up(j), NT)
            if j == 0:
                self.normed_grad[rows, :] = term
            else:
                self.normed_grad[rows, :] += term
            return carry

        lax.fori_loop(0, self.rows // t, step, 0)

    def middle_back(self):
        t = self.tile

        def step(i, carry):
            rows = pl.ds(i * t, t)
            grad, hat = self.normed_grad[rows, :], self.hat_two[rows, :]
            rate = jnp.concatenate([self.rate_two[rows, :]] * (self.width // 128), axis=1)
            self.vec_grad[1:2, :] += jnp.sum(grad * hat, axis=0, keepdims=True)
            self.vec_grad[3:4, :] += jnp.sum(grad, axis=0, keepdims=True)
            out = self.middle_grad[rows, :] + self.norm_back(grad, hat, rate, self.vec[1:2, :])
            self.middle_grad[rows, :] = out
            self.vec_grad[4:5, :] += jnp.sum(out, axis=0, keepdims=True)
            self.middle_low[rows, :] = out.astype(bf16)
            return carry

        lax.fori_loop(0, self.rows // t, step, 0)

    def attend_grad(self, j):
        t = self.tile

        def step(i, carry):
            rows = pl.ds(i * t, t)
            self.attn_grad[j, rows, :] = dot(self.middle_low[rows, :], self.w_out(j)).astype(bf16)
            return carry

        lax.fori_loop(0, self.rows // t, step, 0)

    def attend_back(self, j, first):
        n = self.block

        def step(b, carry):
            rows = pl.ds(b * n, n)
            scale = 1.0 / math.sqrt(HD)
            query = self.qkv[j, rows, 0:128] * jnp.asarray(scale, bf16)
            keys = self.qkv[j, rows, 128:256]
            values = self.qkv[j, rows, 256:384]
            grad_out = self.attn_grad[j, rows, :]
            zero = jnp.zeros_like(query)
            grad_query = jnp.zeros((n, 128), f32)
            grad_keys = jnp.zeros((n, 128), f32)
            grad_values = jnp.zeros((n, 128), f32)
            for place, h in enumerate(self.live(j)):
                own = self.lanes(h, n)
                mine = jnp.where(own, grad_out, zero)
                probs = self.probs[first + place, b]
                grad_probs = dot(values, mine, NT)
                grad_values = grad_values + dot(probs.astype(bf16), mine)
                inner = jnp.sum(probs * grad_probs, axis=0, keepdims=True)
                grad_scores = (probs * (grad_probs - inner)).astype(bf16)
                grad_keys = grad_keys + dot(grad_scores, jnp.where(own, query, zero))
                grad_query = jnp.where(own, dot(grad_scores, keys, TN), grad_query)
            self.grad_proj[j, rows, 0:128] = (grad_query * scale).astype(bf16)
            self.grad_proj[j, rows, 128:256] = grad_keys.astype(bf16)
            self.grad_proj[j, rows, 256:384] = grad_values.astype(bf16)
            return carry

        lax.fori_loop(0, self.blocks, step, 0)

    def entry_back(self):
        t = self.tile

        def step(i, carry):
            rows = pl.ds(i * t, t)
            grad = jnp.zeros((t, self.width), f32)
            for j in range(self.mp):
                grad = grad + dot(self.grad_proj[j, rows, :], self.w_qkv(j), NT)
            hat = self.hat_one[rows, :]
            rate = jnp.concatenate([self.rate_one[rows, :]] * (self.width // 128), axis=1)
            self.vec_grad[0:1, :] += jnp.sum(grad * hat, axis=0, keepdims=True)
            self.vec_grad[2:3, :] += jnp.sum(grad, axis=0, keepdims=True)
            out = self.middle_grad[rows, :] + self.norm_back(grad, hat, rate, self.vec[0:1, :])
            self.middle_grad[rows, :] = out
            self.vec_grad[6:7, :] += jnp.sum(out, axis=0, keepdims=True)
            low = out.astype(bf16)
            self.pos_low[rows, :] = low
            self.pre_grad[rows, :] = dot(low, self.proj_low[...], NT) * self.pos_slope[rows, :]
            return carry

        lax.fori_loop(0, self.rows // t, step, 0)

    def turn(self, source, target):
        n = 128

        def step(i, carry):
            block = source[pl.ds(i * n, n), :].astype(f32)
            target[:, pl.ds(pl.multiple_of(i * n, n), n)] = block.T.astype(bf16)
            return carry

        lax.fori_loop(0, self.rows // n, step, 0)

    def gather_rows(self, source, target):
        for c in range(self.clouds):
            target[pl.ds(PAD * c, PAD), :] = source[pl.ds(SLOT * c, PAD), :]


def layer_scratch(mp, clouds, width, inner, hid):
    rows = clouds * SLOT
    block = GROUP * SLOT
    cols = inner // mp
    heads = mp + mp // 2
    shapes = dict(
        stage=((clouds * PAD, width), f32),
        stream=((rows, width), f32),
        middle_grad=((rows, width), f32),
        mask=((clouds // GROUP, block, block), f32),
        keep=((rows, 128), f32),
        pos_slope=((rows, hid), f32),
        hidden=((rows, hid), bf16),
        hat_one=((rows, width), f32),
        rate_one=((rows, 128), f32),
        normed_one=((rows, width), bf16),
        qkv=((mp, rows, 384), bf16),
        probs=((heads, clouds // GROUP, block, block), f32),
        attn_low=((mp, rows, 128), bf16),
        hat_two=((rows, width), f32),
        rate_two=((rows, 128), f32),
        normed_two=((rows, width), bf16),
        activated=((mp, rows, cols), bf16),
        slope=((mp, rows, cols), f32),
        grad_top=((rows, width), bf16),
        grad_pre=((mp, rows, cols), bf16),
        normed_grad=((rows, width), f32),
        middle_low=((rows, width), bf16),
        attn_grad=((mp, rows, 128), bf16),
        grad_proj=((mp, rows, 384), bf16),
        pos_low=((rows, width), bf16),
        pre_grad=((rows, hid), f32),
        turned=((width, rows), bf16),
    )
    return shapes


def heads_before(mp, j):
    return sum(2 if i < mp // 2 else 1 for i in range(j))


def compute_kernel(names, mp, clouds, width, inner, *args):
    refs = dict(zip(names, args))
    layer = Layer(refs, mp, clouds, width, inner)
    w = layer.w
    cols = inner // mp
    layer.w_qkv = lambda j: w[j, :, 0:384]
    layer.w_out = lambda j: w[j, :, 384:512]
    layer.w_up = lambda j: w[j, :, 512 : 512 + cols]
    layer.w_down = lambda j: w[j, :, 512 + cols : 512 + 2 * cols]
    layer.proj_low[...] = layer.pos_proj[...].astype(bf16)
    layer.spread_rows()
    layer.masks()
    layer.entry()
    for j in range(mp):
        layer.project(j)
        layer.attend(j, heads_before(mp, j))
    layer.middle()
    for j in range(mp):
        layer.feed(j)
    layer.top()
    layer.gather_rows(layer.stream, layer.stage)
    layer.block_out[...] = layer.stage[...].astype(bf16)
    for j in range(mp):
        layer.feed_back(j)
    g = layer.grads
    layer.turn(layer.grad_top, layer.turned)
    for j in range(mp):
        g[j, :, 512 + cols : 512 + 2 * cols] = dot(layer.turned[...], layer.activated[j])
    layer.turn(layer.normed_two, layer.turned)
    for j in range(mp):
        g[j, :, 512 : 512 + cols] = dot(layer.turned[...], layer.grad_pre[j])
    layer.middle_back()
    layer.turn(layer.middle_low, layer.turned)
    for j in range(mp):
        g[j, :, 384:512] = dot(layer.turned[...], layer.attn_low[j])
        layer.attend_grad(j)
        layer.attend_back(j, heads_before(mp, j))
    layer.turn(layer.normed_one, layer.turned)
    for j in range(mp):
        g[j, :, 0:384] = dot(layer.turned[...], layer.grad_proj[j])
    layer.entry_back()
    layer.gather_rows(layer.middle_grad, layer.feats_grad)
    layer.proj_grad[...] = dot(layer.hidden[...], layer.pos_low[...], TN)
    layer.pos_grad[...] = dot(layer.points[...], layer.pre_grad[...], TN, highest)


def compute(mp, width, inner, counts, feats, cotangent, points, w, up_bias, vec, pos_hidden, pos_proj):
    clouds = counts.shape[0]
    hid = pos_proj.shape[0]
    inputs = ["counts", "feats", "cotangent", "points", "w", "up_bias", "vec", "pos_hidden", "pos_proj"]
    outs = dict(
        block_out=((clouds * PAD, width), bf16),
        feats_grad=((clouds * PAD, width), f32),
        grads=(w.shape, f32),
        up_bias_grad=((mp, 8, inner // mp), f32),
        vec_grad=((8, width), f32),
        pos_grad=((8, hid), f32),
        proj_grad=((hid, width), f32),
    )
    scratch = layer_scratch(mp, clouds, width, inner, hid)
    scratch["proj_low"] = ((hid, width), bf16)
    names = inputs + list(outs) + list(scratch)
    vmem = pl.BlockSpec(memory_space=pltpu.VMEM)
    return pl.pallas_call(
        functools.partial(compute_kernel, names, mp, clouds, width, inner),
        out_shape=[jax.ShapeDtypeStruct(*v) for v in outs.values()],
        in_specs=[pl.BlockSpec(memory_space=pltpu.SMEM)] + [vmem] * (len(inputs) - 1),
        out_specs=[vmem] * len(outs),
        scratch_shapes=[pltpu.VMEM(*v) for v in scratch.values()],
        compiler_params=pltpu.CompilerParams(vmem_limit_bytes=60 * 1024 * 1024),
    )(counts, feats, cotangent, points, w, up_bias, vec, pos_hidden, pos_proj)


def shards(
    feats,
    centres,
    counts,
    cotangent,
    qkv_weight,
    out_weight,
    up_weight,
    up_bias,
    down_weight,
    norm_vectors,
    pos_hidden,
    pos_proj,
    qkv_moment,
    out_moment,
    up_moment,
    bias_moment,
    down_moment,
    vector_moment,
    hidden_moment,
    proj_moment,
    qkv_second,
    out_second,
    up_second,
    bias_second,
    down_second,
    vector_second,
    hidden_second,
    proj_second,
):
    mp_count = lax.axis_size("mp")
    mp_index = lax.axis_index("mp")
    dp_index = lax.axis_index("dp")
    share = feats.shape[0] // mp_count
    clouds = share // PAD
    width = feats.shape[1]
    cols = up_weight.shape[1]
    inner = cols * mp_count
    start = mp_index * share
    my_feats = lax.dynamic_slice_in_dim(feats, start, share, 0)
    my_top = lax.dynamic_slice_in_dim(cotangent, start, share, 0)
    my_counts = lax.dynamic_slice_in_dim(counts, mp_index * clouds, clouds, 0)
    my_points = lax.dynamic_slice_in_dim(centres, start, share, 1).T.reshape(clouds, PAD, 3)
    points = jnp.pad(my_points, ((0, 0), (0, SLOT - PAD), (0, 0)))
    points = jnp.concatenate((points, jnp.ones((clouds, SLOT, 1), f32)), axis=2)
    points = jnp.pad(points.reshape(clouds * SLOT, 4), ((0, 0), (0, 4)))
    packed = jnp.concatenate(
        (qkv_weight[0], qkv_weight[1], qkv_weight[2], out_weight.T, up_weight, down_weight.T), axis=1
    ).astype(bf16)
    whole = lax.all_gather(packed, "dp", axis=0, tiled=True)
    whole = lax.all_gather(whole, "mp", axis=0)
    bias = lax.all_gather(jnp.broadcast_to(up_bias[None], (8, cols)), "mp", axis=0)
    vec = jnp.pad(norm_vectors, ((0, 1), (0, 0)))
    hidden = jnp.pad(pos_hidden, ((0, 4), (0, 0)))
    block_out, feats_grad, grads, bias_grad, vec_grad, pos_grad, proj_grad = compute(
        mp_count, width, inner, my_counts, my_feats, my_top, points, whole, bias, vec, hidden, pos_proj
    )
    own = lax.psum_scatter(grads, "mp", scatter_dimension=0, tiled=True)[0]
    own = lax.psum_scatter(own, "dp", scatter_dimension=0, tiled=True)
    bias_grad, vector_grad, pos_grad, proj_grad = lax.psum(
        (bias_grad[:, 0], vec_grad[:7], pos_grad[:4], proj_grad), ("dp", "mp")
    )
    bias_grad = lax.dynamic_index_in_dim(bias_grad, mp_index, 0, keepdims=False)
    qkv_grad = jnp.stack((own[:, 0:128], own[:, 128:256], own[:, 256:384]))
    out_grad = own[:, 384:512].T
    up_grad = own[:, 512 : 512 + cols]
    down_grad = own[:, 512 + cols :].T
    leader = ((dp_index == 0) & (mp_index == 0)).astype(f32)
    first_dp = (dp_index == 0).astype(f32)
    owners = [1.0, 1.0, 1.0, first_dp, 1.0, leader, leader, leader]
    weights = [qkv_weight, out_weight, up_weight, up_bias, down_weight, norm_vectors, pos_hidden, pos_proj]
    moments = [
        qkv_moment,
        out_moment,
        up_moment,
        bias_moment,
        down_moment,
        vector_moment,
        hidden_moment,
        proj_moment,
    ]
    seconds = [
        qkv_second,
        out_second,
        up_second,
        bias_second,
        down_second,
        vector_second,
        hidden_second,
        proj_second,
    ]
    grads = [qkv_grad, out_grad, up_grad, bias_grad, down_grad, vector_grad, pos_grad, proj_grad]
    grad_square = jnp.zeros((), f32)
    weight_square = []
    for i in range(8):
        grad_square = grad_square + owners[i] * jnp.sum(grads[i] * grads[i])
        weight_square.append(owners[i] * piece_squares(weights[i], i))
    totals = lax.psum(jnp.concatenate([grad_square[None]] + weight_square), ("dp", "mp"))
    clip_norm = jnp.sqrt(totals[0])
    factor = jnp.minimum(1.0, clip_max / (clip_norm + 1e-06))
    clipped_list, moment_list, second_list, direction_list, update_square = [], [], [], [], []
    for i in range(8):
        clipped = grads[i] * factor
        moment_new = beta_one * moments[i] + (1.0 - beta_one) * clipped
        second_new = beta_two * seconds[i] + (1.0 - beta_two) * clipped * clipped
        direction = (
            moment_new
            / (1.0 - beta_one**step_count)
            / (jnp.sqrt(second_new / (1.0 - beta_two**step_count)) + adam_eps)
            + decay_rate * weights[i]
        )
        clipped_list.append(clipped)
        moment_list.append(moment_new)
        second_list.append(second_new)
        direction_list.append(direction)
        update_square.append(owners[i] * piece_squares(direction, i))
    update_total = lax.psum(jnp.concatenate(update_square), ("dp", "mp"))
    weight_norm = jnp.sqrt(totals[1:])
    update_norm = jnp.sqrt(update_total)
    trust_ratio = weight_norm / (update_norm + 1e-06)
    outputs = [block_out, feats_grad, clip_norm, jnp.stack((weight_norm, update_norm))]
    for i in range(8):
        new_weight = weights[i] - learn_rate * piece_ratio(trust_ratio, i) * direction_list[i]
        outputs.append(clipped_list[i])
        outputs.append(new_weight)
        outputs.append(moment_list[i])
        outputs.append(second_list[i])
        outputs.append(new_weight.astype(bf16))
    return tuple(outputs)


def solution(mesh):
    qkv, outw, upw, bias, whole = P(None, "dp", "mp"), P("mp", "dp"), P("dp", "mp"), P("mp"), P()
    params = (qkv, outw, upw, bias, outw, whole, whole, whole)
    in_specs = (P("dp", None), P(None, "dp"), P("dp"), P("dp", None)) + params * 3
    rows = P(("dp", "mp"), None)
    out_specs = (rows, rows, P(), P()) + tuple(spec for spec in params for _ in range(5))
    return jax.shard_map(shards, mesh=mesh, in_specs=in_specs, out_specs=out_specs, check_vma=False)
```

```python
import functools
import math

import jax
import jax.numpy as jnp
from jax import lax
from jax.experimental import pallas as pl
from jax.experimental.pallas import tpu as pltpu
from jax.sharding import PartitionSpec as P

HD = 64
PAD = 38
SLOT = 40
GROUP = 4

norm_eps = 1e-05
beta_one = 0.5
beta_two = 0.5
adam_eps = 1e-06
decay_rate = 0.01
learn_rate = 0.3
clip_max = 1.0
step_count = 3.0
neg_fill = -1e30
highest = lax.Precision.HIGHEST
f32 = jnp.float32
bf16 = jnp.bfloat16

NN = (((1,), (0,)), ((), ()))
NT = (((1,), (1,)), ((), ()))
TN = (((0,), (0,)), ((), ()))


def dot(a, b, dims=NN, precision=None):
    return lax.dot_general(a, b, dims, precision=precision, preferred_element_type=f32)


def gelu_pair(v):
    cdf = 0.5 * (1.0 + lax.erf(v * 0.7071067811865476))
    return v * cdf, cdf + v * jnp.exp(-0.5 * v * v) * 0.3989422804014327


def piece_squares(array, tensor_index):
    if tensor_index == 5:
        return jnp.sum(array * array, axis=1)
    return jnp.sum(array * array)[None]


def piece_ratio(trust_ratio, tensor_index):
    if tensor_index < 5:
        return trust_ratio[tensor_index]
    if tensor_index == 5:
        return trust_ratio[5:12][:, None]
    return trust_ratio[tensor_index + 6]


class Layer:
    def __init__(self, refs, mp, clouds, width, inner):
        self.__dict__.update(refs)
        self.mp = mp
        self.clouds = clouds
        self.width = width
        self.inner = inner
        self.rows = clouds * SLOT
        self.block = GROUP * SLOT
        self.blocks = clouds // GROUP
        self.tile = self.rows // 2 if self.rows % 32 == 0 else self.rows
        self.hid = self.proj_low.shape[0]

    def live(self, j):
        return [h for h in range(2) if (2 * j + h) % 2 == 0 or j < self.mp // 2]

    def spread_rows(self):
        zeros = jnp.zeros((SLOT - PAD, self.width), f32)
        self.stage[...] = self.feats[...].astype(f32)
        for c in range(self.clouds):
            self.stream[pl.ds(SLOT * c, PAD), :] = self.stage[pl.ds(PAD * c, PAD), :]
            self.stream[pl.ds(SLOT * c + PAD, SLOT - PAD), :] = zeros
        self.stage[...] = self.cotangent[...].astype(f32)
        for c in range(self.clouds):
            self.middle_grad[pl.ds(SLOT * c, PAD), :] = self.stage[pl.ds(PAD * c, PAD), :]
            self.middle_grad[pl.ds(SLOT * c + PAD, SLOT - PAD), :] = zeros

    def keep_block(self, b, shape, dim):
        place = lax.broadcasted_iota(jnp.int32, shape, dim)
        bound = jnp.zeros(shape, jnp.int32)
        for i in range(GROUP):
            limit = self.counts[b * GROUP + i] + SLOT * i
            inside = (place >= SLOT * i) & (place < limit)
            bound = jnp.where(inside, 1, bound)
        return bound > 0

    def masks(self):
        n = self.block

        def step(b, carry):
            keys = lax.broadcasted_iota(jnp.int32, (n, n), 0)
            query = lax.broadcasted_iota(jnp.int32, (n, n), 1)
            fill = jnp.full((n, n), neg_fill, f32)
            for i in range(GROUP):
                limit = self.counts[b * GROUP + i] + SLOT * i
                inside = (keys >= SLOT * i) & (keys < limit)
                mine = (query >= SLOT * i) & (query < SLOT * (i + 1))
                fill = jnp.where(inside & mine, 0.0, fill)
            self.mask[b] = fill
            self.keep[pl.ds(b * n, n), :] = jnp.where(self.keep_block(b, (n, 128), 0), 1.0, 0.0)
            return carry

        lax.fori_loop(0, self.blocks, step, 0)

    def norm(self, x):
        centre = x - jnp.mean(x, axis=-1, keepdims=True)
        spread = jnp.mean(centre * centre, axis=-1, keepdims=True)
        rate = lax.rsqrt(spread + norm_eps)
        return centre * rate, rate

    def norm_back(self, grad, hat, rate, gain):
        scaled = grad * gain
        first = jnp.mean(scaled, axis=-1, keepdims=True)
        second = jnp.mean(scaled * hat, axis=-1, keepdims=True)
        return rate * (scaled - first - hat * second)

    def entry(self):
        t = self.tile

        def step(i, carry):
            rows = pl.ds(i * t, t)
            pre = dot(self.points[rows, :], self.pos_hidden[...], NN, highest)
            value, slope = gelu_pair(pre)
            hidden = value.astype(bf16)
            self.pos_slope[rows, :] = slope
            self.hidden[rows, :] = hidden
            term = dot(hidden, self.proj_low[...]) + self.vec[6:7, :]
            x = self.stream[rows, :] + term
            hat, rate = self.norm(x)
            self.stream[rows, :] = x
            self.hat_one[rows, :] = hat
            self.rate_one[rows, :] = jnp.broadcast_to(rate, (t, 128))
            self.normed_one[rows, :] = (hat * self.vec[0:1, :] + self.vec[2:3, :]).astype(bf16)
            return carry

        lax.fori_loop(0, self.rows // t, step, 0)

    def project(self, j):
        w = self.width
        t = self.tile

        def step(i, carry):
            rows = pl.ds(i * t, t)
            self.qkv[j, rows, :] = dot(self.normed_one[rows, :], self.w_qkv(j)).astype(bf16)
            return carry

        lax.fori_loop(0, self.rows // t, step, 0)

    def lanes(self, h, n):
        lane = lax.broadcasted_iota(jnp.int32, (n, 128), 1)
        return (lane < HD) if h == 0 else (lane >= HD)

    def attend(self, j, first):
        n = self.block

        def step(b, carry):
            rows = pl.ds(b * n, n)
            query = self.qkv[j, rows, 0:128] * jnp.asarray(1.0 / math.sqrt(HD), bf16)
            keys = self.qkv[j, rows, 128:256]
            values = self.qkv[j, rows, 256:384]
            zero = jnp.zeros_like(query)
            mixed = jnp.zeros((n, 128), f32)
            for place, h in enumerate(self.live(j)):
                own = self.lanes(h, n)
                scores = dot(keys, jnp.where(own, query, zero), NT) + self.mask[b]
                top = jnp.max(scores, axis=0, keepdims=True)
                expo = jnp.exp(scores - top)
                total = jnp.sum(expo, axis=0, keepdims=True)
                probs = expo / total
                self.probs[first + place, b] = probs
                mixed = jnp.where(own, dot(probs.astype(bf16), values, TN), mixed)
            self.attn_low[j, rows, :] = mixed.astype(bf16)
            return carry

        lax.fori_loop(0, self.blocks, step, 0)

    def middle(self):
        t = self.tile

        def step(i, carry):
            rows = pl.ds(i * t, t)
            x = self.stream[rows, :] + self.vec[4:5, :]
            for j in range(self.mp):
                x = x + dot(self.attn_low[j, rows, :], self.w_out(j), NT)
            hat, rate = self.norm(x)
            self.stream[rows, :] = x
            self.hat_two[rows, :] = hat
            self.rate_two[rows, :] = jnp.broadcast_to(rate, (t, 128))
            self.normed_two[rows, :] = (hat * self.vec[1:2, :] + self.vec[3:4, :]).astype(bf16)
            return carry

        lax.fori_loop(0, self.rows // t, step, 0)

    def feed(self, j):
        t = self.tile

        def step(i, carry):
            rows = pl.ds(i * t, t)
            pre = dot(self.normed_two[rows, :], self.w_up(j)) + self.up_bias[j, 0:1, :]
            value, slope = gelu_pair(pre)
            low = value.astype(bf16)
            self.activated[j, rows, :] = low
            self.slope[j, rows, :] = slope
            self.stream[rows, :] += dot(low, self.w_down(j), NT)
            return carry

        lax.fori_loop(0, self.rows // t, step, 0)

    def top(self):
        t = self.tile

        def step(i, carry):
            rows = pl.ds(i * t, t)
            keep = jnp.concatenate([self.keep[rows, :]] * (self.width // 128), axis=1)
            self.stream[rows, :] = (self.stream[rows, :] + self.vec[5:6, :]) * keep
            grad = self.middle_grad[rows, :] * keep
            self.middle_grad[rows, :] = grad
            self.grad_top[rows, :] = grad.astype(bf16)
            self.vec_grad[5:6, :] += jnp.sum(grad, axis=0, keepdims=True)
            return carry

        self.vec_grad[...] = jnp.zeros_like(self.vec_grad)
        self.up_bias_grad[...] = jnp.zeros_like(self.up_bias_grad)
        lax.fori_loop(0, self.rows // t, step, 0)

    def feed_back(self, j):
        t = self.tile

        def step(i, carry):
            rows = pl.ds(i * t, t)
            grad = dot(self.grad_top[rows, :], self.w_down(j)) * self.slope[j, rows, :]
            low = grad.astype(bf16)
            self.grad_pre[j, rows, :] = low
            self.up_bias_grad[j, 0:1, :] += jnp.sum(low.astype(f32), axis=0, keepdims=True)
            term = dot(low, self.w_up(j), NT)
            if j == 0:
                self.normed_grad[rows, :] = term
            else:
                self.normed_grad[rows, :] += term
            return carry

        lax.fori_loop(0, self.rows // t, step, 0)

    def middle_back(self):
        t = self.tile

        def step(i, carry):
            rows = pl.ds(i * t, t)
            grad, hat = self.normed_grad[rows, :], self.hat_two[rows, :]
            rate = jnp.concatenate([self.rate_two[rows, :]] * (self.width // 128), axis=1)
            self.vec_grad[1:2, :] += jnp.sum(grad * hat, axis=0, keepdims=True)
            self.vec_grad[3:4, :] += jnp.sum(grad, axis=0, keepdims=True)
            out = self.middle_grad[rows, :] + self.norm_back(grad, hat, rate, self.vec[1:2, :])
            self.middle_grad[rows, :] = out
            self.vec_grad[4:5, :] += jnp.sum(out, axis=0, keepdims=True)
            self.middle_low[rows, :] = out.astype(bf16)
            return carry

        lax.fori_loop(0, self.rows // t, step, 0)

    def attend_grad(self, j):
        t = self.tile

        def step(i, carry):
            rows = pl.ds(i * t, t)
            self.attn_grad[j, rows, :] = dot(self.middle_low[rows, :], self.w_out(j)).astype(bf16)
            return carry

        lax.fori_loop(0, self.rows // t, step, 0)

    def attend_back(self, j, first):
        n = self.block

        def step(b, carry):
            rows = pl.ds(b * n, n)
            scale = 1.0 / math.sqrt(HD)
            query = self.qkv[j, rows, 0:128] * jnp.asarray(scale, bf16)
            keys = self.qkv[j, rows, 128:256]
            values = self.qkv[j, rows, 256:384]
            grad_out = self.attn_grad[j, rows, :]
            zero = jnp.zeros_like(query)
            grad_query = jnp.zeros((n, 128), f32)
            grad_keys = jnp.zeros((n, 128), f32)
            grad_values = jnp.zeros((n, 128), f32)
            for place, h in enumerate(self.live(j)):
                own = self.lanes(h, n)
                mine = jnp.where(own, grad_out, zero)
                probs = self.probs[first + place, b]
                grad_probs = dot(values, mine, NT)
                grad_values = grad_values + dot(probs.astype(bf16), mine)
                inner = jnp.sum(probs * grad_probs, axis=0, keepdims=True)
                grad_scores = (probs * (grad_probs - inner)).astype(bf16)
                grad_keys = grad_keys + dot(grad_scores, jnp.where(own, query, zero))
                grad_query = jnp.where(own, dot(grad_scores, keys, TN), grad_query)
            self.grad_proj[j, rows, 0:128] = (grad_query * scale).astype(bf16)
            self.grad_proj[j, rows, 128:256] = grad_keys.astype(bf16)
            self.grad_proj[j, rows, 256:384] = grad_values.astype(bf16)
            return carry

        lax.fori_loop(0, self.blocks, step, 0)

    def entry_back(self):
        t = self.tile

        def step(i, carry):
            rows = pl.ds(i * t, t)
            grad = jnp.zeros((t, self.width), f32)
            for j in range(self.mp):
                grad = grad + dot(self.grad_proj[j, rows, :], self.w_qkv(j), NT)
            hat = self.hat_one[rows, :]
            rate = jnp.concatenate([self.rate_one[rows, :]] * (self.width // 128), axis=1)
            self.vec_grad[0:1, :] += jnp.sum(grad * hat, axis=0, keepdims=True)
            self.vec_grad[2:3, :] += jnp.sum(grad, axis=0, keepdims=True)
            out = self.middle_grad[rows, :] + self.norm_back(grad, hat, rate, self.vec[0:1, :])
            self.middle_grad[rows, :] = out
            self.vec_grad[6:7, :] += jnp.sum(out, axis=0, keepdims=True)
            low = out.astype(bf16)
            self.pos_low[rows, :] = low
            self.pre_grad[rows, :] = dot(low, self.proj_low[...], NT) * self.pos_slope[rows, :]
            return carry

        lax.fori_loop(0, self.rows // t, step, 0)

    def turn(self, source, target):
        n = 128

        def step(i, carry):
            block = source[pl.ds(i * n, n), :].astype(f32)
            target[:, pl.ds(pl.multiple_of(i * n, n), n)] = block.T.astype(bf16)
            return carry

        lax.fori_loop(0, self.rows // n, step, 0)

    def gather_rows(self, source, target):
        for c in range(self.clouds):
            target[pl.ds(PAD * c, PAD), :] = source[pl.ds(SLOT * c, PAD), :]


def layer_scratch(mp, clouds, width, inner, hid):
    rows = clouds * SLOT
    block = GROUP * SLOT
    cols = inner // mp
    heads = mp + mp // 2
    shapes = dict(
        stage=((clouds * PAD, width), f32),
        stream=((rows, width), f32),
        middle_grad=((rows, width), f32),
        mask=((clouds // GROUP, block, block), f32),
        keep=((rows, 128), f32),
        pos_slope=((rows, hid), f32),
        hidden=((rows, hid), bf16),
        hat_one=((rows, width), f32),
        rate_one=((rows, 128), f32),
        normed_one=((rows, width), bf16),
        qkv=((mp, rows, 384), bf16),
        probs=((heads, clouds // GROUP, block, block), f32),
        attn_low=((mp, rows, 128), bf16),
        hat_two=((rows, width), f32),
        rate_two=((rows, 128), f32),
        normed_two=((rows, width), bf16),
        activated=((mp, rows, cols), bf16),
        slope=((mp, rows, cols), f32),
        grad_top=((rows, width), bf16),
        grad_pre=((mp, rows, cols), bf16),
        normed_grad=((rows, width), f32),
        middle_low=((rows, width), bf16),
        attn_grad=((mp, rows, 128), bf16),
        grad_proj=((mp, rows, 384), bf16),
        pos_low=((rows, width), bf16),
        pre_grad=((rows, hid), f32),
        turned=((width, rows), bf16),
        turned_mid=((width, rows), bf16),
    )
    return shapes


def heads_before(mp, j):
    return sum(2 if i < mp // 2 else 1 for i in range(j))


def compute_kernel(names, mp, clouds, width, inner, *args):
    refs = dict(zip(names, args))
    layer = Layer(refs, mp, clouds, width, inner)
    w = layer.w
    cols = inner // mp
    layer.w_qkv = lambda j: w[j, :, 0:384]
    layer.w_out = lambda j: w[j, :, 384:512]
    layer.w_up = lambda j: w[j, :, 512 : 512 + cols]
    layer.w_down = lambda j: w[j, :, 512 + cols : 512 + 2 * cols]
    layer.proj_low[...] = layer.pos_proj[...].astype(bf16)
    layer.spread_rows()
    layer.masks()
    layer.entry()
    for j in range(mp):
        layer.project(j)
        layer.attend(j, heads_before(mp, j))
    layer.middle()
    for j in range(mp):
        layer.feed(j)
    layer.top()
    layer.gather_rows(layer.stream, layer.stage)
    layer.block_out[...] = layer.stage[...].astype(bf16)
    for j in range(mp):
        layer.feed_back(j)
    g = layer.grads
    layer.turn(layer.grad_top, layer.turned)
    for j in range(mp):
        g[j, :, 512 + cols : 512 + 2 * cols] = dot(layer.turned[...], layer.activated[j])
    layer.turn(layer.normed_two, layer.turned)
    for j in range(mp):
        g[j, :, 512 : 512 + cols] = dot(layer.turned[...], layer.grad_pre[j])
    layer.middle_back()
    layer.turn(layer.middle_low, layer.turned)
    for j in range(mp):
        g[j, :, 384:512] = dot(layer.turned[...], layer.attn_low[j])
        layer.attend_grad(j)
        layer.attend_back(j, heads_before(mp, j))
    layer.turn(layer.normed_one, layer.turned)
    for j in range(mp):
        g[j, :, 0:384] = dot(layer.turned[...], layer.grad_proj[j])
    layer.entry_back()
    layer.gather_rows(layer.middle_grad, layer.feats_grad)
    layer.proj_grad[...] = dot(layer.hidden[...], layer.pos_low[...], TN)
    layer.pos_grad[...] = dot(layer.points[...], layer.pre_grad[...], TN, highest)


def compute(mp, width, inner, counts, feats, cotangent, points, w, up_bias, vec, pos_hidden, pos_proj):
    clouds = counts.shape[0]
    hid = pos_proj.shape[0]
    inputs = ["counts", "feats", "cotangent", "points", "w", "up_bias", "vec", "pos_hidden", "pos_proj"]
    outs = dict(
        block_out=((clouds * PAD, width), bf16),
        feats_grad=((clouds * PAD, width), f32),
        grads=(w.shape, f32),
        up_bias_grad=((mp, 8, inner // mp), f32),
        vec_grad=((8, width), f32),
        pos_grad=((8, hid), f32),
        proj_grad=((hid, width), f32),
    )
    scratch = layer_scratch(mp, clouds, width, inner, hid)
    scratch["proj_low"] = ((hid, width), bf16)
    names = inputs + list(outs) + list(scratch)
    vmem = pl.BlockSpec(memory_space=pltpu.VMEM)
    return pl.pallas_call(
        functools.partial(compute_kernel, names, mp, clouds, width, inner),
        out_shape=[jax.ShapeDtypeStruct(*v) for v in outs.values()],
        in_specs=[pl.BlockSpec(memory_space=pltpu.SMEM)] + [vmem] * (len(inputs) - 1),
        out_specs=[vmem] * len(outs),
        scratch_shapes=[pltpu.VMEM(*v) for v in scratch.values()],
        compiler_params=pltpu.CompilerParams(vmem_limit_bytes=60 * 1024 * 1024),
    )(counts, feats, cotangent, points, w, up_bias, vec, pos_hidden, pos_proj)


def shards(
    feats,
    centres,
    counts,
    cotangent,
    qkv_weight,
    out_weight,
    up_weight,
    up_bias,
    down_weight,
    norm_vectors,
    pos_hidden,
    pos_proj,
    qkv_moment,
    out_moment,
    up_moment,
    bias_moment,
    down_moment,
    vector_moment,
    hidden_moment,
    proj_moment,
    qkv_second,
    out_second,
    up_second,
    bias_second,
    down_second,
    vector_second,
    hidden_second,
    proj_second,
):
    mp_count = lax.axis_size("mp")
    mp_index = lax.axis_index("mp")
    dp_index = lax.axis_index("dp")
    share = feats.shape[0] // mp_count
    clouds = share // PAD
    width = feats.shape[1]
    cols = up_weight.shape[1]
    inner = cols * mp_count
    start = mp_index * share
    my_feats = lax.dynamic_slice_in_dim(feats, start, share, 0)
    my_top = lax.dynamic_slice_in_dim(cotangent, start, share, 0)
    my_counts = lax.dynamic_slice_in_dim(counts, mp_index * clouds, clouds, 0)
    my_points = lax.dynamic_slice_in_dim(centres, start, share, 1).T.reshape(clouds, PAD, 3)
    points = jnp.pad(my_points, ((0, 0), (0, SLOT - PAD), (0, 0)))
    points = jnp.concatenate((points, jnp.ones((clouds, SLOT, 1), f32)), axis=2)
    points = jnp.pad(points.reshape(clouds * SLOT, 4), ((0, 0), (0, 4)))
    packed = jnp.concatenate(
        (qkv_weight[0], qkv_weight[1], qkv_weight[2], out_weight.T, up_weight, down_weight.T), axis=1
    ).astype(bf16)
    whole = lax.all_gather(packed, "dp", axis=0, tiled=True)
    whole = lax.all_gather(whole, "mp", axis=0)
    bias = lax.all_gather(jnp.broadcast_to(up_bias[None], (8, cols)), "mp", axis=0)
    vec = jnp.pad(norm_vectors, ((0, 1), (0, 0)))
    hidden = jnp.pad(pos_hidden, ((0, 4), (0, 0)))
    block_out, feats_grad, grads, bias_grad, vec_grad, pos_grad, proj_grad = compute(
        mp_count, width, inner, my_counts, my_feats, my_top, points, whole, bias, vec, hidden, pos_proj
    )
    own = lax.psum_scatter(grads, "mp", scatter_dimension=0, tiled=True)[0]
    own = lax.psum_scatter(own, "dp", scatter_dimension=0, tiled=True)
    bias_grad, vector_grad, pos_grad, proj_grad = lax.psum(
        (bias_grad[:, 0], vec_grad[:7], pos_grad[:4], proj_grad), ("dp", "mp")
    )
    bias_grad = lax.dynamic_index_in_dim(bias_grad, mp_index, 0, keepdims=False)
    qkv_grad = jnp.stack((own[:, 0:128], own[:, 128:256], own[:, 256:384]))
    out_grad = own[:, 384:512].T
    up_grad = own[:, 512 : 512 + cols]
    down_grad = own[:, 512 + cols :].T
    leader = ((dp_index == 0) & (mp_index == 0)).astype(f32)
    first_dp = (dp_index == 0).astype(f32)
    owners = [1.0, 1.0, 1.0, first_dp, 1.0, leader, leader, leader]
    weights = [qkv_weight, out_weight, up_weight, up_bias, down_weight, norm_vectors, pos_hidden, pos_proj]
    moments = [
        qkv_moment,
        out_moment,
        up_moment,
        bias_moment,
        down_moment,
        vector_moment,
        hidden_moment,
        proj_moment,
    ]
    seconds = [
        qkv_second,
        out_second,
        up_second,
        bias_second,
        down_second,
        vector_second,
        hidden_second,
        proj_second,
    ]
    grads = [qkv_grad, out_grad, up_grad, bias_grad, down_grad, vector_grad, pos_grad, proj_grad]
    grad_square = jnp.zeros((), f32)
    weight_square = []
    for i in range(8):
        grad_square = grad_square + owners[i] * jnp.sum(grads[i] * grads[i])
        weight_square.append(owners[i] * piece_squares(weights[i], i))
    totals = lax.psum(jnp.concatenate([grad_square[None]] + weight_square), ("dp", "mp"))
    clip_norm = jnp.sqrt(totals[0])
    factor = jnp.minimum(1.0, clip_max / (clip_norm + 1e-06))
    clipped_list, moment_list, second_list, direction_list, update_square = [], [], [], [], []
    for i in range(8):
        clipped = grads[i] * factor
        moment_new = beta_one * moments[i] + (1.0 - beta_one) * clipped
        second_new = beta_two * seconds[i] + (1.0 - beta_two) * clipped * clipped
        direction = (
            moment_new
            / (1.0 - beta_one**step_count)
            / (jnp.sqrt(second_new / (1.0 - beta_two**step_count)) + adam_eps)
            + decay_rate * weights[i]
        )
        clipped_list.append(clipped)
        moment_list.append(moment_new)
        second_list.append(second_new)
        direction_list.append(direction)
        update_square.append(owners[i] * piece_squares(direction, i))
    update_total = lax.psum(jnp.concatenate(update_square), ("dp", "mp"))
    weight_norm = jnp.sqrt(totals[1:])
    update_norm = jnp.sqrt(update_total)
    trust_ratio = weight_norm / (update_norm + 1e-06)
    outputs = [block_out, feats_grad, clip_norm, jnp.stack((weight_norm, update_norm))]
    for i in range(8):
        new_weight = weights[i] - learn_rate * piece_ratio(trust_ratio, i) * direction_list[i]
        outputs.append(clipped_list[i])
        outputs.append(new_weight)
        outputs.append(moment_list[i])
        outputs.append(second_list[i])
        outputs.append(new_weight.astype(bf16))
    return tuple(outputs)


class Links:
    def __init__(self, send, recv):
        dp, mp = lax.axis_index("dp"), lax.axis_index("mp")
        self.z, self.y = dp // 2, lax.rem(dp, 2)
        self.x, self.c = mp // 2, lax.rem(mp, 2)
        self.mp = mp
        self.plane = self.y * 4 + mp
        self.send_sem, self.recv_sem = send, recv
        self.count = 0
        self.sent = []

    def at(self, z, y, x, c):
        return (z * 2 + y, x * 2 + c)

    def core(self):
        return self.at(self.z, self.y, self.x, 1 - self.c)

    def side(self):
        return self.at(self.z, self.y, 1 - self.x, self.c)

    def deep(self):
        return self.at(self.z, 1 - self.y, self.x, self.c)

    def far(self, k):
        return self.at(lax.rem(self.z + k, 4), self.y, self.x, self.c)

    def back(self, k):
        return lax.rem(self.z + 4 - k, 4)

    def round(self, k):
        other = lax.rem(self.plane + k, 8)
        return (self.z * 2 + other // 4, lax.rem(other, 4))

    def peers(self):
        return [self.far(k) for k in range(1, 4)] + [self.round(k) for k in range(1, 8)]

    def greet(self):
        barrier = pltpu.get_barrier_semaphore()
        for who in self.peers():
            pl.semaphore_signal(barrier, inc=1, device_id=who, device_id_type=pl.DeviceIdType.MESH)

    def met(self):
        pl.semaphore_wait(pltpu.get_barrier_semaphore(), 10)

    def copy(self, source, target, who, i):
        return pltpu.make_async_remote_copy(
            src_ref=source,
            dst_ref=target,
            send_sem=self.send_sem.at[i],
            recv_sem=self.recv_sem.at[i],
            device_id=who,
            device_id_type=pl.DeviceIdType.MESH,
        )

    def send(self, source, target, who):
        i = self.count
        self.count += 1
        copy = self.copy(source, target, who, i)
        copy.start()
        self.sent.append(copy)
        return i

    def wait(self, i, target):
        self.copy(target, target, self.core(), i).wait_recv()

    def finish(self):
        for copy in self.sent:
            copy.wait_send()


class Gather:
    def __init__(self, links, w, lo, hi, flip):
        self.links, self.w, self.lo, self.hi, self.flip = links, w, lo, hi, flip

    def part(self, mp, z, y):
        return self.w.at[mp, z, y, :, self.lo : self.hi]

    def spread(self, block):
        k = self.links
        return (k.send(block, block, k.deep()), k.send(block, block, k.side()), k.send(block, block, k.core()))

    def start(self):
        k = self.links
        own = self.part(k.mp, k.z, k.y)
        self.along = [k.send(own, own, k.far(i)) for i in (3, 2, 1)][::-1]
        self.spreads = [self.spread(own)]

    def second(self):
        k = self.links
        for i in (1, 2, 3):
            block = self.part(k.mp, k.back(i), k.y)
            k.wait(self.along[i - 1], block)
            self.spreads.append(self.spread(block))

    def third(self):
        k = self.links
        other = k.mp + 2 - 4 * k.x
        for i in range(4):
            z = k.back(i)
            if self.flip:
                k.wait(self.spreads[i][1], self.part(other, z, k.y))
            else:
                k.wait(self.spreads[i][0], self.part(k.mp, z, 1 - k.y))
        if self.flip:
            block = self.part(other, slice(None), k.y)
            self.wide = k.send(block, block, k.deep())
            self.core_first = k.send(block, block, k.core())
        else:
            block = self.part(k.mp, slice(None), 1 - k.y)
            self.wide = k.send(block, block, k.side())
            self.core_first = k.send(block, block, k.core())

    def fourth(self):
        k = self.links
        other = k.mp + 2 - 4 * k.x
        for i in range(4):
            z = k.back(i)
            if self.flip:
                k.wait(self.spreads[i][0], self.part(k.mp, z, 1 - k.y))
            else:
                k.wait(self.spreads[i][1], self.part(other, z, k.y))
        if self.flip:
            near = self.part(k.mp, slice(None), 1 - k.y)
            self.core_second = k.send(near, near, k.core())
            self.far_wait = self.part(other, slice(None), 1 - k.y)
            k.wait(self.wide, self.far_wait)
            self.core_third = k.send(self.far_wait, self.far_wait, k.core())
        else:
            near = self.part(other, slice(None), k.y)
            self.core_second = k.send(near, near, k.core())
            self.far_wait = self.part(other, slice(None), 1 - k.y)
            k.wait(self.wide, self.far_wait)
            self.core_third = k.send(self.far_wait, self.far_wait, k.core())

    def end(self):
        k = self.links
        twin = k.mp + 1 - 2 * k.c
        other = twin + 2 - 4 * k.x
        for i in range(4):
            k.wait(self.spreads[i][2], self.part(twin, k.back(i), k.y))
        if self.flip:
            k.wait(self.core_first, self.part(other, slice(None), k.y))
            k.wait(self.core_second, self.part(twin, slice(None), 1 - k.y))
        else:
            k.wait(self.core_first, self.part(twin, slice(None), 1 - k.y))
            k.wait(self.core_second, self.part(other, slice(None), k.y))
        k.wait(self.core_third, self.part(other, slice(None), 1 - k.y))


class Scatter:
    def __init__(self, links, refs, flip):
        self.links, self.flip = links, flip
        self.__dict__.update(refs)

    def start(self):
        k = self.links
        self.first = k.send(self.core_out, self.core_in, k.core())

    def pair(self, x, z, y):
        return self.kept[x, z, y] + self.core_in[x, z, y].astype(f32)

    def second(self):
        k = self.links
        k.wait(self.first, self.core_in)
        if self.flip:
            for x in range(2):
                for z in range(4):
                    self.next_out[x, z] = self.pair(x, z, 1 - k.y).astype(bf16)
            self.next = k.send(self.next_out, self.next_in, k.deep())
        else:
            for y in range(2):
                for z in range(4):
                    self.next_out[y, z] = self.pair(1 - k.x, z, y).astype(bf16)
            self.next = k.send(self.next_out, self.next_in, k.side())

    def third(self):
        k = self.links
        k.wait(self.next, self.next_in)
        for z in range(4):
            if self.flip:
                total = self.pair(1 - k.x, z, k.y) + self.next_in[1 - k.x, z].astype(f32)
            else:
                total = self.pair(k.x, z, 1 - k.y) + self.next_in[1 - k.y, z].astype(f32)
            self.last_out[z] = total.astype(bf16)
        self.last = k.send(self.last_out, self.last_in, k.side() if self.flip else k.deep())

    def fourth(self):
        k = self.links
        k.wait(self.last, self.last_in)
        self.along = []
        for i in range(4):
            z = lax.rem(k.z + i, 4)
            mid = self.next_in[k.x, z] if self.flip else self.next_in[k.y, z]
            total = self.pair(k.x, z, k.y) + mid.astype(f32) + self.last_in[z].astype(f32)
            if i == 0:
                self.own[...] = total
            else:
                self.far_out[i - 1] = total.astype(bf16)
                self.along.append(k.send(self.far_out.at[i - 1], self.far_in.at[i - 1], k.far(i)))

    def end(self):
        k = self.links
        total = self.own[...]
        for i in range(3):
            k.wait(self.along[i], self.far_in.at[i])
            total = total + self.far_in[i].astype(f32)
        return total


def scatter_scratch(tag, cols):
    return {
        tag + "kept": ((2, 4, 2, 48, cols), f32),
        tag + "core_out": ((2, 4, 2, 48, cols), bf16),
        tag + "core_in": ((2, 4, 2, 48, cols), bf16),
        tag + "next_out": ((2, 4, 48, cols), bf16),
        tag + "next_in": ((2, 4, 48, cols), bf16),
        tag + "last_out": ((4, 48, cols), bf16),
        tag + "last_in": ((4, 48, cols), bf16),
        tag + "far_out": ((3, 48, cols), bf16),
        tag + "far_in": ((3, 48, cols), bf16),
        tag + "own": ((48, cols), f32),
    }


def stack_rows(rows, height=8):
    place = lax.broadcasted_iota(jnp.int32, (height, 128), 0)
    out = jnp.zeros((height, 128), f32)
    for i, row in enumerate(rows):
        out = jnp.where(place == i, jnp.broadcast_to(row, (height, 128)), out)
    return out


def square_row(array):
    total = jnp.sum(jnp.sum(array * array, axis=0, keepdims=True), axis=1, keepdims=True)
    return jnp.broadcast_to(total, (1, 128))


def adam(grad, factor, moment, second, weight):
    clipped = grad * factor
    moment_new = beta_one * moment + (1.0 - beta_one) * clipped
    second_new = beta_two * second + (1.0 - beta_two) * clipped * clipped
    direction = (
        moment_new
        / (1.0 - beta_one**step_count)
        / (jnp.sqrt(second_new / (1.0 - beta_two**step_count)) + adam_eps)
        + decay_rate * weight
    )
    return clipped, moment_new, second_new, direction


PIECES = ("qkv", "out", "up", "bias", "down", "vector", "hidden", "proj")


def own_parts(own, small, mp):
    cols = (own.shape[1] - 512) // 2

    def wide(row, count):
        return jnp.concatenate([small[row + 8 * i : row + 8 * i + count, :] for i in range(3)], axis=1)

    place = lax.broadcasted_iota(jnp.int32, (8, cols), 0)

    return {
        "qkv": [own[:, 128 * i : 128 * i + 128] for i in range(3)],
        "out": [own[:, 384:512]],
        "up": [own[:, 512 : 512 + cols]],
        "bias": [jnp.sum(jnp.where(place == mp, wide(416, 8), 0.0), axis=0, keepdims=True)],
        "down": [own[:, 512 + cols : 512 + 2 * cols]],
        "vector": [wide(384, 7)],
        "hidden": [small[408:412, :]],
        "proj": [jnp.concatenate([small[128 * i : 128 * i + 128, :] for i in range(3)], axis=1)],
    }


def load(refs, kind, name):
    ref = refs[name + "_" + kind]
    if name == "qkv":
        return [ref[i] for i in range(3)]
    return [ref[...]]


def main_kernel(names, mp, clouds, width, inner, *args):
    refs = dict(zip(names, args))
    layer = Layer(refs, mp, clouds, width, inner)
    cols = inner // mp
    links = Links(layer.send_sem, layer.recv_sem)
    w = layer.w
    links.greet()
    share = clouds * PAD
    rows = pl.ds(pl.multiple_of(links.mp * share, 16), share)
    local = [
        pltpu.make_async_copy(layer.feats_all.at[rows, :], layer.feats, layer.load_sem.at[0]),
        pltpu.make_async_copy(layer.top_all.at[rows, :], layer.cotangent, layer.load_sem.at[1]),
    ]
    late = []
    for i, name in enumerate(name for name in PIECES for kind in ("moment", "second")):
        kind = ("moment", "second")[i % 2]
        source, target = refs[name + "_" + kind + "_all"], refs[name + "_" + kind]
        late.append(pltpu.make_async_copy(source, target, layer.load_sem.at[2 + i]))
    for copy in local + late:
        copy.start()

    def flat(j, lo, hi):
        return w[j, :, :, :, lo:hi].reshape(width, hi - lo)

    layer.w_qkv = lambda j: flat(j, 0, 384)
    layer.w_out = lambda j: flat(j, 384, 512)
    layer.w_up = lambda j: flat(j, 512, 512 + cols)
    layer.w_down = lambda j: flat(j, 512 + cols, 512 + 2 * cols)
    for i in range(3):
        w[links.mp, links.z, links.y, :, 128 * i : 128 * i + 128] = refs["qkv_weight"][i].astype(bf16)
    w[links.mp, links.z, links.y, :, 384:512] = refs["out_weight"][...].astype(bf16)
    w[links.mp, links.z, links.y, :, 512 : 512 + cols] = refs["up_weight"][...].astype(bf16)
    w[links.mp, links.z, links.y, :, 512 + cols : 512 + 2 * cols] = refs["down_weight"][...].astype(bf16)
    layer.up_bias[links.mp] = jnp.broadcast_to(refs["bias_weight"][...], (8, cols))
    links.met()
    gathers = [
        Gather(links, w, 0, 256, False),
        Gather(links, w, 256, 512, True),
        Gather(links, w, 512, 512 + cols, False),
        Gather(links, w, 512 + cols, 512 + 2 * cols, True),
    ]
    for g in gathers[:2]:
        g.start()
    own_bias = layer.up_bias.at[links.mp]
    bias_side = links.send(own_bias, own_bias, links.side())
    bias_core = links.send(own_bias, own_bias, links.core())
    for g in gathers[2:]:
        g.start()
    layer.proj_low[...] = refs["proj_weight"][...].astype(bf16)
    layer.vec = refs["vector_weight"]
    layer.pos_hidden[...] = jnp.zeros((8, 128), f32)
    layer.pos_hidden[0:4, :] = refs["hidden_weight"][...]
    for copy in local:
        copy.wait()
    layer.counts = _Shifted(layer.counts_all, links.mp * clouds)
    layer.spread_rows()
    for g in gathers[:2]:
        g.second()
    layer.masks()
    for g in gathers[:2]:
        g.third()
    layer.entry()
    for g in gathers[2:]:
        g.second()
    for g in gathers[:2]:
        g.fourth()
    other_bias = layer.up_bias.at[links.mp + 2 - 4 * links.x]
    links.wait(bias_side, other_bias)
    bias_last = links.send(other_bias, other_bias, links.core())
    for g in gathers[:2]:
        g.end()
    layer.project(0)
    for g in gathers[2:]:
        g.third()
    layer.attend(0, heads_before(mp, 0))
    for j in range(1, mp):
        layer.project(j)
        layer.attend(j, heads_before(mp, j))
        if j == 1:
            for g in gathers[2:]:
                g.fourth()
    layer.middle()
    for g in gathers[2:]:
        g.end()
    twin = links.mp + 1 - 2 * links.c
    links.wait(bias_core, layer.up_bias.at[twin])
    links.wait(bias_last, layer.up_bias.at[twin + 2 - 4 * links.x])
    for j in range(mp):
        layer.feed(j)
    layer.top()
    layer.gather_rows(layer.stream, layer.stage)
    layer.block_out[...] = layer.stage[...].astype(bf16)

    def scatter(tag, flip):
        return Scatter(links, {n[len(tag) :]: refs[n] for n in names if n.startswith(tag)}, flip)

    down, up = scatter("down__", True), scatter("up__", False)
    qk, vo = scatter("qk__", False), scatter("vo__", True)

    def weigh(target, product):
        for x in range(2):
            block = product(x * 2 + 1 - links.c).astype(bf16)
            target.core_out[x] = block.reshape(4, 2, 48, block.shape[-1])
        for x in range(2):
            block = product(x * 2 + links.c)
            target.kept[x] = block.reshape(4, 2, 48, block.shape[-1])

    def values_out(j):
        values = dot(layer.turned[...], layer.grad_proj[j, :, 256:384])
        return jnp.concatenate([values, dot(layer.turned_mid[...], layer.attn_low[j])], axis=1)

    layer.turn(layer.grad_top, layer.turned)
    weigh(down, lambda j: dot(layer.turned[...], layer.activated[j]))
    down.start()
    layer.feed_back(0)
    down.second()
    for j in range(1, mp):
        layer.feed_back(j)
    layer.turn(layer.normed_two, layer.turned)
    weigh(up, lambda j: dot(layer.turned[...], layer.grad_pre[j]))
    up.start()
    down.third()
    layer.middle_back()
    up.second()
    layer.turn(layer.middle_low, layer.turned_mid)
    for j in range(mp):
        layer.attend_grad(j)
    layer.attend_back(0, heads_before(mp, 0))
    down.fourth()
    up.third()
    layer.attend_back(1, heads_before(mp, 1))
    up.fourth()
    for j in range(2, mp):
        layer.attend_back(j, heads_before(mp, j))
    layer.turn(layer.normed_one, layer.turned)
    weigh(vo, values_out)
    vo.start()
    weigh(qk, lambda j: dot(layer.turned[...], layer.grad_proj[j, :, 0:256]))
    qk.start()
    vo.second()
    layer.entry_back()
    qk.second()
    vo.third()
    layer.proj_grad[...] = dot(layer.hidden[...], layer.pos_low[...], TN)
    layer.pos_grad[...] = dot(layer.points[...], layer.pre_grad[...], TN, highest)
    small = layer.small
    for i in range(3):
        lanes = slice(128 * i, 128 * i + 128)
        small[128 * i : 128 * i + 128, :] = layer.proj_grad[:, lanes]
        small[384 + 8 * i : 392 + 8 * i, :] = layer.vec_grad[:, lanes]
        small[416 + 8 * i : 424 + 8 * i, :] = stack_rows([layer.up_bias_grad[j, 0:1, lanes] for j in range(mp)])
    small[408:416, :] = layer.pos_grad[...]
    small[440:512, :] = jnp.zeros((72, 128), f32)
    layer.plane_out[...] = small[...].astype(bf16).reshape(8, 64, 128)
    layer.plane_in[links.plane] = layer.plane_out[links.plane]
    sums = []
    for k in range(1, 8):
        who = links.round(k)
        block = layer.plane_out.at[lax.rem(links.plane + k, 8)]
        sums.append(links.send(block, layer.plane_in.at[links.plane], who))
    qk.third()
    vo.fourth()
    layer.gather_rows(layer.middle_grad, layer.feats_grad)
    for k in range(1, 8):
        links.wait(sums[k - 1], layer.plane_in.at[lax.rem(links.plane + 8 - k, 8)])
    total = layer.plane_in[0].astype(f32)
    for i in range(1, 8):
        total = total + layer.plane_in[i].astype(f32)
    layer.line_out[...] = total.astype(bf16).reshape(4, 16, 128)
    layer.line_in[links.z] = layer.line_out[links.z]
    sums = []
    for k in range(1, 4):
        block = layer.line_out.at[lax.rem(links.z + k, 4)]
        sums.append(links.send(block, layer.line_in.at[links.z], links.far(k)))
    qk.fourth()
    own = layer.own_grad
    own[:, 512 + cols :] = down.end()
    own[:, 512 : 512 + cols] = up.end()
    own[:, 256:512] = vo.end()
    for k in range(1, 4):
        links.wait(sums[k - 1], layer.line_in.at[links.back(k)])
    total = layer.line_in[0].astype(f32)
    for i in range(1, 4):
        total = total + layer.line_in[i].astype(f32)
    layer.whole[links.plane, links.z] = total.astype(bf16)
    sums = []
    for k in range(1, 4):
        block = layer.whole.at[links.plane, links.z]
        sums.append(links.send(block, block, links.far(k)))
    own[:, 0:256] = qk.end()
    lead = (links.z * 2 + links.y == 0).astype(f32)
    weights = {name: load(refs, "weight", name) for name in PIECES}

    def all_sum(slots, planes, rows):
        slots[links.z] = rows
        marks = []
        for k in range(1, 4):
            block = slots.at[links.z]
            marks.append(links.send(block, block, links.far(k)))
        for k in range(1, 4):
            links.wait(marks[k - 1], slots.at[links.back(k)])
        planes[links.plane] = slots[0] + slots[1] + slots[2] + slots[3]
        marks = []
        for k in range(1, 8):
            block = planes.at[links.plane]
            marks.append(links.send(block, block, links.round(k)))
        return marks

    def all_end(planes, marks):
        for k in range(1, 8):
            links.wait(marks[k - 1], planes.at[lax.rem(links.plane + 8 - k, 8)])
        total = planes[0]
        for i in range(1, 8):
            total = total + planes[i]
        return total

    def five(parts):
        out = []
        for name in ("qkv", "out", "up", "bias", "down"):
            row = sum(square_row(p) for p in parts[name])
            out.append(row * lead if name == "bias" else row)
        return out

    rows = stack_rows([square_row(own[...])] + five(weights))
    marks = all_sum(layer.line_a, layer.plane_a, rows)
    for k in range(1, 4):
        links.wait(sums[k - 1], layer.whole.at[links.plane, links.back(k)])
    sums = []
    for k in range(1, 8):
        block = layer.whole.at[links.plane]
        sums.append(links.send(block, block, links.round(k)))
    for k in range(1, 8):
        links.wait(sums[k - 1], layer.whole.at[lax.rem(links.plane + 8 - k, 8)])
    small[...] = layer.whole[...].astype(f32).reshape(512, 128)
    first = all_end(layer.plane_a, marks)
    layer.small_out[...] = small[...]
    total = first[0:1] + square_row(small[0:440, :])
    factor = jnp.minimum(1.0, clip_max / (jnp.sqrt(total) + 1e-06))[0:1, 0:1]
    for copy in late:
        copy.wait()
    grads = own_parts(own, small, links.mp)
    ways = {}
    for name in ("qkv", "out", "up", "bias", "down"):
        ways[name] = [
            adam(g, factor, m, s, p)[3]
            for g, m, s, p in zip(grads[name], load(refs, "moment", name), load(refs, "second", name), weights[name])
        ]
    marks = all_sum(layer.line_b, layer.plane_b, stack_rows(five(ways)))
    second = all_end(layer.plane_b, marks)
    place = lax.broadcasted_iota(jnp.int32, (8, 128), 0)
    layer.sums[0:8, :] = jnp.where(place == 0, jnp.broadcast_to(total, (8, 128)), first)
    layer.sums[8:16, :] = second
    links.finish()


class _Shifted:
    def __init__(self, ref, start):
        self.ref, self.start = ref, start

    def __getitem__(self, i):
        return self.ref[self.start + i]


SHAPES = ("weight", "moment", "second")


def main_call(mp, inner, counts, feats, cotangent, points, params):
    clouds = counts.shape[0] // mp
    width = feats.shape[1]
    hid = params["proj_weight"].shape[0]
    cols = inner // mp
    smem, vmem = pl.BlockSpec(memory_space=pltpu.SMEM), pl.BlockSpec(memory_space=pltpu.VMEM)
    anywhere = pl.BlockSpec(memory_space=pl.ANY)
    inputs = {"counts_all": (counts, smem), "feats_all": (feats, anywhere), "top_all": (cotangent, anywhere)}
    inputs["points"] = (points, vmem)
    scratch = layer_scratch(mp, clouds, width, inner, hid)
    for name in PIECES:
        inputs[name + "_weight"] = (params[name + "_weight"], vmem)
        for kind in SHAPES[1:]:
            array = params[name + "_" + kind]
            inputs[name + "_" + kind + "_all"] = (array, anywhere)
            scratch[name + "_" + kind] = (array.shape, f32)
    outs = dict(
        block_out=((clouds * PAD, width), bf16),
        feats_grad=((clouds * PAD, width), f32),
        own_grad=((48, 512 + 2 * cols), f32),
        small_out=((512, 128), f32),
        sums=((16, 128), f32),
    )
    scratch.update(
        feats=((clouds * PAD, width), bf16),
        cotangent=((clouds * PAD, width), bf16),
        proj_low=((hid, width), bf16),
        pos_hidden=((8, hid), f32),
        w=((mp, 4, 2, 48, 512 + 2 * cols), bf16),
        up_bias=((mp, 8, cols), f32),
        up_bias_grad=((mp, 8, cols), f32),
        vec_grad=((8, width), f32),
        pos_grad=((8, hid), f32),
        proj_grad=((hid, width), f32),
        small=((512, 128), f32),
        plane_out=((8, 64, 128), bf16),
        plane_in=((8, 64, 128), bf16),
        line_out=((4, 16, 128), bf16),
        line_in=((4, 16, 128), bf16),
        whole=((8, 4, 16, 128), bf16),
        line_a=((4, 8, 128), f32),
        plane_a=((8, 8, 128), f32),
        line_b=((4, 8, 128), f32),
        plane_b=((8, 8, 128), f32),
    )
    for tag, n in (("down__", cols), ("up__", cols), ("qk__", 256), ("vo__", 256)):
        scratch.update(scatter_scratch(tag, n))
    sems = dict(send_sem=192, recv_sem=192, load_sem=18)
    names = list(inputs) + list(outs) + list(scratch) + list(sems)
    return pl.pallas_call(
        functools.partial(main_kernel, names, mp, clouds, width, inner),
        out_shape=[jax.ShapeDtypeStruct(*v) for v in outs.values()],
        in_specs=[v[1] for v in inputs.values()],
        out_specs=[vmem] * len(outs),
        scratch_shapes=[pltpu.VMEM(*v) for v in scratch.values()]
        + [pltpu.SemaphoreType.DMA((n,)) for n in sems.values()],
        compiler_params=pltpu.CompilerParams(
            vmem_limit_bytes=60 * 1024 * 1024, collective_id=0, has_side_effects=True
        ),
    )(*[v[0] for v in inputs.values()])


def update_kernel(names, *args):
    refs = dict(zip(names, args))
    copies = [
        pltpu.make_async_copy(refs["block_in"], refs["block_out"], refs["sem"].at[0]),
        pltpu.make_async_copy(refs["feats_in"], refs["feats_out"], refs["sem"].at[1]),
    ]
    for copy in copies:
        copy.start()
    mp = lax.axis_index("mp")
    sums = refs["sums"][...]
    clip = jnp.sqrt(sums[0:1])
    factor = jnp.minimum(1.0, clip_max / (clip + 1e-06))[0:1, 0:1]
    refs["clip_out"][...] = clip
    grads = own_parts(refs["own"], refs["small"], mp)
    order, squares, steps = 0, [], []
    for name in PIECES:
        weights = load(refs, "weight", name)
        parts = [
            adam(g, factor, m, s, p)
            for g, m, s, p in zip(grads[name], load(refs, "moment", name), load(refs, "second", name), weights)
        ]
        if order < 5:
            pair = [(sums[1 + order : 2 + order, 0:1], sums[8 + order : 9 + order, 0:1])]
        else:
            kept = 1 if name == "vector" else None
            pair = []
            for a in (weights[0], parts[0][3]):
                total = jnp.sum(a * a, axis=1, keepdims=True)
                pair.append(total if kept else jnp.sum(total, axis=0, keepdims=True))
            pair = [tuple(pair)]
        order += 1
        old, way = jnp.sqrt(pair[0][0]), jnp.sqrt(pair[0][1])
        squares.append((old, way))
        ratio = old / (way + 1e-06)
        for i, (weight, part) in enumerate(zip(weights, parts)):
            new = weight - learn_rate * ratio * part[3]
            stored = {"grad": part[0], "new": new, "m": part[1], "s": part[2], "copy": new.astype(bf16)}
            for kind, value in stored.items():
                ref = refs[name + "_out_" + kind]
                if name == "qkv":
                    ref[i] = value
                else:
                    ref[...] = value
    for side in range(2):
        column = jnp.concatenate([s[side] for s in squares], axis=0)
        refs["trust_out"][:, side : side + 1] = column
    for copy in copies:
        copy.wait()


OUT_KINDS = (("grad", f32), ("new", f32), ("m", f32), ("s", f32), ("copy", bf16))


def update_call(block, feats, own, small, sums, params):
    vmem = pl.BlockSpec(memory_space=pltpu.VMEM)
    anywhere = pl.BlockSpec(memory_space=pl.ANY)
    inputs = {"block_in": (block, anywhere), "feats_in": (feats, anywhere)}
    inputs.update(own=(own, vmem), small=(small, vmem), sums=(sums, vmem))
    for name in PIECES:
        for kind in SHAPES:
            inputs[name + "_" + kind] = (params[name + "_" + kind], vmem)
    outs = {"block_out": (block.shape, bf16, anywhere), "feats_out": (feats.shape, f32, anywhere)}
    outs["clip_out"] = ((1, 128), f32, vmem)
    outs["trust_out"] = ((14, 2), f32, vmem)
    for name in PIECES:
        for kind, dtype in OUT_KINDS:
            outs[name + "_out_" + kind] = (params[name + "_weight"].shape, dtype, vmem)
    names = list(inputs) + list(outs) + ["sem"]
    result = pl.pallas_call(
        functools.partial(update_kernel, names),
        out_shape=[jax.ShapeDtypeStruct(*v[:2]) for v in outs.values()],
        in_specs=[v[1] for v in inputs.values()],
        out_specs=[v[2] for v in outs.values()],
        scratch_shapes=[pltpu.SemaphoreType.DMA((2,))],
        compiler_params=pltpu.CompilerParams(vmem_limit_bytes=60 * 1024 * 1024),
    )(*[v[0] for v in inputs.values()])
    return dict(zip(outs, result))


def close_shards(*arrays):
    feats, centres, counts, cotangent = arrays[:4]
    mp_count = lax.axis_size("mp")
    mp_index = lax.axis_index("mp")
    share = feats.shape[0] // mp_count
    clouds = share // PAD
    inner = arrays[6].shape[1] * mp_count
    params = {}
    for k, kind in enumerate(SHAPES):
        for i, name in enumerate(PIECES):
            array = arrays[4 + 8 * k + i]
            if name in ("out", "down"):
                array = array.T
            if name == "bias":
                array = array[None]
            params[name + "_" + kind] = array
    mine = lax.dynamic_slice_in_dim(centres, mp_index * share, share, 1).T.reshape(clouds, PAD, 3)
    points = jnp.pad(mine, ((0, 0), (0, SLOT - PAD), (0, 0)))
    points = jnp.concatenate((points, jnp.ones((clouds, SLOT, 1), f32)), axis=2)
    points = jnp.pad(points.reshape(clouds * SLOT, 4), ((0, 0), (0, 4)))
    block, grad, own, small, sums = main_call(mp_count, inner, counts, feats, cotangent, points, params)
    out = update_call(block, grad, own, small, sums, params)
    outputs = [out["block_out"], out["feats_out"], out["clip_out"][0, 0], out["trust_out"].T]
    for name in PIECES:
        for kind, _ in OUT_KINDS:
            array = out[name + "_out_" + kind]
            if name in ("out", "down"):
                array = array.T
            if name == "bias":
                array = array[0]
            outputs.append(array)
    return tuple(outputs)


def solution(mesh):
    qkv, outw, upw, bias, whole = P(None, "dp", "mp"), P("mp", "dp"), P("dp", "mp"), P("mp"), P()
    params = (qkv, outw, upw, bias, outw, whole, whole, whole)
    in_specs = (P("dp", None), P(None, "dp"), P("dp"), P("dp", None)) + params * 3
    rows = P(("dp", "mp"), None)
    out_specs = (rows, rows, P(), P()) + tuple(spec for spec in params for _ in range(5))
    form = close_shards if (mesh.shape["dp"], mesh.shape["mp"]) == (8, 4) else shards
    return jax.shard_map(form, mesh=mesh, in_specs=in_specs, out_specs=out_specs, check_vma=False)
```

```python
import functools
import math

import jax
import jax.numpy as jnp
from jax import lax
from jax.experimental import pallas as pl
from jax.experimental.pallas import tpu as pltpu
from jax.sharding import PartitionSpec as P

HD = 64
PAD = 38
SLOT = 40
GROUP = 4

norm_eps = 1e-05
beta_one = 0.5
beta_two = 0.5
adam_eps = 1e-06
decay_rate = 0.01
learn_rate = 0.3
clip_max = 1.0
step_count = 3.0
neg_fill = -1e30
highest = lax.Precision.HIGHEST
f32 = jnp.float32
bf16 = jnp.bfloat16

NN = (((1,), (0,)), ((), ()))
NT = (((1,), (1,)), ((), ()))
TN = (((0,), (0,)), ((), ()))


def dot(a, b, dims=NN, precision=None):
    return lax.dot_general(a, b, dims, precision=precision, preferred_element_type=f32)


def gelu_pair(v):
    cdf = 0.5 * (1.0 + lax.erf(v * 0.7071067811865476))
    return v * cdf, cdf + v * jnp.exp(-0.5 * v * v) * 0.3989422804014327


def piece_squares(array, tensor_index):
    if tensor_index == 5:
        return jnp.sum(array * array, axis=1)
    return jnp.sum(array * array)[None]


def piece_ratio(trust_ratio, tensor_index):
    if tensor_index < 5:
        return trust_ratio[tensor_index]
    if tensor_index == 5:
        return trust_ratio[5:12][:, None]
    return trust_ratio[tensor_index + 6]


class Layer:
    def __init__(self, refs, mp, clouds, width, inner):
        self.__dict__.update(refs)
        self.mp = mp
        self.clouds = clouds
        self.width = width
        self.inner = inner
        self.rows = clouds * SLOT
        self.block = GROUP * SLOT
        self.blocks = clouds // GROUP
        self.hid = self.proj_low.shape[0]

    def live(self, j):
        return [h for h in range(2) if (2 * j + h) % 2 == 0 or j < self.mp // 2]

    def spread_rows(self):
        zeros = jnp.zeros((SLOT - PAD, self.width), f32)
        self.stage[...] = self.feats[...].astype(f32)
        for c in range(self.clouds):
            self.stream[pl.ds(SLOT * c, PAD), :] = self.stage[pl.ds(PAD * c, PAD), :]
            self.stream[pl.ds(SLOT * c + PAD, SLOT - PAD), :] = zeros
        self.stage[...] = self.cotangent[...].astype(f32)
        for c in range(self.clouds):
            self.middle_grad[pl.ds(SLOT * c, PAD), :] = self.stage[pl.ds(PAD * c, PAD), :]
            self.middle_grad[pl.ds(SLOT * c + PAD, SLOT - PAD), :] = zeros

    def keep_block(self, b, shape, dim):
        place = lax.broadcasted_iota(jnp.int32, shape, dim)
        bound = jnp.zeros(shape, jnp.int32)
        for i in range(GROUP):
            limit = self.counts[b * GROUP + i] + SLOT * i
            inside = (place >= SLOT * i) & (place < limit)
            bound = jnp.where(inside, 1, bound)
        return bound > 0

    def masks(self):
        n = self.block

        def step(b, carry):
            keys = lax.broadcasted_iota(jnp.int32, (n, n), 0)
            query = lax.broadcasted_iota(jnp.int32, (n, n), 1)
            fill = jnp.full((n, n), neg_fill, f32)
            for i in range(GROUP):
                limit = self.counts[b * GROUP + i] + SLOT * i
                inside = (keys >= SLOT * i) & (keys < limit)
                mine = (query >= SLOT * i) & (query < SLOT * (i + 1))
                fill = jnp.where(inside & mine, 0.0, fill)
            self.mask[b] = fill
            self.keep[pl.ds(b * n, n), :] = jnp.where(self.keep_block(b, (n, 128), 0), 1.0, 0.0)
            return carry

        lax.fori_loop(0, self.blocks, step, 0)

    def norm(self, x):
        centre = x - jnp.mean(x, axis=-1, keepdims=True)
        spread = jnp.mean(centre * centre, axis=-1, keepdims=True)
        rate = lax.rsqrt(spread + norm_eps)
        return centre * rate, rate

    def norm_back(self, grad, hat, rate, gain):
        scaled = grad * gain
        first = jnp.mean(scaled, axis=-1, keepdims=True)
        second = jnp.mean(scaled * hat, axis=-1, keepdims=True)
        return rate * (scaled - first - hat * second)

    def entry(self):
        value, slope = gelu_pair(dot(self.points[...], self.pos_hidden[...], NN, highest))
        hidden = value.astype(bf16)
        self.pos_slope[...] = slope
        self.hidden[...] = hidden
        x = self.stream[...] + (dot(hidden, self.proj_low[...]) + self.vec[6:7, :])
        hat, rate = self.norm(x)
        self.stream[...] = x
        self.hat_one[...] = hat
        self.rate_one[...] = jnp.broadcast_to(rate, (self.rows, 128))
        self.normed_one[...] = (hat * self.vec[0:1, :] + self.vec[2:3, :]).astype(bf16)

    def project(self):
        for j in range(self.mp):
            self.qkv[j] = dot(self.normed_one[...], self.w_qkv(j)).astype(bf16)

    def lanes(self, h, n):
        lane = lax.broadcasted_iota(jnp.int32, (n, 128), 1)
        return (lane < HD) if h == 0 else (lane >= HD)

    def heads(self, rows):
        for j in range(self.mp):
            query = self.qkv[j, rows, 0:128] * jnp.asarray(1.0 / math.sqrt(HD), bf16)
            for h in self.live(j):
                own = self.lanes(h, self.block)
                alone = jnp.where(own, query, jnp.zeros_like(query))
                yield j, own, alone, self.qkv[j, rows, 128:256], self.qkv[j, rows, 256:384]

    def attend(self):
        n = self.block

        def step(b, carry):
            rows = pl.ds(pl.multiple_of(b * n, n), n)
            mask = self.mask[b]
            live = list(self.heads(rows))
            scores = [dot(keys, query, NT) + mask for _, _, query, keys, _ in live]
            low = []
            for i, score in enumerate(scores):
                expo = jnp.exp(score - jnp.max(score, axis=0, keepdims=True))
                probs = expo * (1.0 / jnp.sum(expo, axis=0, keepdims=True))
                self.probs[i, b] = probs
                low.append(probs.astype(bf16))
            mixed = [jnp.zeros((n, 128), f32)] * self.mp
            for probs, (j, own, _, _, values) in zip(low, live):
                mixed[j] = jnp.where(own, dot(probs, values, TN), mixed[j])
            for j in range(self.mp):
                self.attn_low[j, rows, :] = mixed[j].astype(bf16)
            return carry

        lax.fori_loop(0, self.blocks, step, 0, unroll=2)

    def middle(self):
        x = self.stream[...] + self.vec[4:5, :]
        for j in range(self.mp):
            x = x + dot(self.attn_low[j], self.w_out(j), NT)
        hat, rate = self.norm(x)
        self.stream[...] = x
        self.hat_two[...] = hat
        self.rate_two[...] = jnp.broadcast_to(rate, (self.rows, 128))
        self.normed_two[...] = (hat * self.vec[1:2, :] + self.vec[3:4, :]).astype(bf16)

    def feed(self):
        total = self.stream[...]
        for j in range(self.mp):
            pre = dot(self.normed_two[...], self.w_up(j)) + self.up_bias[j, 0:1, :]
            value, slope = gelu_pair(pre)
            low = value.astype(bf16)
            self.activated[j] = low
            self.slope[j] = slope
            total = total + dot(low, self.w_down(j), NT)
        self.stream[...] = total

    def top(self):
        keep = jnp.concatenate([self.keep[...]] * (self.width // 128), axis=1)
        self.stream[...] = (self.stream[...] + self.vec[5:6, :]) * keep

    def grad_start(self):
        self.vec_grad[...] = jnp.zeros_like(self.vec_grad)
        keep = jnp.concatenate([self.keep[...]] * (self.width // 128), axis=1)
        grad = self.middle_grad[...] * keep
        self.middle_grad[...] = grad
        self.grad_top[...] = grad.astype(bf16)
        self.vec_grad[5:6, :] = jnp.sum(grad, axis=0, keepdims=True)

    def feed_back(self):
        total = None
        for j in range(self.mp):
            grad = dot(self.grad_top[...], self.w_down(j)) * self.slope[j]
            low = grad.astype(bf16)
            self.grad_pre[j] = low
            self.up_bias_grad[j, 0:1, :] = jnp.sum(low.astype(f32), axis=0, keepdims=True)
            term = dot(low, self.w_up(j), NT)
            total = term if j == 0 else total + term
        self.normed_grad[...] = total

    def middle_back(self):
        grad, hat = self.normed_grad[...], self.hat_two[...]
        rate = jnp.concatenate([self.rate_two[...]] * (self.width // 128), axis=1)
        self.vec_grad[1:2, :] = jnp.sum(grad * hat, axis=0, keepdims=True)
        self.vec_grad[3:4, :] = jnp.sum(grad, axis=0, keepdims=True)
        out = self.middle_grad[...] + self.norm_back(grad, hat, rate, self.vec[1:2, :])
        self.middle_grad[...] = out
        self.vec_grad[4:5, :] = jnp.sum(out, axis=0, keepdims=True)
        low = out.astype(bf16)
        self.middle_low[...] = low
        for j in range(self.mp):
            self.attn_grad[j] = dot(low, self.w_out(j)).astype(bf16)

    def attend_back(self):
        n = self.block
        scale = 1.0 / math.sqrt(HD)

        def step(b, carry):
            rows = pl.ds(pl.multiple_of(b * n, n), n)
            live = list(self.heads(rows))
            mine = []
            for j, own, _, _, _ in live:
                grad = self.attn_grad[j, rows, :]
                mine.append(jnp.where(own, grad, jnp.zeros_like(grad)))
            grad_probs = [dot(values, g, NT) for g, (_, _, _, _, values) in zip(mine, live)]
            scores = []
            grad_values = [jnp.zeros((n, 128), f32)] * self.mp
            for i, (j, _, _, _, _) in enumerate(live):
                probs = self.probs[i, b]
                grad_values[j] = grad_values[j] + dot(probs.astype(bf16), mine[i])
                inner = jnp.sum(probs * grad_probs[i], axis=0, keepdims=True)
                scores.append((probs * (grad_probs[i] - inner)).astype(bf16))
            grad_query = [jnp.zeros((n, 128), f32)] * self.mp
            grad_keys = [jnp.zeros((n, 128), f32)] * self.mp
            for grad, (j, own, query, keys, _) in zip(scores, live):
                grad_keys[j] = grad_keys[j] + dot(grad, query)
                grad_query[j] = jnp.where(own, dot(grad, keys, TN), grad_query[j])
            for j in range(self.mp):
                self.grad_proj[j, rows, 0:128] = (grad_query[j] * scale).astype(bf16)
                self.grad_proj[j, rows, 128:256] = grad_keys[j].astype(bf16)
                self.grad_proj[j, rows, 256:384] = grad_values[j].astype(bf16)
            return carry

        lax.fori_loop(0, self.blocks, step, 0, unroll=2)

    def entry_back(self):
        grad = None
        for j in range(self.mp):
            term = dot(self.grad_proj[j], self.w_qkv(j), NT)
            grad = term if j == 0 else grad + term
        hat = self.hat_one[...]
        rate = jnp.concatenate([self.rate_one[...]] * (self.width // 128), axis=1)
        self.vec_grad[0:1, :] = jnp.sum(grad * hat, axis=0, keepdims=True)
        self.vec_grad[2:3, :] = jnp.sum(grad, axis=0, keepdims=True)
        out = self.middle_grad[...] + self.norm_back(grad, hat, rate, self.vec[0:1, :])
        self.middle_grad[...] = out
        self.vec_grad[6:7, :] = jnp.sum(out, axis=0, keepdims=True)
        low = out.astype(bf16)
        self.pos_low[...] = low
        self.pre_grad[...] = dot(low, self.proj_low[...], NT) * self.pos_slope[...]

    def turn(self, source, target):
        for i in range(self.rows // 128):
            target[:, 128 * i : 128 * i + 128] = source[128 * i : 128 * i + 128, :].T

    def gather_rows(self, source, target):
        for c in range(self.clouds):
            target[pl.ds(PAD * c, PAD), :] = source[pl.ds(SLOT * c, PAD), :]


def layer_scratch(mp, clouds, width, inner, hid):
    rows = clouds * SLOT
    block = GROUP * SLOT
    cols = inner // mp
    heads = mp + mp // 2
    shapes = dict(
        stage=((clouds * PAD, width), f32),
        stream=((rows, width), f32),
        middle_grad=((rows, width), f32),
        mask=((clouds // GROUP, block, block), f32),
        keep=((rows, 128), f32),
        pos_slope=((rows, hid), f32),
        hidden=((rows, hid), bf16),
        hat_one=((rows, width), f32),
        rate_one=((rows, 128), f32),
        normed_one=((rows, width), bf16),
        qkv=((mp, rows, 384), bf16),
        probs=((heads, clouds // GROUP, block, block), f32),
        attn_low=((mp, rows, 128), bf16),
        hat_two=((rows, width), f32),
        rate_two=((rows, 128), f32),
        normed_two=((rows, width), bf16),
        activated=((mp, rows, cols), bf16),
        slope=((mp, rows, cols), f32),
        grad_top=((rows, width), bf16),
        grad_pre=((mp, rows, cols), bf16),
        normed_grad=((rows, width), f32),
        middle_low=((rows, width), bf16),
        attn_grad=((mp, rows, 128), bf16),
        grad_proj=((mp, rows, 384), bf16),
        pos_low=((rows, width), bf16),
        pre_grad=((rows, hid), f32),
        turned=((width, rows), bf16),
        turned_mid=((width, rows), bf16),
    )
    return shapes


def compute_kernel(names, mp, clouds, width, inner, *args):
    refs = dict(zip(names, args))
    layer = Layer(refs, mp, clouds, width, inner)
    w = layer.w
    cols = inner // mp
    layer.w_qkv = lambda j: w[j, :, 0:384]
    layer.w_out = lambda j: w[j, :, 384:512]
    layer.w_up = lambda j: w[j, :, 512 : 512 + cols]
    layer.w_down = lambda j: w[j, :, 512 + cols : 512 + 2 * cols]
    layer.proj_low[...] = layer.pos_proj[...].astype(bf16)
    layer.spread_rows()
    layer.masks()
    layer.entry()
    layer.project()
    layer.attend()
    layer.middle()
    layer.feed()
    layer.top()
    layer.gather_rows(layer.stream, layer.stage)
    layer.block_out[...] = layer.stage[...].astype(bf16)
    layer.grad_start()
    layer.feed_back()
    g = layer.grads
    layer.turn(layer.grad_top, layer.turned)
    for j in range(mp):
        g[j, :, 512 + cols : 512 + 2 * cols] = dot(layer.turned[...], layer.activated[j])
    layer.turn(layer.normed_two, layer.turned)
    for j in range(mp):
        g[j, :, 512 : 512 + cols] = dot(layer.turned[...], layer.grad_pre[j])
    layer.middle_back()
    layer.turn(layer.middle_low, layer.turned)
    for j in range(mp):
        g[j, :, 384:512] = dot(layer.turned[...], layer.attn_low[j])
    layer.attend_back()
    layer.turn(layer.normed_one, layer.turned)
    for j in range(mp):
        g[j, :, 0:384] = dot(layer.turned[...], layer.grad_proj[j])
    layer.entry_back()
    layer.gather_rows(layer.middle_grad, layer.feats_grad)
    layer.proj_grad[...] = dot(layer.hidden[...], layer.pos_low[...], TN)
    layer.pos_grad[...] = dot(layer.points[...], layer.pre_grad[...], TN, highest)


def compute(mp, width, inner, counts, feats, cotangent, points, w, up_bias, vec, pos_hidden, pos_proj):
    clouds = counts.shape[0]
    hid = pos_proj.shape[0]
    inputs = ["counts", "feats", "cotangent", "points", "w", "up_bias", "vec", "pos_hidden", "pos_proj"]
    outs = dict(
        block_out=((clouds * PAD, width), bf16),
        feats_grad=((clouds * PAD, width), f32),
        grads=(w.shape, f32),
        up_bias_grad=((mp, 8, inner // mp), f32),
        vec_grad=((8, width), f32),
        pos_grad=((8, hid), f32),
        proj_grad=((hid, width), f32),
    )
    scratch = layer_scratch(mp, clouds, width, inner, hid)
    scratch["proj_low"] = ((hid, width), bf16)
    names = inputs + list(outs) + list(scratch)
    vmem = pl.BlockSpec(memory_space=pltpu.VMEM)
    return pl.pallas_call(
        functools.partial(compute_kernel, names, mp, clouds, width, inner),
        out_shape=[jax.ShapeDtypeStruct(*v) for v in outs.values()],
        in_specs=[pl.BlockSpec(memory_space=pltpu.SMEM)] + [vmem] * (len(inputs) - 1),
        out_specs=[vmem] * len(outs),
        scratch_shapes=[pltpu.VMEM(*v) for v in scratch.values()],
        compiler_params=pltpu.CompilerParams(vmem_limit_bytes=60 * 1024 * 1024),
    )(counts, feats, cotangent, points, w, up_bias, vec, pos_hidden, pos_proj)


def shards(
    feats,
    centres,
    counts,
    cotangent,
    qkv_weight,
    out_weight,
    up_weight,
    up_bias,
    down_weight,
    norm_vectors,
    pos_hidden,
    pos_proj,
    qkv_moment,
    out_moment,
    up_moment,
    bias_moment,
    down_moment,
    vector_moment,
    hidden_moment,
    proj_moment,
    qkv_second,
    out_second,
    up_second,
    bias_second,
    down_second,
    vector_second,
    hidden_second,
    proj_second,
):
    mp_count = lax.axis_size("mp")
    mp_index = lax.axis_index("mp")
    dp_index = lax.axis_index("dp")
    share = feats.shape[0] // mp_count
    clouds = share // PAD
    width = feats.shape[1]
    cols = up_weight.shape[1]
    inner = cols * mp_count
    start = mp_index * share
    my_feats = lax.dynamic_slice_in_dim(feats, start, share, 0)
    my_top = lax.dynamic_slice_in_dim(cotangent, start, share, 0)
    my_counts = lax.dynamic_slice_in_dim(counts, mp_index * clouds, clouds, 0)
    my_points = lax.dynamic_slice_in_dim(centres, start, share, 1).T.reshape(clouds, PAD, 3)
    points = jnp.pad(my_points, ((0, 0), (0, SLOT - PAD), (0, 0)))
    points = jnp.concatenate((points, jnp.ones((clouds, SLOT, 1), f32)), axis=2)
    points = jnp.pad(points.reshape(clouds * SLOT, 4), ((0, 0), (0, 4)))
    packed = jnp.concatenate(
        (qkv_weight[0], qkv_weight[1], qkv_weight[2], out_weight.T, up_weight, down_weight.T), axis=1
    ).astype(bf16)
    whole = lax.all_gather(packed, "dp", axis=0, tiled=True)
    whole = lax.all_gather(whole, "mp", axis=0)
    bias = lax.all_gather(jnp.broadcast_to(up_bias[None], (8, cols)), "mp", axis=0)
    vec = jnp.pad(norm_vectors, ((0, 1), (0, 0)))
    hidden = jnp.pad(pos_hidden, ((0, 4), (0, 0)))
    block_out, feats_grad, grads, bias_grad, vec_grad, pos_grad, proj_grad = compute(
        mp_count, width, inner, my_counts, my_feats, my_top, points, whole, bias, vec, hidden, pos_proj
    )
    own = lax.psum_scatter(grads, "mp", scatter_dimension=0, tiled=True)[0]
    own = lax.psum_scatter(own, "dp", scatter_dimension=0, tiled=True)
    bias_grad, vector_grad, pos_grad, proj_grad = lax.psum(
        (bias_grad[:, 0], vec_grad[:7], pos_grad[:4], proj_grad), ("dp", "mp")
    )
    bias_grad = lax.dynamic_index_in_dim(bias_grad, mp_index, 0, keepdims=False)
    qkv_grad = jnp.stack((own[:, 0:128], own[:, 128:256], own[:, 256:384]))
    out_grad = own[:, 384:512].T
    up_grad = own[:, 512 : 512 + cols]
    down_grad = own[:, 512 + cols :].T
    leader = ((dp_index == 0) & (mp_index == 0)).astype(f32)
    first_dp = (dp_index == 0).astype(f32)
    owners = [1.0, 1.0, 1.0, first_dp, 1.0, leader, leader, leader]
    weights = [qkv_weight, out_weight, up_weight, up_bias, down_weight, norm_vectors, pos_hidden, pos_proj]
    moments = [
        qkv_moment,
        out_moment,
        up_moment,
        bias_moment,
        down_moment,
        vector_moment,
        hidden_moment,
        proj_moment,
    ]
    seconds = [
        qkv_second,
        out_second,
        up_second,
        bias_second,
        down_second,
        vector_second,
        hidden_second,
        proj_second,
    ]
    grads = [qkv_grad, out_grad, up_grad, bias_grad, down_grad, vector_grad, pos_grad, proj_grad]
    grad_square = jnp.zeros((), f32)
    weight_square = []
    for i in range(8):
        grad_square = grad_square + owners[i] * jnp.sum(grads[i] * grads[i])
        weight_square.append(owners[i] * piece_squares(weights[i], i))
    totals = lax.psum(jnp.concatenate([grad_square[None]] + weight_square), ("dp", "mp"))
    clip_norm = jnp.sqrt(totals[0])
    factor = jnp.minimum(1.0, clip_max / (clip_norm + 1e-06))
    clipped_list, moment_list, second_list, direction_list, update_square = [], [], [], [], []
    for i in range(8):
        clipped = grads[i] * factor
        moment_new = beta_one * moments[i] + (1.0 - beta_one) * clipped
        second_new = beta_two * seconds[i] + (1.0 - beta_two) * clipped * clipped
        direction = (
            moment_new
            / (1.0 - beta_one**step_count)
            / (jnp.sqrt(second_new / (1.0 - beta_two**step_count)) + adam_eps)
            + decay_rate * weights[i]
        )
        clipped_list.append(clipped)
        moment_list.append(moment_new)
        second_list.append(second_new)
        direction_list.append(direction)
        update_square.append(owners[i] * piece_squares(direction, i))
    update_total = lax.psum(jnp.concatenate(update_square), ("dp", "mp"))
    weight_norm = jnp.sqrt(totals[1:])
    update_norm = jnp.sqrt(update_total)
    trust_ratio = weight_norm / (update_norm + 1e-06)
    outputs = [block_out, feats_grad, clip_norm, jnp.stack((weight_norm, update_norm))]
    for i in range(8):
        new_weight = weights[i] - learn_rate * piece_ratio(trust_ratio, i) * direction_list[i]
        outputs.append(clipped_list[i])
        outputs.append(new_weight)
        outputs.append(moment_list[i])
        outputs.append(second_list[i])
        outputs.append(new_weight.astype(bf16))
    return tuple(outputs)


class Links:
    def __init__(self, send, recv):
        dp, mp = lax.axis_index("dp"), lax.axis_index("mp")
        self.z, self.y = dp // 2, lax.rem(dp, 2)
        self.x, self.c = mp // 2, lax.rem(mp, 2)
        self.mp = mp
        self.plane = self.y * 4 + mp
        self.send_sem, self.recv_sem = send, recv
        self.count = 0
        self.sent = []

    def at(self, z, y, x, c):
        return (z * 2 + y, x * 2 + c)

    def core(self):
        return self.at(self.z, self.y, self.x, 1 - self.c)

    def side(self):
        return self.at(self.z, self.y, 1 - self.x, self.c)

    def deep(self):
        return self.at(self.z, 1 - self.y, self.x, self.c)

    def far(self, k):
        return self.at(lax.rem(self.z + k, 4), self.y, self.x, self.c)

    def back(self, k):
        return lax.rem(self.z + 4 - k, 4)

    def round(self, k):
        other = lax.rem(self.plane + k, 8)
        return (self.z * 2 + other // 4, lax.rem(other, 4))

    def peers(self):
        return [self.far(k) for k in range(1, 4)] + [self.round(k) for k in range(1, 8)]

    def greet(self):
        barrier = pltpu.get_barrier_semaphore()
        for who in self.peers():
            pl.semaphore_signal(barrier, inc=1, device_id=who, device_id_type=pl.DeviceIdType.MESH)

    def met(self):
        pl.semaphore_wait(pltpu.get_barrier_semaphore(), 10)

    def copy(self, source, target, who, i):
        return pltpu.make_async_remote_copy(
            src_ref=source,
            dst_ref=target,
            send_sem=self.send_sem.at[i],
            recv_sem=self.recv_sem.at[i],
            device_id=who,
            device_id_type=pl.DeviceIdType.MESH,
        )

    def send(self, source, target, who):
        i = self.count
        self.count += 1
        copy = self.copy(source, target, who, i)
        copy.start()
        self.sent.append(copy)
        return i

    def wait(self, i, target):
        self.copy(target, target, self.core(), i).wait_recv()

    def finish(self):
        for copy in self.sent:
            copy.wait_send()


class Gather:
    def __init__(self, links, w, lo, hi, flip):
        self.links, self.w, self.lo, self.hi, self.flip = links, w, lo, hi, flip

    def part(self, mp, z, y):
        return self.w.at[mp, z, y, :, self.lo : self.hi]

    def spread(self, block):
        k = self.links
        return (k.send(block, block, k.deep()), k.send(block, block, k.side()), k.send(block, block, k.core()))

    def start(self):
        k = self.links
        own = self.part(k.mp, k.z, k.y)
        self.along = [k.send(own, own, k.far(i)) for i in (3, 2, 1)][::-1]
        self.spreads = [self.spread(own)]

    def second(self):
        k = self.links
        for i in (1, 2, 3):
            block = self.part(k.mp, k.back(i), k.y)
            k.wait(self.along[i - 1], block)
            self.spreads.append(self.spread(block))

    def third(self):
        k = self.links
        other = k.mp + 2 - 4 * k.x
        for i in range(4):
            z = k.back(i)
            if self.flip:
                k.wait(self.spreads[i][1], self.part(other, z, k.y))
            else:
                k.wait(self.spreads[i][0], self.part(k.mp, z, 1 - k.y))
        if self.flip:
            block = self.part(other, slice(None), k.y)
            self.wide = k.send(block, block, k.deep())
            self.core_first = k.send(block, block, k.core())
        else:
            block = self.part(k.mp, slice(None), 1 - k.y)
            self.wide = k.send(block, block, k.side())
            self.core_first = k.send(block, block, k.core())

    def fourth(self):
        k = self.links
        other = k.mp + 2 - 4 * k.x
        for i in range(4):
            z = k.back(i)
            if self.flip:
                k.wait(self.spreads[i][0], self.part(k.mp, z, 1 - k.y))
            else:
                k.wait(self.spreads[i][1], self.part(other, z, k.y))
        if self.flip:
            near = self.part(k.mp, slice(None), 1 - k.y)
            self.core_second = k.send(near, near, k.core())
            self.far_wait = self.part(other, slice(None), 1 - k.y)
            k.wait(self.wide, self.far_wait)
            self.core_third = k.send(self.far_wait, self.far_wait, k.core())
        else:
            near = self.part(other, slice(None), k.y)
            self.core_second = k.send(near, near, k.core())
            self.far_wait = self.part(other, slice(None), 1 - k.y)
            k.wait(self.wide, self.far_wait)
            self.core_third = k.send(self.far_wait, self.far_wait, k.core())

    def end(self):
        k = self.links
        twin = k.mp + 1 - 2 * k.c
        other = twin + 2 - 4 * k.x
        for i in range(4):
            k.wait(self.spreads[i][2], self.part(twin, k.back(i), k.y))
        if self.flip:
            k.wait(self.core_first, self.part(other, slice(None), k.y))
            k.wait(self.core_second, self.part(twin, slice(None), 1 - k.y))
        else:
            k.wait(self.core_first, self.part(twin, slice(None), 1 - k.y))
            k.wait(self.core_second, self.part(other, slice(None), k.y))
        k.wait(self.core_third, self.part(other, slice(None), 1 - k.y))


class Scatter:
    def __init__(self, links, refs, flip):
        self.links, self.flip = links, flip
        self.__dict__.update(refs)

    def start(self):
        k = self.links
        self.first = k.send(self.core_out, self.core_in, k.core())

    def pair(self, x, z, y):
        return self.kept[x, z, y] + self.core_in[x, z, y].astype(f32)

    def second(self):
        k = self.links
        k.wait(self.first, self.core_in)
        if self.flip:
            for x in range(2):
                for z in range(4):
                    self.next_out[x, z] = self.pair(x, z, 1 - k.y).astype(bf16)
            self.next = k.send(self.next_out, self.next_in, k.deep())
        else:
            for y in range(2):
                for z in range(4):
                    self.next_out[y, z] = self.pair(1 - k.x, z, y).astype(bf16)
            self.next = k.send(self.next_out, self.next_in, k.side())

    def third(self):
        k = self.links
        k.wait(self.next, self.next_in)
        for z in range(4):
            if self.flip:
                total = self.pair(1 - k.x, z, k.y) + self.next_in[1 - k.x, z].astype(f32)
            else:
                total = self.pair(k.x, z, 1 - k.y) + self.next_in[1 - k.y, z].astype(f32)
            self.last_out[z] = total.astype(bf16)
        self.last = k.send(self.last_out, self.last_in, k.side() if self.flip else k.deep())

    def fourth(self):
        k = self.links
        k.wait(self.last, self.last_in)
        self.along = []
        for i in range(4):
            z = lax.rem(k.z + i, 4)
            mid = self.next_in[k.x, z] if self.flip else self.next_in[k.y, z]
            total = self.pair(k.x, z, k.y) + mid.astype(f32) + self.last_in[z].astype(f32)
            if i == 0:
                self.own[...] = total
            else:
                self.far_out[i - 1] = total.astype(bf16)
                self.along.append(k.send(self.far_out.at[i - 1], self.far_in.at[i - 1], k.far(i)))

    def end(self):
        k = self.links
        total = self.own[...]
        for i in range(3):
            k.wait(self.along[i], self.far_in.at[i])
            total = total + self.far_in[i].astype(f32)
        return total


def scatter_scratch(tag, cols):
    return {
        tag + "kept": ((2, 4, 2, 48, cols), f32),
        tag + "core_out": ((2, 4, 2, 48, cols), bf16),
        tag + "core_in": ((2, 4, 2, 48, cols), bf16),
        tag + "next_out": ((2, 4, 48, cols), bf16),
        tag + "next_in": ((2, 4, 48, cols), bf16),
        tag + "last_out": ((4, 48, cols), bf16),
        tag + "last_in": ((4, 48, cols), bf16),
        tag + "far_out": ((3, 48, cols), bf16),
        tag + "far_in": ((3, 48, cols), bf16),
        tag + "own": ((48, cols), f32),
    }


def stack_rows(rows, height=8):
    place = lax.broadcasted_iota(jnp.int32, (height, 128), 0)
    out = jnp.zeros((height, 128), f32)
    for i, row in enumerate(rows):
        out = jnp.where(place == i, jnp.broadcast_to(row, (height, 128)), out)
    return out


def square_row(array):
    total = jnp.sum(jnp.sum(array * array, axis=0, keepdims=True), axis=1, keepdims=True)
    return jnp.broadcast_to(total, (1, 128))


def adam(grad, factor, moment, second, weight):
    clipped = grad * factor
    moment_new = beta_one * moment + (1.0 - beta_one) * clipped
    second_new = beta_two * second + (1.0 - beta_two) * clipped * clipped
    direction = (
        moment_new
        / (1.0 - beta_one**step_count)
        / (jnp.sqrt(second_new / (1.0 - beta_two**step_count)) + adam_eps)
        + decay_rate * weight
    )
    return clipped, moment_new, second_new, direction


PIECES = ("qkv", "out", "up", "bias", "down", "vector", "hidden", "proj")


def own_parts(own, small, mp):
    cols = (own.shape[1] - 512) // 2

    def wide(row, count):
        return jnp.concatenate([small[row + 8 * i : row + 8 * i + count, :] for i in range(3)], axis=1)

    place = lax.broadcasted_iota(jnp.int32, (8, cols), 0)

    return {
        "qkv": [own[:, 128 * i : 128 * i + 128] for i in range(3)],
        "out": [own[:, 384:512]],
        "up": [own[:, 512 : 512 + cols]],
        "bias": [jnp.sum(jnp.where(place == mp, wide(416, 8), 0.0), axis=0, keepdims=True)],
        "down": [own[:, 512 + cols : 512 + 2 * cols]],
        "vector": [wide(384, 7)],
        "hidden": [small[408:412, :]],
        "proj": [jnp.concatenate([small[128 * i : 128 * i + 128, :] for i in range(3)], axis=1)],
    }


def load(refs, kind, name):
    ref = refs[name + "_" + kind]
    if name == "qkv":
        return [ref[i] for i in range(3)]
    return [ref[...].reshape(1, -1)] if name == "bias" else [ref[...]]


def main_kernel(names, mp, clouds, width, inner, *args):
    refs = dict(zip(names, args))
    layer = Layer(refs, mp, clouds, width, inner)
    cols = inner // mp
    links = Links(layer.send_sem, layer.recv_sem)
    w = layer.w
    links.greet()
    share = clouds * PAD
    rows = pl.ds(pl.multiple_of(links.mp * share, 16), share)
    local = [
        pltpu.make_async_copy(layer.feats_all.at[rows, :], layer.feats, layer.load_sem.at[0]),
        pltpu.make_async_copy(layer.top_all.at[rows, :], layer.cotangent, layer.load_sem.at[1]),
    ]
    late = []
    for i, name in enumerate(name for name in PIECES for kind in ("moment", "second")):
        kind = ("moment", "second")[i % 2]
        source, target = refs[name + "_" + kind + "_all"], refs[name + "_" + kind]
        late.append(pltpu.make_async_copy(source, target, layer.load_sem.at[2 + i]))
    for copy in local + late:
        copy.start()

    def flat(j, lo, hi):
        return w[j, :, :, :, lo:hi].reshape(width, hi - lo)

    layer.w_qkv = lambda j: flat(j, 0, 384)
    layer.w_out = lambda j: flat(j, 384, 512)
    layer.w_up = lambda j: flat(j, 512, 512 + cols)
    layer.w_down = lambda j: flat(j, 512 + cols, 512 + 2 * cols)
    for i in range(3):
        w[links.mp, links.z, links.y, :, 128 * i : 128 * i + 128] = refs["qkv_weight"][i].astype(bf16)
    w[links.mp, links.z, links.y, :, 384:512] = refs["out_weight"][...].astype(bf16)
    w[links.mp, links.z, links.y, :, 512 : 512 + cols] = refs["up_weight"][...].astype(bf16)
    w[links.mp, links.z, links.y, :, 512 + cols : 512 + 2 * cols] = refs["down_weight"][...].astype(bf16)
    layer.up_bias[links.mp] = jnp.broadcast_to(refs["bias_weight"][...].reshape(1, cols), (8, cols))
    links.met()
    gathers = [
        Gather(links, w, 0, 256, False),
        Gather(links, w, 256, 512, True),
        Gather(links, w, 512, 512 + cols, False),
        Gather(links, w, 512 + cols, 512 + 2 * cols, True),
    ]
    for g in gathers[:2]:
        g.start()
    own_bias = layer.up_bias.at[links.mp]
    bias_side = links.send(own_bias, own_bias, links.side())
    bias_core = links.send(own_bias, own_bias, links.core())
    for g in gathers[2:]:
        g.start()
    layer.proj_low[...] = refs["proj_weight"][...].astype(bf16)
    layer.vec = refs["vector_weight"]
    layer.pos_hidden[...] = jnp.zeros((8, 128), f32)
    layer.pos_hidden[0:4, :] = refs["hidden_weight"][...]
    for copy in local:
        copy.wait()
    layer.counts = _Shifted(layer.counts_all, links.mp * clouds)
    layer.spread_rows()
    for g in gathers[:2]:
        g.second()
    layer.masks()
    for g in gathers[:2]:
        g.third()
    layer.entry()
    for g in gathers[2:]:
        g.second()
    for g in gathers[:2]:
        g.fourth()
    other_bias = layer.up_bias.at[links.mp + 2 - 4 * links.x]
    links.wait(bias_side, other_bias)
    bias_last = links.send(other_bias, other_bias, links.core())
    for g in gathers[:2]:
        g.end()
    layer.project()
    for g in gathers[2:]:
        g.third()
    layer.attend()
    for g in gathers[2:]:
        g.fourth()
    layer.middle()
    for g in gathers[2:]:
        g.end()
    twin = links.mp + 1 - 2 * links.c
    links.wait(bias_core, layer.up_bias.at[twin])
    links.wait(bias_last, layer.up_bias.at[twin + 2 - 4 * links.x])
    layer.feed()

    def scatter(tag, flip):
        return Scatter(links, {n[len(tag) :]: refs[n] for n in names if n.startswith(tag)}, flip)

    down, up = scatter("down__", True), scatter("up__", False)
    qk, vo = scatter("qk__", False), scatter("vo__", True)

    def weigh(product, *targets):
        for x in range(2):
            pair = [product(2 * x), product(2 * x + 1)]
            kept = jnp.where(links.c == 0, pair[0], pair[1])
            sent = jnp.where(links.c == 0, pair[1], pair[0]).astype(bf16)
            lo = 0
            for target in targets:
                hi = lo + target.kept.shape[-1]
                target.core_out[x] = sent[:, lo:hi].reshape(4, 2, 48, hi - lo)
                target.kept[x] = kept[:, lo:hi].reshape(4, 2, 48, hi - lo)
                lo = hi

    def heads_out(j):
        parts = dot(layer.turned[...], layer.grad_proj[j]), dot(layer.turned_mid[...], layer.attn_low[j])
        return jnp.concatenate(parts, axis=1)

    layer.grad_start()
    layer.turn(layer.grad_top, layer.turned)
    weigh(lambda j: dot(layer.turned[...], layer.activated[j]), down)
    down.start()
    layer.top()
    layer.gather_rows(layer.stream, layer.stage)
    layer.block_out[...] = layer.stage[...].astype(bf16)
    down.second()
    layer.feed_back()
    layer.turn(layer.normed_two, layer.turned)
    weigh(lambda j: dot(layer.turned[...], layer.grad_pre[j]), up)
    up.start()
    down.third()
    layer.middle_back()
    up.second()
    layer.turn(layer.middle_low, layer.turned_mid)
    down.fourth()
    layer.attend_back()
    up.third()
    layer.turn(layer.normed_one, layer.turned)
    weigh(heads_out, qk, vo)
    qk.start()
    vo.start()
    up.fourth()
    vo.second()
    layer.entry_back()
    qk.second()
    vo.third()
    layer.proj_grad[...] = dot(layer.hidden[...], layer.pos_low[...], TN)
    layer.pos_grad[...] = dot(layer.points[...], layer.pre_grad[...], TN, highest)
    small = layer.small
    for i in range(3):
        lanes = slice(128 * i, 128 * i + 128)
        small[128 * i : 128 * i + 128, :] = layer.proj_grad[:, lanes]
        small[384 + 8 * i : 392 + 8 * i, :] = layer.vec_grad[:, lanes]
        small[416 + 8 * i : 424 + 8 * i, :] = stack_rows([layer.up_bias_grad[j, 0:1, lanes] for j in range(mp)])
    small[408:416, :] = layer.pos_grad[...]
    small[440:512, :] = jnp.zeros((72, 128), f32)
    layer.plane_out[...] = small[...].astype(bf16).reshape(8, 64, 128)
    layer.plane_in[links.plane] = layer.plane_out[links.plane]
    sums = []
    for k in range(1, 8):
        who = links.round(k)
        block = layer.plane_out.at[lax.rem(links.plane + k, 8)]
        sums.append(links.send(block, layer.plane_in.at[links.plane], who))
    qk.third()
    vo.fourth()
    layer.gather_rows(layer.middle_grad, layer.feats_grad)
    for k in range(1, 8):
        links.wait(sums[k - 1], layer.plane_in.at[lax.rem(links.plane + 8 - k, 8)])
    total = layer.plane_in[0].astype(f32)
    for i in range(1, 8):
        total = total + layer.plane_in[i].astype(f32)
    layer.line_out[...] = total.astype(bf16).reshape(4, 16, 128)
    layer.line_in[links.z] = layer.line_out[links.z]
    sums = []
    for k in range(1, 4):
        block = layer.line_out.at[lax.rem(links.z + k, 4)]
        sums.append(links.send(block, layer.line_in.at[links.z], links.far(k)))
    qk.fourth()
    own = layer.own_grad
    own[:, 512 + cols :] = down.end()
    own[:, 512 : 512 + cols] = up.end()
    own[:, 256:512] = vo.end()
    for k in range(1, 4):
        links.wait(sums[k - 1], layer.line_in.at[links.back(k)])
    total = layer.line_in[0].astype(f32)
    for i in range(1, 4):
        total = total + layer.line_in[i].astype(f32)
    layer.whole[links.plane, links.z] = total.astype(bf16)
    sums = []
    for k in range(1, 4):
        block = layer.whole.at[links.plane, links.z]
        sums.append(links.send(block, block, links.far(k)))
    own[:, 0:256] = qk.end()
    lead = (links.z * 2 + links.y == 0).astype(f32)
    weights = {name: load(refs, "weight", name) for name in PIECES}

    def all_sum(slots, planes, rows):
        slots[links.z] = rows
        marks = []
        for k in range(1, 4):
            block = slots.at[links.z]
            marks.append(links.send(block, block, links.far(k)))
        for k in range(1, 4):
            links.wait(marks[k - 1], slots.at[links.back(k)])
        planes[links.plane] = slots[0] + slots[1] + slots[2] + slots[3]
        marks = []
        for k in range(1, 8):
            block = planes.at[links.plane]
            marks.append(links.send(block, block, links.round(k)))
        return marks

    def all_end(planes, marks):
        for k in range(1, 8):
            links.wait(marks[k - 1], planes.at[lax.rem(links.plane + 8 - k, 8)])
        total = planes[0]
        for i in range(1, 8):
            total = total + planes[i]
        return total

    def five(parts):
        out = []
        for name in ("qkv", "out", "up", "bias", "down"):
            row = sum(square_row(p) for p in parts[name])
            out.append(row * lead if name == "bias" else row)
        return out

    rows = stack_rows([square_row(own[...])] + five(weights))
    marks = all_sum(layer.line_a, layer.plane_a, rows)
    for k in range(1, 4):
        links.wait(sums[k - 1], layer.whole.at[links.plane, links.back(k)])
    sums = []
    for k in range(1, 8):
        block = layer.whole.at[links.plane]
        sums.append(links.send(block, block, links.round(k)))
    for k in range(1, 8):
        links.wait(sums[k - 1], layer.whole.at[lax.rem(links.plane + 8 - k, 8)])
    small[...] = layer.whole[...].astype(f32).reshape(512, 128)
    first = all_end(layer.plane_a, marks)
    layer.small_out[...] = small[...]
    total = first[0:1] + square_row(small[0:440, :])
    factor = jnp.minimum(1.0, clip_max / (jnp.sqrt(total) + 1e-06))[0:1, 0:1]
    for copy in late:
        copy.wait()
    grads = own_parts(own, small, links.mp)
    ways = {}
    for name in ("qkv", "out", "up", "bias", "down"):
        ways[name] = [
            adam(g, factor, m, s, p)[3]
            for g, m, s, p in zip(grads[name], load(refs, "moment", name), load(refs, "second", name), weights[name])
        ]
    marks = all_sum(layer.line_b, layer.plane_b, stack_rows(five(ways)))
    second = all_end(layer.plane_b, marks)
    place = lax.broadcasted_iota(jnp.int32, (8, 128), 0)
    layer.sums[0:8, :] = jnp.where(place == 0, jnp.broadcast_to(total, (8, 128)), first)
    layer.sums[8:16, :] = second
    links.finish()


class _Shifted:
    def __init__(self, ref, start):
        self.ref, self.start = ref, start

    def __getitem__(self, i):
        return self.ref[self.start + i]


SHAPES = ("weight", "moment", "second")


def main_call(mp, inner, counts, feats, cotangent, points, params):
    clouds = counts.shape[0] // mp
    width = feats.shape[1]
    hid = params["proj_weight"].shape[0]
    cols = inner // mp
    smem, vmem = pl.BlockSpec(memory_space=pltpu.SMEM), pl.BlockSpec(memory_space=pltpu.VMEM)
    anywhere = pl.BlockSpec(memory_space=pl.ANY)
    inputs = {"counts_all": (counts, smem), "feats_all": (feats, anywhere), "top_all": (cotangent, anywhere)}
    inputs["points"] = (points, vmem)
    scratch = layer_scratch(mp, clouds, width, inner, hid)
    for name in PIECES:
        inputs[name + "_weight"] = (params[name + "_weight"], vmem)
        for kind in SHAPES[1:]:
            array = params[name + "_" + kind]
            inputs[name + "_" + kind + "_all"] = (array, anywhere)
            scratch[name + "_" + kind] = (array.shape, f32)
    outs = dict(
        block_out=((clouds * PAD, width), bf16),
        feats_grad=((clouds * PAD, width), f32),
        own_grad=((48, 512 + 2 * cols), f32),
        small_out=((512, 128), f32),
        sums=((16, 128), f32),
    )
    scratch.update(
        feats=((clouds * PAD, width), bf16),
        cotangent=((clouds * PAD, width), bf16),
        proj_low=((hid, width), bf16),
        pos_hidden=((8, hid), f32),
        w=((mp, 4, 2, 48, 512 + 2 * cols), bf16),
        up_bias=((mp, 8, cols), f32),
        up_bias_grad=((mp, 8, cols), f32),
        vec_grad=((8, width), f32),
        pos_grad=((8, hid), f32),
        proj_grad=((hid, width), f32),
        small=((512, 128), f32),
        plane_out=((8, 64, 128), bf16),
        plane_in=((8, 64, 128), bf16),
        line_out=((4, 16, 128), bf16),
        line_in=((4, 16, 128), bf16),
        whole=((8, 4, 16, 128), bf16),
        line_a=((4, 8, 128), f32),
        plane_a=((8, 8, 128), f32),
        line_b=((4, 8, 128), f32),
        plane_b=((8, 8, 128), f32),
    )
    for tag, n in (("down__", cols), ("up__", cols), ("qk__", 256), ("vo__", 256)):
        scratch.update(scatter_scratch(tag, n))
    sems = dict(send_sem=192, recv_sem=192, load_sem=18)
    names = list(inputs) + list(outs) + list(scratch) + list(sems)
    return pl.pallas_call(
        functools.partial(main_kernel, names, mp, clouds, width, inner),
        out_shape=[jax.ShapeDtypeStruct(*v) for v in outs.values()],
        in_specs=[v[1] for v in inputs.values()],
        out_specs=[vmem] * len(outs),
        scratch_shapes=[pltpu.VMEM(*v) for v in scratch.values()]
        + [pltpu.SemaphoreType.DMA((n,)) for n in sems.values()],
        compiler_params=pltpu.CompilerParams(
            vmem_limit_bytes=60 * 1024 * 1024, collective_id=0, has_side_effects=True
        ),
    )(*[v[0] for v in inputs.values()])


def update_kernel(names, *args):
    refs = dict(zip(names, args))
    copies = [
        pltpu.make_async_copy(refs["block_in"], refs["block_out"], refs["sem"].at[0]),
        pltpu.make_async_copy(refs["feats_in"], refs["feats_out"], refs["sem"].at[1]),
    ]
    for copy in copies:
        copy.start()
    mp = lax.axis_index("mp")
    sums = refs["sums"][...]
    clip = jnp.sqrt(sums[0:1])
    factor = jnp.minimum(1.0, clip_max / (clip + 1e-06))[0:1, 0:1]
    refs["clip_out"][...] = clip
    grads = own_parts(refs["own"], refs["small"], mp)
    order, squares, steps = 0, [], []
    for name in PIECES:
        weights = load(refs, "weight", name)
        parts = [
            adam(g, factor, m, s, p)
            for g, m, s, p in zip(grads[name], load(refs, "moment", name), load(refs, "second", name), weights)
        ]
        if order < 5:
            pair = [(sums[1 + order : 2 + order, 0:1], sums[8 + order : 9 + order, 0:1])]
        else:
            kept = 1 if name == "vector" else None
            pair = []
            for a in (weights[0], parts[0][3]):
                total = jnp.sum(a * a, axis=1, keepdims=True)
                pair.append(total if kept else jnp.sum(total, axis=0, keepdims=True))
            pair = [tuple(pair)]
        order += 1
        old, way = jnp.sqrt(pair[0][0]), jnp.sqrt(pair[0][1])
        squares.append((old, way))
        ratio = old / (way + 1e-06)
        for i, (weight, part) in enumerate(zip(weights, parts)):
            new = weight - learn_rate * ratio * part[3]
            stored = {"grad": part[0], "new": new, "m": part[1], "s": part[2], "copy": new.astype(bf16)}
            for kind, value in stored.items():
                ref = refs[name + "_out_" + kind]
                if name == "qkv":
                    ref[i] = value
                else:
                    ref[...] = value.reshape(ref.shape)
    place = lax.broadcasted_iota(jnp.int32, (8, 128), 0)
    lane = lax.broadcasted_iota(jnp.int32, (8, 128), 1)
    trust = jnp.zeros((8, 128), f32)
    for side in range(2):
        column = 0
        for pair in squares:
            for r in range(pair[side].shape[0]):
                value = jnp.broadcast_to(pair[side][r : r + 1, :], (8, 128))
                trust = jnp.where((place == side) & (lane == column), value, trust)
                column += 1
    refs["trust_out"][...] = trust[0:2, 0:14]
    for copy in copies:
        copy.wait()


OUT_KINDS = (("grad", f32), ("new", f32), ("m", f32), ("s", f32), ("copy", bf16))


def update_call(block, feats, own, small, sums, params):
    vmem = pl.BlockSpec(memory_space=pltpu.VMEM)
    anywhere = pl.BlockSpec(memory_space=pl.ANY)
    inputs = {"block_in": (block, vmem), "feats_in": (feats, vmem)}
    inputs.update(own=(own, vmem), small=(small, vmem), sums=(sums, vmem))
    for name in PIECES:
        for kind in SHAPES:
            inputs[name + "_" + kind] = (params[name + "_" + kind], vmem)
    outs = {"block_out": (block.shape, bf16, anywhere), "feats_out": (feats.shape, f32, anywhere)}
    outs["clip_out"] = ((1, 128), f32, vmem)
    outs["trust_out"] = ((2, 14), f32, vmem)
    for name in PIECES:
        for kind, dtype in OUT_KINDS:
            outs[name + "_out_" + kind] = (params[name + "_weight"].shape, dtype, vmem)
    names = list(inputs) + list(outs) + ["sem"]
    result = pl.pallas_call(
        functools.partial(update_kernel, names),
        out_shape=[jax.ShapeDtypeStruct(*v[:2]) for v in outs.values()],
        in_specs=[v[1] for v in inputs.values()],
        out_specs=[v[2] for v in outs.values()],
        scratch_shapes=[pltpu.SemaphoreType.DMA((2,))],
        compiler_params=pltpu.CompilerParams(vmem_limit_bytes=60 * 1024 * 1024),
    )(*[v[0] for v in inputs.values()])
    return dict(zip(outs, result))


def close_shards(*arrays):
    feats, centres, counts, cotangent = arrays[:4]
    mp_count = lax.axis_size("mp")
    mp_index = lax.axis_index("mp")
    share = feats.shape[0] // mp_count
    clouds = share // PAD
    inner = arrays[6].shape[1] * mp_count
    params = {}
    for k, kind in enumerate(SHAPES):
        for i, name in enumerate(PIECES):
            array = arrays[4 + 8 * k + i]
            if name in ("out", "down"):
                array = array.T
            params[name + "_" + kind] = array
    mine = lax.dynamic_slice_in_dim(centres, mp_index * share, share, 1).T.reshape(clouds, PAD, 3)
    points = jnp.pad(mine, ((0, 0), (0, SLOT - PAD), (0, 0)))
    points = jnp.concatenate((points, jnp.ones((clouds, SLOT, 1), f32)), axis=2)
    points = jnp.pad(points.reshape(clouds * SLOT, 4), ((0, 0), (0, 4)))
    block, grad, own, small, sums = main_call(mp_count, inner, counts, feats, cotangent, points, params)
    out = update_call(block, grad, own, small, sums, params)
    outputs = [out["block_out"], out["feats_out"], out["clip_out"][0, 0], out["trust_out"]]
    for name in PIECES:
        for kind, _ in OUT_KINDS:
            array = out[name + "_out_" + kind]
            if name in ("out", "down"):
                array = array.T
            outputs.append(array)
    return tuple(outputs)


def solution(mesh):
    qkv, outw, upw, bias, whole = P(None, "dp", "mp"), P("mp", "dp"), P("dp", "mp"), P("mp"), P()
    params = (qkv, outw, upw, bias, outw, whole, whole, whole)
    in_specs = (P("dp", None), P(None, "dp"), P("dp"), P("dp", None)) + params * 3
    rows = P(("dp", "mp"), None)
    out_specs = (rows, rows, P(), P()) + tuple(spec for spec in params for _ in range(5))
    form = close_shards if (mesh.shape["dp"], mesh.shape["mp"]) == (8, 4) else shards
    return jax.shard_map(form, mesh=mesh, in_specs=in_specs, out_specs=out_specs, check_vma=False)
```

```python
import functools
import math

import jax
import jax.numpy as jnp
from jax import lax
from jax.experimental import pallas as pl
from jax.experimental.pallas import tpu as pltpu
from jax.sharding import PartitionSpec as P

HD = 64
PAD = 38
SLOT = 40
GROUP = 4

norm_eps = 1e-05
beta_one = 0.5
beta_two = 0.5
adam_eps = 1e-06
decay_rate = 0.01
learn_rate = 0.3
clip_max = 1.0
step_count = 3.0
neg_fill = -1e30
highest = lax.Precision.HIGHEST
f32 = jnp.float32
bf16 = jnp.bfloat16

NN = (((1,), (0,)), ((), ()))
NT = (((1,), (1,)), ((), ()))
TN = (((0,), (0,)), ((), ()))


def dot(a, b, dims=NN, precision=None):
    return lax.dot_general(a, b, dims, precision=precision, preferred_element_type=f32)


def gelu_pair(v):
    cdf = 0.5 * (1.0 + lax.erf(v * 0.7071067811865476))
    return v * cdf, cdf + v * jnp.exp(-0.5 * v * v) * 0.3989422804014327


def piece_squares(array, tensor_index):
    if tensor_index == 5:
        return jnp.sum(array * array, axis=1)
    return jnp.sum(array * array)[None]


def piece_ratio(trust_ratio, tensor_index):
    if tensor_index < 5:
        return trust_ratio[tensor_index]
    if tensor_index == 5:
        return trust_ratio[5:12][:, None]
    return trust_ratio[tensor_index + 6]


class Layer:
    def __init__(self, refs, mp, clouds, width, inner):
        self.__dict__.update(refs)
        self.mp = mp
        self.clouds = clouds
        self.width = width
        self.inner = inner
        self.rows = clouds * SLOT
        self.block = GROUP * SLOT
        self.blocks = clouds // GROUP
        self.hid = self.proj_low.shape[0]

    def live(self, j):
        return [h for h in range(2) if (2 * j + h) % 2 == 0 or j < self.mp // 2]

    def spread_rows(self):
        zeros = jnp.zeros((SLOT - PAD, self.width), f32)
        self.stage[...] = self.feats[...].astype(f32)
        for c in range(self.clouds):
            self.stream[pl.ds(SLOT * c, PAD), :] = self.stage[pl.ds(PAD * c, PAD), :]
            self.stream[pl.ds(SLOT * c + PAD, SLOT - PAD), :] = zeros
        self.stage[...] = self.cotangent[...].astype(f32)
        for c in range(self.clouds):
            self.middle_grad[pl.ds(SLOT * c, PAD), :] = self.stage[pl.ds(PAD * c, PAD), :]
            self.middle_grad[pl.ds(SLOT * c + PAD, SLOT - PAD), :] = zeros

    def keep_block(self, b, shape, dim):
        place = lax.broadcasted_iota(jnp.int32, shape, dim)
        bound = jnp.zeros(shape, jnp.int32)
        for i in range(GROUP):
            limit = self.counts[b * GROUP + i] + SLOT * i
            inside = (place >= SLOT * i) & (place < limit)
            bound = jnp.where(inside, 1, bound)
        return bound > 0

    def masks(self):
        n = self.block

        def step(b, carry):
            keys = lax.broadcasted_iota(jnp.int32, (n, n), 0)
            query = lax.broadcasted_iota(jnp.int32, (n, n), 1)
            fill = jnp.full((n, n), neg_fill, f32)
            for i in range(GROUP):
                limit = self.counts[b * GROUP + i] + SLOT * i
                inside = (keys >= SLOT * i) & (keys < limit)
                mine = (query >= SLOT * i) & (query < SLOT * (i + 1))
                fill = jnp.where(inside & mine, 0.0, fill)
            self.mask[b] = fill
            self.keep[pl.ds(b * n, n), :] = jnp.where(self.keep_block(b, (n, 128), 0), 1.0, 0.0)
            return carry

        lax.fori_loop(0, self.blocks, step, 0)

    def norm(self, x):
        centre = x - jnp.mean(x, axis=-1, keepdims=True)
        spread = jnp.mean(centre * centre, axis=-1, keepdims=True)
        rate = lax.rsqrt(spread + norm_eps)
        return centre * rate, rate

    def norm_back(self, grad, hat, rate, gain):
        scaled = grad * gain
        first = jnp.mean(scaled, axis=-1, keepdims=True)
        second = jnp.mean(scaled * hat, axis=-1, keepdims=True)
        return rate * (scaled - first - hat * second)

    def entry(self):
        value, slope = gelu_pair(dot(self.points[...], self.pos_hidden[...], NN, highest))
        hidden = value.astype(bf16)
        self.pos_slope[...] = slope
        self.hidden[...] = hidden
        x = self.stream[...] + (dot(hidden, self.proj_low[...]) + self.vec[6:7, :])
        hat, rate = self.norm(x)
        self.stream[...] = x
        self.hat_one[...] = hat
        self.rate_one[...] = jnp.broadcast_to(rate, (self.rows, 128))
        self.normed_one[...] = (hat * self.vec[0:1, :] + self.vec[2:3, :]).astype(bf16)

    def project(self):
        for j in range(self.mp):
            self.qkv[j] = dot(self.normed_one[...], self.w_qkv(j)).astype(bf16)

    def lanes(self, h, n):
        lane = lax.broadcasted_iota(jnp.int32, (n, 128), 1)
        return (lane < HD) if h == 0 else (lane >= HD)

    def heads(self, rows):
        for j in range(self.mp):
            query = self.qkv[j, rows, 0:128] * jnp.asarray(1.0 / math.sqrt(HD), bf16)
            for h in self.live(j):
                own = self.lanes(h, self.block)
                alone = jnp.where(own, query, jnp.zeros_like(query))
                yield j, own, alone, self.qkv[j, rows, 128:256], self.qkv[j, rows, 256:384]

    def attend(self, start, stop):
        n = self.block

        def step(b, carry):
            rows = pl.ds(pl.multiple_of(b * n, n), n)
            mask = self.mask[b]
            live = list(self.heads(rows))
            scores = [dot(keys, query, NT) + mask for _, _, query, keys, _ in live]
            low = []
            for i, score in enumerate(scores):
                expo = jnp.exp(score - jnp.max(score, axis=0, keepdims=True))
                probs = expo * (1.0 / jnp.sum(expo, axis=0, keepdims=True))
                self.probs[i, b] = probs
                low.append(probs.astype(bf16))
            mixed = [jnp.zeros((n, 128), f32)] * self.mp
            for probs, (j, own, _, _, values) in zip(low, live):
                mixed[j] = jnp.where(own, dot(probs, values, TN), mixed[j])
            for j in range(self.mp):
                self.attn_low[j, rows, :] = mixed[j].astype(bf16)
            return carry

        lax.fori_loop(start, stop, step, 0, unroll=2)

    def middle(self):
        x = self.stream[...] + self.vec[4:5, :]
        for j in range(self.mp):
            x = x + dot(self.attn_low[j], self.w_out(j), NT)
        hat, rate = self.norm(x)
        self.stream[...] = x
        self.hat_two[...] = hat
        self.rate_two[...] = jnp.broadcast_to(rate, (self.rows, 128))
        self.normed_two[...] = (hat * self.vec[1:2, :] + self.vec[3:4, :]).astype(bf16)

    def feed(self):
        total = self.stream[...]
        for j in range(self.mp):
            pre = dot(self.normed_two[...], self.w_up(j)) + self.up_bias[j, 0:1, :]
            value, slope = gelu_pair(pre)
            low = value.astype(bf16)
            self.activated[j] = low
            self.slope[j] = slope
            total = total + dot(low, self.w_down(j), NT)
        self.stream[...] = total

    def top(self):
        keep = jnp.concatenate([self.keep[...]] * (self.width // 128), axis=1)
        self.stream[...] = (self.stream[...] + self.vec[5:6, :]) * keep

    def grad_start(self):
        self.vec_grad[...] = jnp.zeros_like(self.vec_grad)
        keep = jnp.concatenate([self.keep[...]] * (self.width // 128), axis=1)
        grad = self.middle_grad[...] * keep
        self.middle_grad[...] = grad
        self.grad_top[...] = grad.astype(bf16)
        self.vec_grad[5:6, :] = jnp.sum(grad, axis=0, keepdims=True)

    def feed_back(self):
        total = None
        for j in range(self.mp):
            grad = dot(self.grad_top[...], self.w_down(j)) * self.slope[j]
            low = grad.astype(bf16)
            self.grad_pre[j] = low
            self.up_bias_grad[j, 0:1, :] = jnp.sum(low.astype(f32), axis=0, keepdims=True)
            term = dot(low, self.w_up(j), NT)
            total = term if j == 0 else total + term
        self.normed_grad[...] = total

    def middle_back(self):
        grad, hat = self.normed_grad[...], self.hat_two[...]
        rate = jnp.concatenate([self.rate_two[...]] * (self.width // 128), axis=1)
        self.vec_grad[1:2, :] = jnp.sum(grad * hat, axis=0, keepdims=True)
        self.vec_grad[3:4, :] = jnp.sum(grad, axis=0, keepdims=True)
        out = self.middle_grad[...] + self.norm_back(grad, hat, rate, self.vec[1:2, :])
        self.middle_grad[...] = out
        self.vec_grad[4:5, :] = jnp.sum(out, axis=0, keepdims=True)
        low = out.astype(bf16)
        self.middle_low[...] = low
        for j in range(self.mp):
            self.attn_grad[j] = dot(low, self.w_out(j)).astype(bf16)

    def attend_back(self):
        n = self.block
        scale = 1.0 / math.sqrt(HD)

        def step(b, carry):
            rows = pl.ds(pl.multiple_of(b * n, n), n)
            live = list(self.heads(rows))
            mine = []
            for j, own, _, _, _ in live:
                grad = self.attn_grad[j, rows, :]
                mine.append(jnp.where(own, grad, jnp.zeros_like(grad)))
            grad_probs = [dot(values, g, NT) for g, (_, _, _, _, values) in zip(mine, live)]
            scores = []
            grad_values = [jnp.zeros((n, 128), f32)] * self.mp
            for i, (j, _, _, _, _) in enumerate(live):
                probs = self.probs[i, b]
                grad_values[j] = grad_values[j] + dot(probs.astype(bf16), mine[i])
                inner = jnp.sum(probs * grad_probs[i], axis=0, keepdims=True)
                scores.append((probs * (grad_probs[i] - inner)).astype(bf16))
            grad_query = [jnp.zeros((n, 128), f32)] * self.mp
            grad_keys = [jnp.zeros((n, 128), f32)] * self.mp
            for grad, (j, own, query, keys, _) in zip(scores, live):
                grad_keys[j] = grad_keys[j] + dot(grad, query)
                grad_query[j] = jnp.where(own, dot(grad, keys, TN), grad_query[j])
            for j in range(self.mp):
                self.grad_proj[j, rows, 0:128] = (grad_query[j] * scale).astype(bf16)
                self.grad_proj[j, rows, 128:256] = grad_keys[j].astype(bf16)
                self.grad_proj[j, rows, 256:384] = grad_values[j].astype(bf16)
            return carry

        lax.fori_loop(0, self.blocks, step, 0, unroll=2)

    def entry_back(self):
        grad = None
        for j in range(self.mp):
            term = dot(self.grad_proj[j], self.w_qkv(j), NT)
            grad = term if j == 0 else grad + term
        hat = self.hat_one[...]
        rate = jnp.concatenate([self.rate_one[...]] * (self.width // 128), axis=1)
        self.vec_grad[0:1, :] = jnp.sum(grad * hat, axis=0, keepdims=True)
        self.vec_grad[2:3, :] = jnp.sum(grad, axis=0, keepdims=True)
        out = self.middle_grad[...] + self.norm_back(grad, hat, rate, self.vec[0:1, :])
        self.middle_grad[...] = out
        self.vec_grad[6:7, :] = jnp.sum(out, axis=0, keepdims=True)
        low = out.astype(bf16)
        self.pos_low[...] = low
        self.pre_grad[...] = dot(low, self.proj_low[...], NT) * self.pos_slope[...]

    def turn(self, source, target):
        for i in range(self.rows // 128):
            target[:, 128 * i : 128 * i + 128] = source[128 * i : 128 * i + 128, :].T

    def gather_rows(self, source, target):
        for c in range(self.clouds):
            target[pl.ds(PAD * c, PAD), :] = source[pl.ds(SLOT * c, PAD), :]


def layer_scratch(mp, clouds, width, inner, hid):
    rows = clouds * SLOT
    block = GROUP * SLOT
    cols = inner // mp
    heads = mp + mp // 2
    shapes = dict(
        stage=((clouds * PAD, width), f32),
        stream=((rows, width), f32),
        middle_grad=((rows, width), f32),
        mask=((clouds // GROUP, block, block), f32),
        keep=((rows, 128), f32),
        pos_slope=((rows, hid), f32),
        hidden=((rows, hid), bf16),
        hat_one=((rows, width), f32),
        rate_one=((rows, 128), f32),
        normed_one=((rows, width), bf16),
        qkv=((mp, rows, 384), bf16),
        probs=((heads, clouds // GROUP, block, block), f32),
        attn_low=((mp, rows, 128), bf16),
        hat_two=((rows, width), f32),
        rate_two=((rows, 128), f32),
        normed_two=((rows, width), bf16),
        activated=((mp, rows, cols), bf16),
        slope=((mp, rows, cols), f32),
        grad_top=((rows, width), bf16),
        grad_pre=((mp, rows, cols), bf16),
        normed_grad=((rows, width), f32),
        middle_low=((rows, width), bf16),
        attn_grad=((mp, rows, 128), bf16),
        grad_proj=((mp, rows, 384), bf16),
        pos_low=((rows, width), bf16),
        pre_grad=((rows, hid), f32),
        turned=((width, rows), bf16),
    )
    return shapes


def compute_kernel(names, mp, clouds, width, inner, *args):
    refs = dict(zip(names, args))
    layer = Layer(refs, mp, clouds, width, inner)
    w = layer.w
    cols = inner // mp
    layer.w_qkv = lambda j: w[j, :, 0:384]
    layer.w_out = lambda j: w[j, :, 384:512]
    layer.w_up = lambda j: w[j, :, 512 : 512 + cols]
    layer.w_down = lambda j: w[j, :, 512 + cols : 512 + 2 * cols]
    layer.proj_low[...] = layer.pos_proj[...].astype(bf16)
    layer.spread_rows()
    layer.masks()
    layer.entry()
    layer.project()
    layer.attend(0, layer.blocks)
    layer.middle()
    layer.feed()
    layer.top()
    layer.gather_rows(layer.stream, layer.stage)
    layer.block_out[...] = layer.stage[...].astype(bf16)
    layer.grad_start()
    layer.feed_back()
    g = layer.grads
    layer.turn(layer.grad_top, layer.turned)
    for j in range(mp):
        g[j, :, 512 + cols : 512 + 2 * cols] = dot(layer.turned[...], layer.activated[j])
    layer.turn(layer.normed_two, layer.turned)
    for j in range(mp):
        g[j, :, 512 : 512 + cols] = dot(layer.turned[...], layer.grad_pre[j])
    layer.middle_back()
    layer.turn(layer.middle_low, layer.turned)
    for j in range(mp):
        g[j, :, 384:512] = dot(layer.turned[...], layer.attn_low[j])
    layer.attend_back()
    layer.turn(layer.normed_one, layer.turned)
    for j in range(mp):
        g[j, :, 0:384] = dot(layer.turned[...], layer.grad_proj[j])
    layer.entry_back()
    layer.gather_rows(layer.middle_grad, layer.feats_grad)
    layer.proj_grad[...] = dot(layer.hidden[...], layer.pos_low[...], TN)
    layer.pos_grad[...] = dot(layer.points[...], layer.pre_grad[...], TN, highest)


def compute(mp, width, inner, counts, feats, cotangent, points, w, up_bias, vec, pos_hidden, pos_proj):
    clouds = counts.shape[0]
    hid = pos_proj.shape[0]
    inputs = ["counts", "feats", "cotangent", "points", "w", "up_bias", "vec", "pos_hidden", "pos_proj"]
    outs = dict(
        block_out=((clouds * PAD, width), bf16),
        feats_grad=((clouds * PAD, width), f32),
        grads=(w.shape, f32),
        up_bias_grad=((mp, 8, inner // mp), f32),
        vec_grad=((8, width), f32),
        pos_grad=((8, hid), f32),
        proj_grad=((hid, width), f32),
    )
    scratch = layer_scratch(mp, clouds, width, inner, hid)
    scratch["proj_low"] = ((hid, width), bf16)
    names = inputs + list(outs) + list(scratch)
    vmem = pl.BlockSpec(memory_space=pltpu.VMEM)
    return pl.pallas_call(
        functools.partial(compute_kernel, names, mp, clouds, width, inner),
        out_shape=[jax.ShapeDtypeStruct(*v) for v in outs.values()],
        in_specs=[pl.BlockSpec(memory_space=pltpu.SMEM)] + [vmem] * (len(inputs) - 1),
        out_specs=[vmem] * len(outs),
        scratch_shapes=[pltpu.VMEM(*v) for v in scratch.values()],
        compiler_params=pltpu.CompilerParams(vmem_limit_bytes=60 * 1024 * 1024),
    )(counts, feats, cotangent, points, w, up_bias, vec, pos_hidden, pos_proj)


def shards(
    feats,
    centres,
    counts,
    cotangent,
    qkv_weight,
    out_weight,
    up_weight,
    up_bias,
    down_weight,
    norm_vectors,
    pos_hidden,
    pos_proj,
    qkv_moment,
    out_moment,
    up_moment,
    bias_moment,
    down_moment,
    vector_moment,
    hidden_moment,
    proj_moment,
    qkv_second,
    out_second,
    up_second,
    bias_second,
    down_second,
    vector_second,
    hidden_second,
    proj_second,
):
    mp_count = lax.axis_size("mp")
    mp_index = lax.axis_index("mp")
    dp_index = lax.axis_index("dp")
    share = feats.shape[0] // mp_count
    clouds = share // PAD
    width = feats.shape[1]
    cols = up_weight.shape[1]
    inner = cols * mp_count
    start = mp_index * share
    my_feats = lax.dynamic_slice_in_dim(feats, start, share, 0)
    my_top = lax.dynamic_slice_in_dim(cotangent, start, share, 0)
    my_counts = lax.dynamic_slice_in_dim(counts, mp_index * clouds, clouds, 0)
    my_points = lax.dynamic_slice_in_dim(centres, start, share, 1).T.reshape(clouds, PAD, 3)
    points = jnp.pad(my_points, ((0, 0), (0, SLOT - PAD), (0, 0)))
    points = jnp.concatenate((points, jnp.ones((clouds, SLOT, 1), f32)), axis=2)
    points = jnp.pad(points.reshape(clouds * SLOT, 4), ((0, 0), (0, 4)))
    packed = jnp.concatenate(
        (qkv_weight[0], qkv_weight[1], qkv_weight[2], out_weight.T, up_weight, down_weight.T), axis=1
    ).astype(bf16)
    whole = lax.all_gather(packed, "dp", axis=0, tiled=True)
    whole = lax.all_gather(whole, "mp", axis=0)
    bias = lax.all_gather(jnp.broadcast_to(up_bias[None], (8, cols)), "mp", axis=0)
    vec = jnp.pad(norm_vectors, ((0, 1), (0, 0)))
    hidden = jnp.pad(pos_hidden, ((0, 4), (0, 0)))
    block_out, feats_grad, grads, bias_grad, vec_grad, pos_grad, proj_grad = compute(
        mp_count, width, inner, my_counts, my_feats, my_top, points, whole, bias, vec, hidden, pos_proj
    )
    own = lax.psum_scatter(grads, "mp", scatter_dimension=0, tiled=True)[0]
    own = lax.psum_scatter(own, "dp", scatter_dimension=0, tiled=True)
    bias_grad, vector_grad, pos_grad, proj_grad = lax.psum(
        (bias_grad[:, 0], vec_grad[:7], pos_grad[:4], proj_grad), ("dp", "mp")
    )
    bias_grad = lax.dynamic_index_in_dim(bias_grad, mp_index, 0, keepdims=False)
    qkv_grad = jnp.stack((own[:, 0:128], own[:, 128:256], own[:, 256:384]))
    out_grad = own[:, 384:512].T
    up_grad = own[:, 512 : 512 + cols]
    down_grad = own[:, 512 + cols :].T
    leader = ((dp_index == 0) & (mp_index == 0)).astype(f32)
    first_dp = (dp_index == 0).astype(f32)
    owners = [1.0, 1.0, 1.0, first_dp, 1.0, leader, leader, leader]
    weights = [qkv_weight, out_weight, up_weight, up_bias, down_weight, norm_vectors, pos_hidden, pos_proj]
    moments = [
        qkv_moment,
        out_moment,
        up_moment,
        bias_moment,
        down_moment,
        vector_moment,
        hidden_moment,
        proj_moment,
    ]
    seconds = [
        qkv_second,
        out_second,
        up_second,
        bias_second,
        down_second,
        vector_second,
        hidden_second,
        proj_second,
    ]
    grads = [qkv_grad, out_grad, up_grad, bias_grad, down_grad, vector_grad, pos_grad, proj_grad]
    grad_square = jnp.zeros((), f32)
    weight_square = []
    for i in range(8):
        grad_square = grad_square + owners[i] * jnp.sum(grads[i] * grads[i])
        weight_square.append(owners[i] * piece_squares(weights[i], i))
    totals = lax.psum(jnp.concatenate([grad_square[None]] + weight_square), ("dp", "mp"))
    clip_norm = jnp.sqrt(totals[0])
    factor = jnp.minimum(1.0, clip_max / (clip_norm + 1e-06))
    clipped_list, moment_list, second_list, direction_list, update_square = [], [], [], [], []
    for i in range(8):
        clipped = grads[i] * factor
        moment_new = beta_one * moments[i] + (1.0 - beta_one) * clipped
        second_new = beta_two * seconds[i] + (1.0 - beta_two) * clipped * clipped
        direction = (
            moment_new
            / (1.0 - beta_one**step_count)
            / (jnp.sqrt(second_new / (1.0 - beta_two**step_count)) + adam_eps)
            + decay_rate * weights[i]
        )
        clipped_list.append(clipped)
        moment_list.append(moment_new)
        second_list.append(second_new)
        direction_list.append(direction)
        update_square.append(owners[i] * piece_squares(direction, i))
    update_total = lax.psum(jnp.concatenate(update_square), ("dp", "mp"))
    weight_norm = jnp.sqrt(totals[1:])
    update_norm = jnp.sqrt(update_total)
    trust_ratio = weight_norm / (update_norm + 1e-06)
    outputs = [block_out, feats_grad, clip_norm, jnp.stack((weight_norm, update_norm))]
    for i in range(8):
        new_weight = weights[i] - learn_rate * piece_ratio(trust_ratio, i) * direction_list[i]
        outputs.append(clipped_list[i])
        outputs.append(new_weight)
        outputs.append(moment_list[i])
        outputs.append(second_list[i])
        outputs.append(new_weight.astype(bf16))
    return tuple(outputs)


class Links:
    def __init__(self, send, recv):
        dp, mp = lax.axis_index("dp"), lax.axis_index("mp")
        self.z, self.y = dp // 2, lax.rem(dp, 2)
        self.x, self.c = mp // 2, lax.rem(mp, 2)
        self.mp = mp
        self.plane = self.y * 4 + mp
        self.line = [self.z, self.z + 1 - 2 * lax.rem(self.z, 2), lax.rem(self.z + 2, 4), 3 - self.z]
        self.send_sem, self.recv_sem = send, recv
        self.counts = [0, 0]
        self.sent = []

    def at(self, z, y, x, c):
        return (z * 2 + y, x * 2 + c)

    def core(self):
        return self.at(self.z, self.y, self.x, 1 - self.c)

    def side(self):
        return self.at(self.z, self.y, 1 - self.x, self.c)

    def deep(self):
        return self.at(self.z, 1 - self.y, self.x, self.c)

    def far(self, k):
        return self.at(self.line[k], self.y, self.x, self.c)

    def round(self, k):
        other = lax.rem(self.plane + k, 8)
        return (self.z * 2 + other // 4, lax.rem(other, 4))

    def peers(self):
        return [self.far(k) for k in range(1, 4)] + [self.round(k) for k in range(1, 8)]

    def greet(self):
        barrier = pltpu.get_barrier_semaphore()
        for who in self.peers():
            pl.semaphore_signal(barrier, inc=1, device_id=who, device_id_type=pl.DeviceIdType.MESH)

    def met(self):
        pl.semaphore_wait(pltpu.get_barrier_semaphore(), 10)

    def copy(self, source, target, i):
        return pltpu.make_async_remote_copy(
            src_ref=source,
            dst_ref=target,
            send_sem=self.send_sem.at[i] if i < self.send_sem.shape[0] else self.send_sem.at[0],
            recv_sem=self.recv_sem.at[i] if i < self.recv_sem.shape[0] else self.recv_sem.at[0],
            device_id=self.core(),
            device_id_type=pl.DeviceIdType.MESH,
        )

    def mark(self, side):
        self.counts[side] += 1
        return self.counts[side] - 1

    def send(self, source, target, who, out=None, into=None):
        into = self.mark(1) if into is None else into
        copy = pltpu.make_async_remote_copy(
            src_ref=source,
            dst_ref=target,
            send_sem=self.send_sem.at[self.mark(0) if out is None else out],
            recv_sem=self.recv_sem.at[into],
            device_id=who,
            device_id_type=pl.DeviceIdType.MESH,
        )
        copy.start()
        if out is None:
            self.sent.append(copy)
        return into

    def wait(self, i, target):
        self.copy(target, target, i).wait_recv()

    def sent_all(self, out, source):
        self.sent.append(self.copy(source, source, out))

    def finish(self):
        for copy in self.sent:
            copy.wait_send()


class Gather:
    def __init__(self, links, w, lo, hi, flip):
        self.links, self.w, self.lo, self.hi, self.flip = links, w, lo, hi, flip

    def part(self, mp, z, y):
        return self.w.at[mp, z, y, :, self.lo : self.hi]

    def start(self):
        k = self.links
        own = self.part(k.mp, k.z, k.y)
        self.along = [k.send(own, own, k.far(i)) for i in (1, 2, 3)]
        self.out = [k.mark(0) for _ in range(5)]
        self.first = [k.mark(1) for _ in range(4)]
        self.into = [k.mark(1) for _ in range(4)]

    def step(self, i):
        k = self.links
        block = self.part(k.mp, k.line[i], k.y)
        if i:
            k.wait(self.along[i - 1], block)
        near, next_ = (k.side(), k.deep()) if self.flip else (k.deep(), k.side())
        k.send(block, block, near, self.out[0], self.first[i])
        k.send(block, block, k.core(), self.out[1], self.into[0])
        k.send(block, block, next_, self.out[2], self.into[1])

    def regions(self, mp, z):
        k = self.links
        across = mp + 2 - 4 * k.x
        side, deep = self.part(across, z, k.y), self.part(mp, z, 1 - k.y)
        return (side, deep) if self.flip else (deep, side), self.part(across, z, 1 - k.y)

    def hop(self, i):
        k = self.links
        block = self.regions(k.mp, k.line[i])[0][0]
        k.wait(self.first[i], block)
        k.send(block, block, k.deep() if self.flip else k.side(), self.out[3], self.into[2])
        k.send(block, block, k.core(), self.out[4], self.into[3])

    def rest(self):
        k = self.links
        block = self.regions(k.mp, slice(None))[0][1]
        k.wait(self.into[1], block)
        self.rest_twin = k.send(block, block, k.core())

    def corner(self):
        k = self.links
        block = self.regions(k.mp, slice(None))[1]
        k.wait(self.into[2], block)
        self.corner_twin = k.send(block, block, k.core())

    def end(self):
        k = self.links
        twin = k.mp + 1 - 2 * k.c
        near, corner = self.regions(twin, slice(None))
        k.wait(self.into[0], self.part(twin, slice(None), k.y))
        k.wait(self.into[3], near[0])
        k.wait(self.rest_twin, near[1])
        k.wait(self.corner_twin, corner)
        line = self.part(k.mp, slice(None), k.y)
        first = self.regions(k.mp, slice(None))[0][0]
        for out, block in zip(self.out, (line, line, line, first, first)):
            k.sent_all(out, block)


class Scatter:
    def __init__(self, links, refs, flip):
        self.links, self.flip = links, flip
        self.__dict__.update(refs)

    def start(self):
        k = self.links
        self.first = k.send(self.core_out, self.core_in, k.core())

    def pair(self, x, z, y):
        return self.kept[x, z, y] + self.core_in[x, z, y].astype(f32)

    def second(self):
        k = self.links
        k.wait(self.first, self.core_in)
        if self.flip:
            for x in range(2):
                for z in range(4):
                    self.next_out[x, z] = self.pair(x, z, 1 - k.y).astype(bf16)
            self.next = k.send(self.next_out, self.next_in, k.deep())
        else:
            for y in range(2):
                for z in range(4):
                    self.next_out[y, z] = self.pair(1 - k.x, z, y).astype(bf16)
            self.next = k.send(self.next_out, self.next_in, k.side())

    def third(self):
        k = self.links
        k.wait(self.next, self.next_in)
        for z in range(4):
            if self.flip:
                total = self.pair(1 - k.x, z, k.y) + self.next_in[1 - k.x, z].astype(f32)
            else:
                total = self.pair(k.x, z, 1 - k.y) + self.next_in[1 - k.y, z].astype(f32)
            self.last_out[z] = total.astype(bf16)
        self.last = k.send(self.last_out, self.last_in, k.side() if self.flip else k.deep())

    def fourth(self):
        k = self.links
        k.wait(self.last, self.last_in)
        self.along = []
        for i in range(4):
            z = k.line[i]
            mid = self.next_in[k.x, z] if self.flip else self.next_in[k.y, z]
            total = self.pair(k.x, z, k.y) + mid.astype(f32) + self.last_in[z].astype(f32)
            if i == 0:
                self.own[...] = total
            else:
                self.far_out[i - 1] = total.astype(bf16)
                self.along.append(k.send(self.far_out.at[i - 1], self.far_in.at[i - 1], k.far(i)))

    def end(self):
        k = self.links
        total = self.own[...]
        for i in range(3):
            k.wait(self.along[i], self.far_in.at[i])
            total = total + self.far_in[i].astype(f32)
        return total


def scatter_scratch(tag, cols):
    return {
        tag + "kept": ((2, 4, 2, 48, cols), f32),
        tag + "core_out": ((2, 4, 2, 48, cols), bf16),
        tag + "core_in": ((2, 4, 2, 48, cols), bf16),
        tag + "next_out": ((2, 4, 48, cols), bf16),
        tag + "next_in": ((2, 4, 48, cols), bf16),
        tag + "last_out": ((4, 48, cols), bf16),
        tag + "last_in": ((4, 48, cols), bf16),
        tag + "far_out": ((3, 48, cols), bf16),
        tag + "far_in": ((3, 48, cols), bf16),
        tag + "own": ((48, cols), f32),
    }


def stack_rows(rows, height=8):
    place = lax.broadcasted_iota(jnp.int32, (height, 128), 0)
    out = jnp.zeros((height, 128), f32)
    for i, row in enumerate(rows):
        out = jnp.where(place == i, jnp.broadcast_to(row, (height, 128)), out)
    return out


def square_row(array):
    total = jnp.sum(jnp.sum(array * array, axis=0, keepdims=True), axis=1, keepdims=True)
    return jnp.broadcast_to(total, (1, 128))


def adam(grad, factor, moment, second, weight):
    clipped = grad * factor
    moment_new = beta_one * moment + (1.0 - beta_one) * clipped
    second_new = beta_two * second + (1.0 - beta_two) * clipped * clipped
    direction = (
        moment_new
        / (1.0 - beta_one**step_count)
        / (jnp.sqrt(second_new / (1.0 - beta_two**step_count)) + adam_eps)
        + decay_rate * weight
    )
    return clipped, moment_new, second_new, direction


PIECES = ("qkv", "out", "up", "bias", "down", "vector", "hidden", "proj")


def own_parts(own, small, mp):
    cols = (own.shape[1] - 512) // 2

    def wide(row, count):
        return jnp.concatenate([small[row + 8 * i : row + 8 * i + count, :] for i in range(3)], axis=1)

    place = lax.broadcasted_iota(jnp.int32, (8, cols), 0)

    return {
        "qkv": [own[:, 128 * i : 128 * i + 128] for i in range(3)],
        "out": [own[:, 384:512]],
        "up": [own[:, 512 : 512 + cols]],
        "bias": [jnp.sum(jnp.where(place == mp, wide(416, 8), 0.0), axis=0, keepdims=True)],
        "down": [own[:, 512 + cols : 512 + 2 * cols]],
        "vector": [wide(384, 7)],
        "hidden": [small[408:412, :]],
        "proj": [jnp.concatenate([small[128 * i : 128 * i + 128, :] for i in range(3)], axis=1)],
    }


def load(refs, kind, name):
    ref = refs[name + "_" + kind]
    if name == "qkv":
        return [ref[i] for i in range(3)]
    return [ref[...].reshape(1, -1)] if name == "bias" else [ref[...]]


def main_kernel(names, mp, clouds, width, inner, *args):
    refs = dict(zip(names, args))
    layer = Layer(refs, mp, clouds, width, inner)
    cols = inner // mp
    links = Links(layer.send_sem, layer.recv_sem)
    w = layer.w
    links.greet()
    share = clouds * PAD
    rows = pl.ds(pl.multiple_of(links.mp * share, 16), share)
    sources = {"feats": layer.feats_all.at[rows, :], "cotangent": layer.top_all.at[rows, :]}
    for kind in SHAPES:
        for name in PIECES:
            sources[name + "_" + kind] = refs[name + "_" + kind + "_all"]
    sources["points"] = layer.points_all
    copies = {
        name: pltpu.make_async_copy(source, refs[name], layer.load_sem.at[i])
        for i, (name, source) in enumerate(sources.items())
    }
    first = [name + "_weight" for name in ("qkv", "out", "up", "down", "bias")]
    early = ["feats", "points", "hidden_weight", "proj_weight", "vector_weight", "cotangent"]
    late = [copy for name, copy in copies.items() if name not in first + early]
    for name in first + early:
        copies[name].start()

    def flat(j, lo, hi):
        return w[j, :, :, :, lo:hi].reshape(width, hi - lo)

    layer.w_qkv = lambda j: flat(j, 0, 384)
    layer.w_out = lambda j: flat(j, 384, 512)
    layer.w_up = lambda j: flat(j, 512, 512 + cols)
    layer.w_down = lambda j: flat(j, 512 + cols, 512 + 2 * cols)
    for name in first:
        copies[name].wait()
    for i in range(3):
        w[links.mp, links.z, links.y, :, 128 * i : 128 * i + 128] = refs["qkv_weight"][i].astype(bf16)
    w[links.mp, links.z, links.y, :, 384:512] = refs["out_weight"][...].astype(bf16)
    w[links.mp, links.z, links.y, :, 512 : 512 + cols] = refs["up_weight"][...].astype(bf16)
    w[links.mp, links.z, links.y, :, 512 + cols : 512 + 2 * cols] = refs["down_weight"][...].astype(bf16)
    layer.up_bias[links.mp] = jnp.broadcast_to(refs["bias_weight"][...].reshape(1, cols), (8, cols))
    links.met()
    gathers = [
        Gather(links, w, 0, 256, False),
        Gather(links, w, 256, 512, True),
        Gather(links, w, 512, 512 + cols, False),
        Gather(links, w, 512 + cols, 512 + 2 * cols, True),
    ]
    near, wide = gathers[:2], gathers[2:]

    def each(group, step, *a):
        for g in group:
            getattr(g, step)(*a)

    for group in (near, wide):
        each(group, "start")
        each(group, "step", 0)
    own_bias = layer.up_bias.at[links.mp]
    bias_side = links.send(own_bias, own_bias, links.side())
    bias_core = links.send(own_bias, own_bias, links.core())
    for copy in late:
        copy.start()
    for name in early:
        copies[name].wait()
    layer.proj_low[...] = refs["proj_weight"][...].astype(bf16)
    layer.vec = jnp.concatenate([refs["vector_weight"][...], jnp.zeros((1, width), f32)], axis=0)
    layer.pos_hidden[...] = jnp.concatenate([refs["hidden_weight"][...], jnp.zeros((4, 128), f32)], axis=0)
    layer.counts = _Shifted(layer.counts_all, links.mp * clouds)
    layer.spread_rows()
    each(near, "step", 1)
    layer.entry()
    each(near, "step", 2)
    layer.masks()
    each(near, "step", 3)
    each(near, "hop", 0)
    each(near, "hop", 1)
    layer.grad_start()
    each(near, "hop", 2)
    each(wide, "step", 1)
    layer.turn(layer.grad_top, layer.turned_top)
    each(near, "hop", 3)
    each(wide, "step", 2)
    layer.turn(layer.normed_one, layer.turned_one)
    other_bias = layer.up_bias.at[links.mp + 2 - 4 * links.x]
    links.wait(bias_side, other_bias)
    bias_last = links.send(other_bias, other_bias, links.core())
    lead = (links.z * 2 + links.y == 0).astype(f32)

    def five(parts):
        out = []
        for name in ("qkv", "out", "up", "bias", "down"):
            row = sum(square_row(p) for p in parts[name])
            out.append(row * lead if name == "bias" else row)
        return out

    weights = {name: load(refs, "weight", name) for name in PIECES}
    layer.old_rows[...] = stack_rows([jnp.zeros((1, 128), f32)] + five(weights))
    each(near, "rest")
    each(wide, "step", 3)
    each(near, "corner")
    each(wide, "hop", 0)
    each(wide, "hop", 1)
    each(near, "end")
    layer.project()
    each(wide, "hop", 2)
    each(wide, "hop", 3)
    layer.attend(0, layer.blocks // 2)
    each(wide, "rest")
    layer.attend(layer.blocks // 2, layer.blocks)
    each(wide, "corner")
    layer.middle()
    layer.turn(layer.normed_two, layer.turned_two)
    each(wide, "end")
    twin = links.mp + 1 - 2 * links.c
    links.wait(bias_core, layer.up_bias.at[twin])
    links.wait(bias_last, layer.up_bias.at[twin + 2 - 4 * links.x])
    layer.feed()

    def scatter(tag, flip):
        return Scatter(links, {n[len(tag) :]: refs[n] for n in names if n.startswith(tag)}, flip)

    down, up = scatter("down__", True), scatter("up__", False)
    qk, vo = scatter("qk__", False), scatter("vo__", True)

    def weigh(product, *targets):
        for x in range(2):
            pair = [product(2 * x), product(2 * x + 1)]
            kept = jnp.where(links.c == 0, pair[0], pair[1])
            sent = jnp.where(links.c == 0, pair[1], pair[0]).astype(bf16)
            lo = 0
            for target in targets:
                hi = lo + target.kept.shape[-1]
                target.core_out[x] = sent[:, lo:hi].reshape(4, 2, 48, hi - lo)
                target.kept[x] = kept[:, lo:hi].reshape(4, 2, 48, hi - lo)
                lo = hi

    def heads_out(j):
        parts = dot(layer.turned_one[...], layer.grad_proj[j]), dot(layer.turned_mid[...], layer.attn_low[j])
        return jnp.concatenate(parts, axis=1)

    weigh(lambda j: dot(layer.turned_top[...], layer.activated[j]), down)
    down.start()
    layer.feed_back()
    down.second()
    weigh(lambda j: dot(layer.turned_two[...], layer.grad_pre[j]), up)
    up.start()
    layer.middle_back()
    up.second()
    layer.turn(layer.middle_low, layer.turned_mid)
    layer.attend_back()
    down.third()
    weigh(heads_out, qk, vo)
    qk.start()
    vo.start()
    up.third()
    down.fourth()
    qk.second()
    vo.second()
    layer.entry_back()
    layer.proj_grad[...] = dot(layer.hidden[...], layer.pos_low[...], TN)
    layer.pos_grad[...] = dot(layer.points[...], layer.pre_grad[...], TN, highest)
    small = layer.small
    for i in range(3):
        lanes = slice(128 * i, 128 * i + 128)
        small[128 * i : 128 * i + 128, :] = layer.proj_grad[:, lanes]
        small[384 + 8 * i : 392 + 8 * i, :] = layer.vec_grad[:, lanes]
        small[416 + 8 * i : 424 + 8 * i, :] = stack_rows([layer.up_bias_grad[j, 0:1, lanes] for j in range(mp)])
    small[408:416, :] = layer.pos_grad[...]
    small[440:512, :] = jnp.zeros((72, 128), f32)
    layer.plane_out[...] = small[...].astype(bf16).reshape(8, 64, 128)
    layer.plane_in[links.plane] = layer.plane_out[links.plane]
    sums = []
    for k in range(1, 8):
        who = links.round(k)
        block = layer.plane_out.at[lax.rem(links.plane + k, 8)]
        sums.append(links.send(block, layer.plane_in.at[links.plane], who))
    up.fourth()
    layer.gather_rows(layer.middle_grad, layer.stage)
    out_copies = [pltpu.make_async_copy(layer.stage, layer.feats_grad, layer.store_sem.at[0])]
    out_copies[0].start()
    layer.top()
    layer.gather_rows(layer.stream, layer.stage_top)
    layer.block_low[...] = layer.stage_top[...].astype(bf16)
    out_copies.append(pltpu.make_async_copy(layer.block_low, layer.block_out, layer.store_sem.at[1]))
    out_copies[1].start()
    qk.third()
    vo.third()
    for k in range(1, 8):
        links.wait(sums[k - 1], layer.plane_in.at[lax.rem(links.plane + 8 - k, 8)])
    total = layer.plane_in[0].astype(f32)
    for i in range(1, 8):
        total = total + layer.plane_in[i].astype(f32)
    layer.line_out[...] = total.astype(bf16).reshape(4, 16, 128)
    layer.line_in[links.z] = layer.line_out[links.z]
    sums = []
    for k in range(1, 4):
        block = layer.line_out.at[links.line[k]]
        sums.append(links.send(block, layer.line_in.at[links.z], links.far(k)))
    qk.fourth()
    vo.fourth()
    own = layer.own_grad
    own[:, 512 + cols :] = down.end()
    own[:, 512 : 512 + cols] = up.end()
    own[:, 256:512] = vo.end()
    for k in range(1, 4):
        links.wait(sums[k - 1], layer.line_in.at[links.line[k]])
    total = layer.line_in[0].astype(f32)
    for i in range(1, 4):
        total = total + layer.line_in[i].astype(f32)
    layer.whole[links.plane, links.z] = total.astype(bf16)
    sums = []
    for k in range(1, 4):
        block = layer.whole.at[links.plane, links.z]
        sums.append(links.send(block, block, links.far(k)))
    own[:, 0:256] = qk.end()
    def all_sum(slots, planes, rows):
        slots[links.z] = rows
        marks = []
        for k in range(1, 4):
            block = slots.at[links.z]
            marks.append(links.send(block, block, links.far(k)))
        for k in range(1, 4):
            links.wait(marks[k - 1], slots.at[links.line[k]])
        planes[links.plane] = slots[0] + slots[1] + slots[2] + slots[3]
        marks = []
        for k in range(1, 8):
            block = planes.at[links.plane]
            marks.append(links.send(block, block, links.round(k)))
        return marks

    def all_end(planes, marks):
        for k in range(1, 8):
            links.wait(marks[k - 1], planes.at[lax.rem(links.plane + 8 - k, 8)])
        total = planes[0]
        for i in range(1, 8):
            total = total + planes[i]
        return total

    place = lax.broadcasted_iota(jnp.int32, (8, 128), 0)
    square = jnp.broadcast_to(square_row(own[...]), (8, 128))
    marks = all_sum(layer.line_a, layer.plane_a, jnp.where(place == 0, square, layer.old_rows[...]))
    for k in range(1, 4):
        links.wait(sums[k - 1], layer.whole.at[links.plane, links.line[k]])
    sums = []
    for k in range(1, 8):
        block = layer.whole.at[links.plane]
        sums.append(links.send(block, block, links.round(k)))
    for k in range(1, 8):
        links.wait(sums[k - 1], layer.whole.at[lax.rem(links.plane + 8 - k, 8)])
    small[...] = layer.whole[...].astype(f32).reshape(512, 128)
    first = all_end(layer.plane_a, marks)
    layer.small_out[...] = small[...]
    total = first[0:1] + square_row(small[0:440, :])
    factor = jnp.minimum(1.0, clip_max / (jnp.sqrt(total) + 1e-06))[0:1, 0:1]
    for copy in late:
        copy.wait()
    grads = own_parts(own, small, links.mp)
    ways = {}
    for name in ("qkv", "out", "up", "bias", "down"):
        ways[name] = [
            adam(g, factor, m, s, p)[3]
            for g, m, s, p in zip(grads[name], load(refs, "moment", name), load(refs, "second", name), weights[name])
        ]
    marks = all_sum(layer.line_b, layer.plane_b, stack_rows(five(ways)))
    second = all_end(layer.plane_b, marks)
    layer.sums[0:8, :] = jnp.where(place == 0, jnp.broadcast_to(total, (8, 128)), first)
    layer.sums[8:16, :] = second
    for copy in out_copies:
        copy.wait()
    links.finish()
    assert links.counts == [SENDS, ARRIVALS], links.counts


class _Shifted:
    def __init__(self, ref, start):
        self.ref, self.start = ref, start

    def __getitem__(self, i):
        return self.ref[self.start + i]


SHAPES = ("weight", "moment", "second")
SENDS, ARRIVALS = 107, 119


def main_call(mp, inner, counts, feats, cotangent, points, params):
    clouds = counts.shape[0] // mp
    width = feats.shape[1]
    hid = params["proj_weight"].shape[0]
    cols = inner // mp
    rows = clouds * SLOT
    smem, vmem = pl.BlockSpec(memory_space=pltpu.SMEM), pl.BlockSpec(memory_space=pltpu.VMEM)
    anywhere = pl.BlockSpec(memory_space=pl.ANY)
    inputs = {"counts_all": (counts, smem), "feats_all": (feats, anywhere), "top_all": (cotangent, anywhere)}
    inputs["points_all"] = (points, anywhere)
    scratch = layer_scratch(mp, clouds, width, inner, hid)
    scratch["points"] = (points.shape, f32)
    for name in PIECES:
        for kind in SHAPES:
            array = params[name + "_" + kind]
            inputs[name + "_" + kind + "_all"] = (array, anywhere)
            scratch[name + "_" + kind] = (array.shape, f32)
    outs = dict(
        block_out=((clouds * PAD, width), bf16),
        feats_grad=((clouds * PAD, width), f32),
        own_grad=((48, 512 + 2 * cols), f32),
        small_out=((512, 128), f32),
        sums=((16, 128), f32),
    )
    scratch.update(
        stage_top=((clouds * PAD, width), f32),
        block_low=((clouds * PAD, width), bf16),
        old_rows=((8, 128), f32),
        turned_top=((width, rows), bf16),
        turned_one=((width, rows), bf16),
        turned_two=((width, rows), bf16),
        turned_mid=((width, rows), bf16),
        feats=((clouds * PAD, width), bf16),
        cotangent=((clouds * PAD, width), bf16),
        proj_low=((hid, width), bf16),
        pos_hidden=((8, hid), f32),
        w=((mp, 4, 2, 48, 512 + 2 * cols), bf16),
        up_bias=((mp, 8, cols), f32),
        up_bias_grad=((mp, 8, cols), f32),
        vec_grad=((8, width), f32),
        pos_grad=((8, hid), f32),
        proj_grad=((hid, width), f32),
        small=((512, 128), f32),
        plane_out=((8, 64, 128), bf16),
        plane_in=((8, 64, 128), bf16),
        line_out=((4, 16, 128), bf16),
        line_in=((4, 16, 128), bf16),
        whole=((8, 4, 16, 128), bf16),
        line_a=((4, 8, 128), f32),
        plane_a=((8, 8, 128), f32),
        line_b=((4, 8, 128), f32),
        plane_b=((8, 8, 128), f32),
    )
    for tag, n in (("down__", cols), ("up__", cols), ("qk__", 256), ("vo__", 256)):
        scratch.update(scatter_scratch(tag, n))
    sems = dict(send_sem=SENDS, recv_sem=ARRIVALS, load_sem=27, store_sem=2)
    names = list(inputs) + list(outs) + list(scratch) + list(sems)
    return pl.pallas_call(
        functools.partial(main_kernel, names, mp, clouds, width, inner),
        out_shape=[jax.ShapeDtypeStruct(*v) for v in outs.values()],
        in_specs=[v[1] for v in inputs.values()],
        out_specs=[anywhere, anywhere, vmem, vmem, vmem],
        scratch_shapes=[pltpu.VMEM(*v) for v in scratch.values()]
        + [pltpu.SemaphoreType.DMA((n,)) for n in sems.values()],
        compiler_params=pltpu.CompilerParams(
            vmem_limit_bytes=60 * 1024 * 1024, collective_id=0, has_side_effects=True
        ),
    )(*[v[0] for v in inputs.values()])


def update_kernel(names, *args):
    refs = dict(zip(names, args))
    copies = [
        pltpu.make_async_copy(refs["block_in"], refs["block_out"], refs["sem"].at[0]),
        pltpu.make_async_copy(refs["feats_in"], refs["feats_out"], refs["sem"].at[1]),
    ]
    for copy in copies:
        copy.start()
    mp = lax.axis_index("mp")
    sums = refs["sums"][...]
    clip = jnp.sqrt(sums[0:1])
    factor = jnp.minimum(1.0, clip_max / (clip + 1e-06))[0:1, 0:1]
    refs["clip_out"][...] = clip
    grads = own_parts(refs["own"], refs["small"], mp)
    order, squares, steps = 0, [], []
    for name in PIECES:
        weights = load(refs, "weight", name)
        parts = [
            adam(g, factor, m, s, p)
            for g, m, s, p in zip(grads[name], load(refs, "moment", name), load(refs, "second", name), weights)
        ]
        if order < 5:
            pair = [(sums[1 + order : 2 + order, 0:1], sums[8 + order : 9 + order, 0:1])]
        else:
            kept = 1 if name == "vector" else None
            pair = []
            for a in (weights[0], parts[0][3]):
                total = jnp.sum(a * a, axis=1, keepdims=True)
                pair.append(total if kept else jnp.sum(total, axis=0, keepdims=True))
            pair = [tuple(pair)]
        order += 1
        old, way = jnp.sqrt(pair[0][0]), jnp.sqrt(pair[0][1])
        squares.append((old, way))
        ratio = old / (way + 1e-06)
        for i, (weight, part) in enumerate(zip(weights, parts)):
            new = weight - learn_rate * ratio * part[3]
            stored = {"grad": part[0], "new": new, "m": part[1], "s": part[2], "copy": new.astype(bf16)}
            for kind, value in stored.items():
                ref = refs[name + "_out_" + kind]
                if name == "qkv":
                    ref[i] = value
                else:
                    ref[...] = value.reshape(ref.shape)
    place = lax.broadcasted_iota(jnp.int32, (8, 128), 0)
    lane = lax.broadcasted_iota(jnp.int32, (8, 128), 1)
    trust = jnp.zeros((8, 128), f32)
    for side in range(2):
        column = 0
        for pair in squares:
            for r in range(pair[side].shape[0]):
                value = jnp.broadcast_to(pair[side][r : r + 1, :], (8, 128))
                trust = jnp.where((place == side) & (lane == column), value, trust)
                column += 1
    refs["trust_out"][...] = trust[0:2, 0:14]
    for copy in copies:
        copy.wait()


OUT_KINDS = (("grad", f32), ("new", f32), ("m", f32), ("s", f32), ("copy", bf16))


def update_call(block, feats, own, small, sums, params):
    vmem = pl.BlockSpec(memory_space=pltpu.VMEM)
    anywhere = pl.BlockSpec(memory_space=pl.ANY)
    inputs = {"block_in": (block, vmem), "feats_in": (feats, vmem)}
    inputs.update(own=(own, vmem), small=(small, vmem), sums=(sums, vmem))
    for name in PIECES:
        for kind in SHAPES:
            inputs[name + "_" + kind] = (params[name + "_" + kind], vmem)
    outs = {"block_out": (block.shape, bf16, anywhere), "feats_out": (feats.shape, f32, anywhere)}
    outs["clip_out"] = ((1, 128), f32, vmem)
    outs["trust_out"] = ((2, 14), f32, vmem)
    for name in PIECES:
        for kind, dtype in OUT_KINDS:
            outs[name + "_out_" + kind] = (params[name + "_weight"].shape, dtype, vmem)
    names = list(inputs) + list(outs) + ["sem"]
    result = pl.pallas_call(
        functools.partial(update_kernel, names),
        out_shape=[jax.ShapeDtypeStruct(*v[:2]) for v in outs.values()],
        in_specs=[v[1] for v in inputs.values()],
        out_specs=[v[2] for v in outs.values()],
        scratch_shapes=[pltpu.SemaphoreType.DMA((2,))],
        compiler_params=pltpu.CompilerParams(vmem_limit_bytes=60 * 1024 * 1024),
    )(*[v[0] for v in inputs.values()])
    return dict(zip(outs, result))


def close_shards(*arrays):
    feats, centres, counts, cotangent = arrays[:4]
    mp_count = lax.axis_size("mp")
    mp_index = lax.axis_index("mp")
    share = feats.shape[0] // mp_count
    clouds = share // PAD
    inner = arrays[6].shape[1] * mp_count
    params = {}
    for k, kind in enumerate(SHAPES):
        for i, name in enumerate(PIECES):
            array = arrays[4 + 8 * k + i]
            if name in ("out", "down"):
                array = array.T
            params[name + "_" + kind] = array
    mine = lax.dynamic_slice_in_dim(centres, mp_index * share, share, 1).T.reshape(clouds, PAD, 3)
    points = jnp.pad(mine, ((0, 0), (0, SLOT - PAD), (0, 0)))
    points = jnp.concatenate((points, jnp.ones((clouds, SLOT, 1), f32)), axis=2)
    points = jnp.pad(points.reshape(clouds * SLOT, 4), ((0, 0), (0, 4)))
    block, grad, own, small, sums = main_call(mp_count, inner, counts, feats, cotangent, points, params)
    out = update_call(block, grad, own, small, sums, params)
    outputs = [out["block_out"], out["feats_out"], out["clip_out"][0, 0], out["trust_out"]]
    for name in PIECES:
        for kind, _ in OUT_KINDS:
            array = out[name + "_out_" + kind]
            if name in ("out", "down"):
                array = array.T
            outputs.append(array)
    return tuple(outputs)


def solution(mesh):
    qkv, outw, upw, bias, whole = P(None, "dp", "mp"), P("mp", "dp"), P("dp", "mp"), P("mp"), P()
    params = (qkv, outw, upw, bias, outw, whole, whole, whole)
    in_specs = (P("dp", None), P(None, "dp"), P("dp"), P("dp", None)) + params * 3
    rows = P(("dp", "mp"), None)
    out_specs = (rows, rows, P(), P()) + tuple(spec for spec in params for _ in range(5))
    form = close_shards if (mesh.shape["dp"], mesh.shape["mp"]) == (8, 4) else shards
    return jax.shard_map(form, mesh=mesh, in_specs=in_specs, out_specs=out_specs, check_vma=False)
```

```python
import functools
import math

import jax
import jax.numpy as jnp
from jax import lax
from jax.experimental import pallas as pl
from jax.experimental.pallas import tpu as pltpu
from jax.sharding import PartitionSpec as P

HD = 64
PAD = 38
SLOT = 40
GROUP = 4

norm_eps = 1e-05
beta_one = 0.5
beta_two = 0.5
adam_eps = 1e-06
decay_rate = 0.01
learn_rate = 0.3
clip_max = 1.0
step_count = 3.0
neg_fill = -1e30
highest = lax.Precision.HIGHEST
f32 = jnp.float32
bf16 = jnp.bfloat16

NN = (((1,), (0,)), ((), ()))
NT = (((1,), (1,)), ((), ()))
TN = (((0,), (0,)), ((), ()))


def dot(a, b, dims=NN, precision=None):
    return lax.dot_general(a, b, dims, precision=precision, preferred_element_type=f32)


def gelu_pair(v):
    cdf = 0.5 * (1.0 + lax.erf(v * 0.7071067811865476))
    return v * cdf, cdf + v * jnp.exp(-0.5 * v * v) * 0.3989422804014327


def piece_squares(array, tensor_index):
    if tensor_index == 5:
        return jnp.sum(array * array, axis=1)
    return jnp.sum(array * array)[None]


def piece_ratio(trust_ratio, tensor_index):
    if tensor_index < 5:
        return trust_ratio[tensor_index]
    if tensor_index == 5:
        return trust_ratio[5:12][:, None]
    return trust_ratio[tensor_index + 6]


def side_by_side(take, parts):
    return jnp.concatenate([take(j) for j in parts], axis=1)


class Layer:
    def __init__(self, refs, mp, clouds, width, inner):
        self.__dict__.update(refs)
        self.mp = mp
        self.clouds = clouds
        self.width = width
        self.inner = inner
        self.rows = clouds * SLOT
        self.block = GROUP * SLOT
        self.blocks = clouds // GROUP
        self.hid = self.proj_low.shape[0]

    def live(self, j):
        return [h for h in range(2) if (2 * j + h) % 2 == 0 or j < self.mp // 2]

    def spread_rows(self):
        zeros = jnp.zeros((SLOT - PAD, self.width), f32)
        self.stage[...] = self.feats[...].astype(f32)
        for c in range(self.clouds):
            self.stream[pl.ds(SLOT * c, PAD), :] = self.stage[pl.ds(PAD * c, PAD), :]
            self.stream[pl.ds(SLOT * c + PAD, SLOT - PAD), :] = zeros
        self.stage[...] = self.cotangent[...].astype(f32)
        for c in range(self.clouds):
            self.middle_grad[pl.ds(SLOT * c, PAD), :] = self.stage[pl.ds(PAD * c, PAD), :]
            self.middle_grad[pl.ds(SLOT * c + PAD, SLOT - PAD), :] = zeros

    def keep_block(self, b, shape, dim):
        place = lax.broadcasted_iota(jnp.int32, shape, dim)
        bound = jnp.zeros(shape, jnp.int32)
        for i in range(GROUP):
            limit = self.counts[b * GROUP + i] + SLOT * i
            inside = (place >= SLOT * i) & (place < limit)
            bound = jnp.where(inside, 1, bound)
        return bound > 0

    def masks(self):
        n = self.block

        def step(b, carry):
            keys = lax.broadcasted_iota(jnp.int32, (n, n), 0)
            query = lax.broadcasted_iota(jnp.int32, (n, n), 1)
            fill = jnp.full((n, n), neg_fill, f32)
            for i in range(GROUP):
                limit = self.counts[b * GROUP + i] + SLOT * i
                inside = (keys >= SLOT * i) & (keys < limit)
                mine = (query >= SLOT * i) & (query < SLOT * (i + 1))
                fill = jnp.where(inside & mine, 0.0, fill)
            self.mask[b] = fill
            self.keep[pl.ds(b * n, n), :] = jnp.where(self.keep_block(b, (n, 128), 0), 1.0, 0.0)
            return carry

        lax.fori_loop(0, self.blocks, step, 0)

    def norm(self, x):
        centre = x - jnp.mean(x, axis=-1, keepdims=True)
        spread = jnp.mean(centre * centre, axis=-1, keepdims=True)
        rate = lax.rsqrt(spread + norm_eps)
        return centre * rate, rate

    def norm_back(self, grad, hat, rate, gain):
        scaled = grad * gain
        first = jnp.mean(scaled, axis=-1, keepdims=True)
        second = jnp.mean(scaled * hat, axis=-1, keepdims=True)
        return rate * (scaled - first - hat * second)

    def entry(self):
        value, slope = gelu_pair(dot(self.points[...], self.pos_hidden[...], NN, highest))
        hidden = value.astype(bf16)
        self.pos_slope[...] = slope
        self.hidden[...] = hidden
        x = self.stream[...] + (dot(hidden, self.proj_low[...]) + self.vec[6:7, :])
        hat, rate = self.norm(x)
        self.stream[...] = x
        self.hat_one[...] = hat
        self.rate_one[...] = jnp.broadcast_to(rate, (self.rows, 128))
        self.normed_one[...] = (hat * self.vec[0:1, :] + self.vec[2:3, :]).astype(bf16)

    def project(self):
        for j in range(0, self.mp, 2):
            both = dot(self.normed_one[...], side_by_side(self.w_qkv, (j, j + 1))).astype(bf16)
            self.qkv[j], self.qkv[j + 1] = both[:, :384], both[:, 384:]

    def lanes(self, h, n):
        lane = lax.broadcasted_iota(jnp.int32, (n, 128), 1)
        return (lane < HD) if h == 0 else (lane >= HD)

    def heads(self, rows):
        for j in range(self.mp):
            query = self.qkv[j, rows, 0:128] * jnp.asarray(1.0 / math.sqrt(HD), bf16)
            for h in self.live(j):
                own = self.lanes(h, self.block)
                alone = jnp.where(own, query, jnp.zeros_like(query))
                yield j, own, alone, self.qkv[j, rows, 128:256], self.qkv[j, rows, 256:384]

    def attend(self, start, stop):
        n = self.block

        def step(b, carry):
            rows = pl.ds(pl.multiple_of(b * n, n), n)
            mask = self.mask[b]
            live = list(self.heads(rows))
            scores = [dot(keys, query, NT) + mask for _, _, query, keys, _ in live]
            low = []
            for i, score in enumerate(scores):
                expo = jnp.exp(score - jnp.max(score, axis=0, keepdims=True))
                probs = expo * (1.0 / jnp.sum(expo, axis=0, keepdims=True))
                self.probs[i, b] = probs
                low.append(probs.astype(bf16))
            mixed = [jnp.zeros((n, 128), f32)] * self.mp
            for probs, (j, own, _, _, values) in zip(low, live):
                mixed[j] = jnp.where(own, dot(probs, values, TN), mixed[j])
            for j in range(self.mp):
                self.attn_low[j, rows, :] = mixed[j].astype(bf16)
            return carry

        lax.fori_loop(start, stop, step, 0, unroll=2)

    def middle(self):
        parts = range(self.mp)
        mixed = side_by_side(lambda j: self.attn_low[j], parts)
        x = self.stream[...] + self.vec[4:5, :] + dot(mixed, side_by_side(self.w_out, parts), NT)
        hat, rate = self.norm(x)
        self.stream[...] = x
        self.hat_two[...] = hat
        self.rate_two[...] = jnp.broadcast_to(rate, (self.rows, 128))
        self.normed_two[...] = (hat * self.vec[1:2, :] + self.vec[3:4, :]).astype(bf16)

    def feed(self):
        total = self.stream[...]
        for j in range(0, self.mp, 2):
            pair = (j, j + 1)
            bias = side_by_side(lambda i: self.up_bias[i, 0:1, :], pair)
            value, slope = gelu_pair(dot(self.normed_two[...], side_by_side(self.w_up, pair)) + bias)
            low = value.astype(bf16)
            half = low.shape[1] // 2
            for k, i in enumerate(pair):
                self.activated[i] = low[:, k * half : (k + 1) * half]
                self.slope[i] = slope[:, k * half : (k + 1) * half]
            total = total + dot(low, side_by_side(self.w_down, pair), NT)
        self.stream[...] = total

    def top(self):
        keep = jnp.concatenate([self.keep[...]] * (self.width // 128), axis=1)
        self.stream[...] = (self.stream[...] + self.vec[5:6, :]) * keep

    def grad_start(self):
        self.vec_grad[...] = jnp.zeros_like(self.vec_grad)
        keep = jnp.concatenate([self.keep[...]] * (self.width // 128), axis=1)
        grad = self.middle_grad[...] * keep
        self.middle_grad[...] = grad
        self.grad_top[...] = grad.astype(bf16)
        self.vec_grad[5:6, :] = jnp.sum(grad, axis=0, keepdims=True)

    def feed_back(self):
        total = None
        for j in range(0, self.mp, 2):
            pair = (j, j + 1)
            grad = dot(self.grad_top[...], side_by_side(self.w_down, pair))
            low = (grad * side_by_side(lambda i: self.slope[i], pair)).astype(bf16)
            bias = jnp.sum(low.astype(f32), axis=0, keepdims=True)
            half = low.shape[1] // 2
            for k, i in enumerate(pair):
                self.grad_pre[i] = low[:, k * half : (k + 1) * half]
                self.up_bias_grad[i, 0:1, :] = bias[:, k * half : (k + 1) * half]
            term = dot(low, side_by_side(self.w_up, pair), NT)
            total = term if j == 0 else total + term
        self.normed_grad[...] = total

    def middle_back(self):
        grad, hat = self.normed_grad[...], self.hat_two[...]
        rate = jnp.concatenate([self.rate_two[...]] * (self.width // 128), axis=1)
        self.vec_grad[1:2, :] = jnp.sum(grad * hat, axis=0, keepdims=True)
        self.vec_grad[3:4, :] = jnp.sum(grad, axis=0, keepdims=True)
        out = self.middle_grad[...] + self.norm_back(grad, hat, rate, self.vec[1:2, :])
        self.middle_grad[...] = out
        self.vec_grad[4:5, :] = jnp.sum(out, axis=0, keepdims=True)
        low = out.astype(bf16)
        self.middle_low[...] = low
        grads = dot(low, side_by_side(self.w_out, range(self.mp))).astype(bf16)
        for j in range(self.mp):
            self.attn_grad[j] = grads[:, 128 * j : 128 * j + 128]

    def attend_back(self):
        n = self.block
        scale = 1.0 / math.sqrt(HD)

        def step(b, carry):
            rows = pl.ds(pl.multiple_of(b * n, n), n)
            live = list(self.heads(rows))
            mine = []
            for j, own, _, _, _ in live:
                grad = self.attn_grad[j, rows, :]
                mine.append(jnp.where(own, grad, jnp.zeros_like(grad)))
            grad_probs = [dot(values, g, NT) for g, (_, _, _, _, values) in zip(mine, live)]
            scores = []
            grad_values = [jnp.zeros((n, 128), f32)] * self.mp
            for i, (j, _, _, _, _) in enumerate(live):
                probs = self.probs[i, b]
                grad_values[j] = grad_values[j] + dot(probs.astype(bf16), mine[i])
                inner = jnp.sum(probs * grad_probs[i], axis=0, keepdims=True)
                scores.append((probs * (grad_probs[i] - inner)).astype(bf16))
            grad_query = [jnp.zeros((n, 128), f32)] * self.mp
            grad_keys = [jnp.zeros((n, 128), f32)] * self.mp
            for grad, (j, own, query, keys, _) in zip(scores, live):
                grad_keys[j] = grad_keys[j] + dot(grad, query)
                grad_query[j] = jnp.where(own, dot(grad, keys, TN), grad_query[j])
            for j in range(self.mp):
                self.grad_proj[j, rows, 0:128] = (grad_query[j] * scale).astype(bf16)
                self.grad_proj[j, rows, 128:256] = grad_keys[j].astype(bf16)
                self.grad_proj[j, rows, 256:384] = grad_values[j].astype(bf16)
            return carry

        lax.fori_loop(0, self.blocks, step, 0, unroll=2)

    def entry_back(self):
        grad = None
        for j in range(0, self.mp, 2):
            pair = (j, j + 1)
            term = dot(side_by_side(lambda i: self.grad_proj[i], pair), side_by_side(self.w_qkv, pair), NT)
            grad = term if j == 0 else grad + term
        hat = self.hat_one[...]
        rate = jnp.concatenate([self.rate_one[...]] * (self.width // 128), axis=1)
        self.vec_grad[0:1, :] = jnp.sum(grad * hat, axis=0, keepdims=True)
        self.vec_grad[2:3, :] = jnp.sum(grad, axis=0, keepdims=True)
        out = self.middle_grad[...] + self.norm_back(grad, hat, rate, self.vec[0:1, :])
        self.middle_grad[...] = out
        self.vec_grad[6:7, :] = jnp.sum(out, axis=0, keepdims=True)
        low = out.astype(bf16)
        self.pos_low[...] = low
        self.pre_grad[...] = dot(low, self.proj_low[...], NT) * self.pos_slope[...]

    def turn(self, source, target):
        for i in range(self.rows // 128):
            target[:, 128 * i : 128 * i + 128] = source[128 * i : 128 * i + 128, :].T

    def gather_rows(self, source, target):
        for c in range(self.clouds):
            target[pl.ds(PAD * c, PAD), :] = source[pl.ds(SLOT * c, PAD), :]


def layer_scratch(mp, clouds, width, inner, hid):
    rows = clouds * SLOT
    block = GROUP * SLOT
    cols = inner // mp
    heads = mp + mp // 2
    shapes = dict(
        stage=((clouds * PAD, width), f32),
        stream=((rows, width), f32),
        middle_grad=((rows, width), f32),
        mask=((clouds // GROUP, block, block), f32),
        keep=((rows, 128), f32),
        pos_slope=((rows, hid), f32),
        hidden=((rows, hid), bf16),
        hat_one=((rows, width), f32),
        rate_one=((rows, 128), f32),
        normed_one=((rows, width), bf16),
        qkv=((mp, rows, 384), bf16),
        probs=((heads, clouds // GROUP, block, block), f32),
        attn_low=((mp, rows, 128), bf16),
        hat_two=((rows, width), f32),
        rate_two=((rows, 128), f32),
        normed_two=((rows, width), bf16),
        activated=((mp, rows, cols), bf16),
        slope=((mp, rows, cols), f32),
        grad_top=((rows, width), bf16),
        grad_pre=((mp, rows, cols), bf16),
        normed_grad=((rows, width), f32),
        middle_low=((rows, width), bf16),
        attn_grad=((mp, rows, 128), bf16),
        grad_proj=((mp, rows, 384), bf16),
        pos_low=((rows, width), bf16),
        pre_grad=((rows, hid), f32),
        turned=((width, rows), bf16),
    )
    return shapes


def compute_kernel(names, mp, clouds, width, inner, *args):
    refs = dict(zip(names, args))
    layer = Layer(refs, mp, clouds, width, inner)
    w = layer.w
    cols = inner // mp
    layer.w_qkv = lambda j: w[j, :, 0:384]
    layer.w_out = lambda j: w[j, :, 384:512]
    layer.w_up = lambda j: w[j, :, 512 : 512 + cols]
    layer.w_down = lambda j: w[j, :, 512 + cols : 512 + 2 * cols]
    layer.proj_low[...] = layer.pos_proj[...].astype(bf16)
    layer.spread_rows()
    layer.masks()
    layer.entry()
    layer.project()
    layer.attend(0, layer.blocks)
    layer.middle()
    layer.feed()
    layer.top()
    layer.gather_rows(layer.stream, layer.stage)
    layer.block_out[...] = layer.stage[...].astype(bf16)
    layer.grad_start()
    layer.feed_back()
    g = layer.grads
    layer.turn(layer.grad_top, layer.turned)
    for j in range(mp):
        g[j, :, 512 + cols : 512 + 2 * cols] = dot(layer.turned[...], layer.activated[j])
    layer.turn(layer.normed_two, layer.turned)
    for j in range(mp):
        g[j, :, 512 : 512 + cols] = dot(layer.turned[...], layer.grad_pre[j])
    layer.middle_back()
    layer.turn(layer.middle_low, layer.turned)
    for j in range(mp):
        g[j, :, 384:512] = dot(layer.turned[...], layer.attn_low[j])
    layer.attend_back()
    layer.turn(layer.normed_one, layer.turned)
    for j in range(mp):
        g[j, :, 0:384] = dot(layer.turned[...], layer.grad_proj[j])
    layer.entry_back()
    layer.gather_rows(layer.middle_grad, layer.feats_grad)
    layer.proj_grad[...] = dot(layer.hidden[...], layer.pos_low[...], TN)
    layer.pos_grad[...] = dot(layer.points[...], layer.pre_grad[...], TN, highest)


def compute(mp, width, inner, counts, feats, cotangent, points, w, up_bias, vec, pos_hidden, pos_proj):
    clouds = counts.shape[0]
    hid = pos_proj.shape[0]
    inputs = ["counts", "feats", "cotangent", "points", "w", "up_bias", "vec", "pos_hidden", "pos_proj"]
    outs = dict(
        block_out=((clouds * PAD, width), bf16),
        feats_grad=((clouds * PAD, width), f32),
        grads=(w.shape, f32),
        up_bias_grad=((mp, 8, inner // mp), f32),
        vec_grad=((8, width), f32),
        pos_grad=((8, hid), f32),
        proj_grad=((hid, width), f32),
    )
    scratch = layer_scratch(mp, clouds, width, inner, hid)
    scratch["proj_low"] = ((hid, width), bf16)
    names = inputs + list(outs) + list(scratch)
    vmem = pl.BlockSpec(memory_space=pltpu.VMEM)
    return pl.pallas_call(
        functools.partial(compute_kernel, names, mp, clouds, width, inner),
        out_shape=[jax.ShapeDtypeStruct(*v) for v in outs.values()],
        in_specs=[pl.BlockSpec(memory_space=pltpu.SMEM)] + [vmem] * (len(inputs) - 1),
        out_specs=[vmem] * len(outs),
        scratch_shapes=[pltpu.VMEM(*v) for v in scratch.values()],
        compiler_params=pltpu.CompilerParams(vmem_limit_bytes=60 * 1024 * 1024),
    )(counts, feats, cotangent, points, w, up_bias, vec, pos_hidden, pos_proj)


def shards(
    feats,
    centres,
    counts,
    cotangent,
    qkv_weight,
    out_weight,
    up_weight,
    up_bias,
    down_weight,
    norm_vectors,
    pos_hidden,
    pos_proj,
    qkv_moment,
    out_moment,
    up_moment,
    bias_moment,
    down_moment,
    vector_moment,
    hidden_moment,
    proj_moment,
    qkv_second,
    out_second,
    up_second,
    bias_second,
    down_second,
    vector_second,
    hidden_second,
    proj_second,
):
    mp_count = lax.axis_size("mp")
    mp_index = lax.axis_index("mp")
    dp_index = lax.axis_index("dp")
    share = feats.shape[0] // mp_count
    clouds = share // PAD
    width = feats.shape[1]
    cols = up_weight.shape[1]
    inner = cols * mp_count
    start = mp_index * share
    my_feats = lax.dynamic_slice_in_dim(feats, start, share, 0)
    my_top = lax.dynamic_slice_in_dim(cotangent, start, share, 0)
    my_counts = lax.dynamic_slice_in_dim(counts, mp_index * clouds, clouds, 0)
    my_points = lax.dynamic_slice_in_dim(centres, start, share, 1).T.reshape(clouds, PAD, 3)
    points = jnp.pad(my_points, ((0, 0), (0, SLOT - PAD), (0, 0)))
    points = jnp.concatenate((points, jnp.ones((clouds, SLOT, 1), f32)), axis=2)
    points = jnp.pad(points.reshape(clouds * SLOT, 4), ((0, 0), (0, 4)))
    packed = jnp.concatenate(
        (qkv_weight[0], qkv_weight[1], qkv_weight[2], out_weight.T, up_weight, down_weight.T), axis=1
    ).astype(bf16)
    whole = lax.all_gather(packed, "dp", axis=0, tiled=True)
    whole = lax.all_gather(whole, "mp", axis=0)
    bias = lax.all_gather(jnp.broadcast_to(up_bias[None], (8, cols)), "mp", axis=0)
    vec = jnp.pad(norm_vectors, ((0, 1), (0, 0)))
    hidden = jnp.pad(pos_hidden, ((0, 4), (0, 0)))
    block_out, feats_grad, grads, bias_grad, vec_grad, pos_grad, proj_grad = compute(
        mp_count, width, inner, my_counts, my_feats, my_top, points, whole, bias, vec, hidden, pos_proj
    )
    own = lax.psum_scatter(grads, "mp", scatter_dimension=0, tiled=True)[0]
    own = lax.psum_scatter(own, "dp", scatter_dimension=0, tiled=True)
    bias_grad, vector_grad, pos_grad, proj_grad = lax.psum(
        (bias_grad[:, 0], vec_grad[:7], pos_grad[:4], proj_grad), ("dp", "mp")
    )
    bias_grad = lax.dynamic_index_in_dim(bias_grad, mp_index, 0, keepdims=False)
    qkv_grad = jnp.stack((own[:, 0:128], own[:, 128:256], own[:, 256:384]))
    out_grad = own[:, 384:512].T
    up_grad = own[:, 512 : 512 + cols]
    down_grad = own[:, 512 + cols :].T
    leader = ((dp_index == 0) & (mp_index == 0)).astype(f32)
    first_dp = (dp_index == 0).astype(f32)
    owners = [1.0, 1.0, 1.0, first_dp, 1.0, leader, leader, leader]
    weights = [qkv_weight, out_weight, up_weight, up_bias, down_weight, norm_vectors, pos_hidden, pos_proj]
    moments = [
        qkv_moment,
        out_moment,
        up_moment,
        bias_moment,
        down_moment,
        vector_moment,
        hidden_moment,
        proj_moment,
    ]
    seconds = [
        qkv_second,
        out_second,
        up_second,
        bias_second,
        down_second,
        vector_second,
        hidden_second,
        proj_second,
    ]
    grads = [qkv_grad, out_grad, up_grad, bias_grad, down_grad, vector_grad, pos_grad, proj_grad]
    grad_square = jnp.zeros((), f32)
    weight_square = []
    for i in range(8):
        grad_square = grad_square + owners[i] * jnp.sum(grads[i] * grads[i])
        weight_square.append(owners[i] * piece_squares(weights[i], i))
    totals = lax.psum(jnp.concatenate([grad_square[None]] + weight_square), ("dp", "mp"))
    clip_norm = jnp.sqrt(totals[0])
    factor = jnp.minimum(1.0, clip_max / (clip_norm + 1e-06))
    clipped_list, moment_list, second_list, direction_list, update_square = [], [], [], [], []
    for i in range(8):
        clipped = grads[i] * factor
        moment_new = beta_one * moments[i] + (1.0 - beta_one) * clipped
        second_new = beta_two * seconds[i] + (1.0 - beta_two) * clipped * clipped
        direction = (
            moment_new
            / (1.0 - beta_one**step_count)
            / (jnp.sqrt(second_new / (1.0 - beta_two**step_count)) + adam_eps)
            + decay_rate * weights[i]
        )
        clipped_list.append(clipped)
        moment_list.append(moment_new)
        second_list.append(second_new)
        direction_list.append(direction)
        update_square.append(owners[i] * piece_squares(direction, i))
    update_total = lax.psum(jnp.concatenate(update_square), ("dp", "mp"))
    weight_norm = jnp.sqrt(totals[1:])
    update_norm = jnp.sqrt(update_total)
    trust_ratio = weight_norm / (update_norm + 1e-06)
    outputs = [block_out, feats_grad, clip_norm, jnp.stack((weight_norm, update_norm))]
    for i in range(8):
        new_weight = weights[i] - learn_rate * piece_ratio(trust_ratio, i) * direction_list[i]
        outputs.append(clipped_list[i])
        outputs.append(new_weight)
        outputs.append(moment_list[i])
        outputs.append(second_list[i])
        outputs.append(new_weight.astype(bf16))
    return tuple(outputs)


class Links:
    def __init__(self, send, recv):
        dp, mp = lax.axis_index("dp"), lax.axis_index("mp")
        self.z, self.y = dp // 2, lax.rem(dp, 2)
        self.x, self.c = mp // 2, lax.rem(mp, 2)
        self.mp = mp
        self.plane = self.y * 4 + mp
        self.me = dp * 4 + mp
        self.line = [self.z, self.z + 1 - 2 * lax.rem(self.z, 2), lax.rem(self.z + 2, 4), 3 - self.z]
        self.send_sem, self.recv_sem = send, recv
        self.counts = [0, 0]
        self.sent = []

    def at(self, z, y, x, c):
        return (z * 2 + y, x * 2 + c)

    def core(self):
        return self.at(self.z, self.y, self.x, 1 - self.c)

    def side(self):
        return self.at(self.z, self.y, 1 - self.x, self.c)

    def deep(self):
        return self.at(self.z, 1 - self.y, self.x, self.c)

    def far(self, k):
        return self.at(self.line[k], self.y, self.x, self.c)

    def round(self, k):
        other = lax.rem(self.plane + k, 8)
        return (self.z * 2 + other // 4, lax.rem(other, 4))

    def any(self, k):
        other = lax.rem(self.me + k, 32)
        return (other // 4, lax.rem(other, 4))

    def peers(self):
        return [self.far(k) for k in range(1, 4)] + [self.round(k) for k in range(1, 8)]

    def greet(self, everyone=False):
        barrier = pltpu.get_barrier_semaphore()
        for who in [self.any(k) for k in range(1, 32)] if everyone else self.peers():
            pl.semaphore_signal(barrier, inc=1, device_id=who, device_id_type=pl.DeviceIdType.MESH)

    def met(self, count):
        pl.semaphore_wait(pltpu.get_barrier_semaphore(), count)

    def copy(self, source, target, i):
        return pltpu.make_async_remote_copy(
            src_ref=source,
            dst_ref=target,
            send_sem=self.send_sem.at[i] if i < self.send_sem.shape[0] else self.send_sem.at[0],
            recv_sem=self.recv_sem.at[i] if i < self.recv_sem.shape[0] else self.recv_sem.at[0],
            device_id=self.core(),
            device_id_type=pl.DeviceIdType.MESH,
        )

    def mark(self, side):
        self.counts[side] += 1
        return self.counts[side] - 1

    def send(self, source, target, who, out=None, into=None):
        into = self.mark(1) if into is None else into
        copy = pltpu.make_async_remote_copy(
            src_ref=source,
            dst_ref=target,
            send_sem=self.send_sem.at[self.mark(0) if out is None else out],
            recv_sem=self.recv_sem.at[into],
            device_id=who,
            device_id_type=pl.DeviceIdType.MESH,
        )
        copy.start()
        if out is None:
            self.sent.append(copy)
        return into

    def wait(self, i, target):
        self.copy(target, target, i).wait_recv()

    def sent_all(self, out, source):
        self.sent.append(self.copy(source, source, out))

    def finish(self):
        for copy in self.sent:
            copy.wait_send()


class Gather:
    def __init__(self, links, w, lo, hi, flip):
        self.links, self.w, self.lo, self.hi, self.flip = links, w, lo, hi, flip

    def part(self, mp, z, y):
        return self.w.at[mp, z, y, :, self.lo : self.hi]

    def start(self):
        k = self.links
        own = self.part(k.mp, k.z, k.y)
        self.along = [k.send(own, own, k.far(i)) for i in (1, 2, 3)]
        self.out = [k.mark(0) for _ in range(5)]
        self.first = [k.mark(1) for _ in range(4)]
        self.into = [k.mark(1) for _ in range(4)]

    def step(self, i):
        k = self.links
        block = self.part(k.mp, k.line[i], k.y)
        if i:
            k.wait(self.along[i - 1], block)
        near, next_ = (k.side(), k.deep()) if self.flip else (k.deep(), k.side())
        k.send(block, block, near, self.out[0], self.first[i])
        k.send(block, block, k.core(), self.out[1], self.into[0])
        k.send(block, block, next_, self.out[2], self.into[1])

    def regions(self, mp, z):
        k = self.links
        across = mp + 2 - 4 * k.x
        side, deep = self.part(across, z, k.y), self.part(mp, z, 1 - k.y)
        return (side, deep) if self.flip else (deep, side), self.part(across, z, 1 - k.y)

    def hop(self, i):
        k = self.links
        block = self.regions(k.mp, k.line[i])[0][0]
        k.wait(self.first[i], block)
        k.send(block, block, k.deep() if self.flip else k.side(), self.out[3], self.into[2])
        k.send(block, block, k.core(), self.out[4], self.into[3])

    def rest(self):
        k = self.links
        block = self.regions(k.mp, slice(None))[0][1]
        k.wait(self.into[1], block)
        self.rest_twin = k.send(block, block, k.core())

    def corner(self):
        k = self.links
        block = self.regions(k.mp, slice(None))[1]
        k.wait(self.into[2], block)
        self.corner_twin = k.send(block, block, k.core())

    def end(self):
        k = self.links
        twin = k.mp + 1 - 2 * k.c
        near, corner = self.regions(twin, slice(None))
        k.wait(self.into[0], self.part(twin, slice(None), k.y))
        k.wait(self.into[3], near[0])
        k.wait(self.rest_twin, near[1])
        k.wait(self.corner_twin, corner)
        line = self.part(k.mp, slice(None), k.y)
        first = self.regions(k.mp, slice(None))[0][0]
        for out, block in zip(self.out, (line, line, line, first, first)):
            k.sent_all(out, block)


class Scatter:
    def __init__(self, links, refs, flip):
        self.links, self.flip = links, flip
        self.__dict__.update(refs)

    def start(self):
        k = self.links
        self.first = k.send(self.core_out, self.core_in, k.core())

    def pair(self, x, z, y):
        return self.kept[x, z, y] + self.core_in[x, z, y].astype(f32)

    def second(self):
        k = self.links
        k.wait(self.first, self.core_in)
        if self.flip:
            for x in range(2):
                for z in range(4):
                    self.next_out[x, z] = self.pair(x, z, 1 - k.y).astype(bf16)
            self.next = k.send(self.next_out, self.next_in, k.deep())
        else:
            for y in range(2):
                for z in range(4):
                    self.next_out[y, z] = self.pair(1 - k.x, z, y).astype(bf16)
            self.next = k.send(self.next_out, self.next_in, k.side())

    def third(self):
        k = self.links
        k.wait(self.next, self.next_in)
        for z in range(4):
            if self.flip:
                total = self.pair(1 - k.x, z, k.y) + self.next_in[1 - k.x, z].astype(f32)
            else:
                total = self.pair(k.x, z, 1 - k.y) + self.next_in[1 - k.y, z].astype(f32)
            self.last_out[z] = total.astype(bf16)
        self.last = k.send(self.last_out, self.last_in, k.side() if self.flip else k.deep())

    def fourth(self):
        k = self.links
        k.wait(self.last, self.last_in)
        self.along = []
        for i in range(4):
            z = k.line[i]
            mid = self.next_in[k.x, z] if self.flip else self.next_in[k.y, z]
            total = self.pair(k.x, z, k.y) + mid.astype(f32) + self.last_in[z].astype(f32)
            if i == 0:
                self.own[...] = total
            else:
                self.far_out[i - 1] = total.astype(bf16)
                self.along.append(k.send(self.far_out.at[i - 1], self.far_in.at[i - 1], k.far(i)))

    def end(self):
        k = self.links
        total = self.own[...]
        for i in range(3):
            k.wait(self.along[i], self.far_in.at[i])
            total = total + self.far_in[i].astype(f32)
        return total


def scatter_scratch(tag, cols):
    return {
        tag + "kept": ((2, 4, 2, 48, cols), f32),
        tag + "core_out": ((2, 4, 2, 48, cols), bf16),
        tag + "core_in": ((2, 4, 2, 48, cols), bf16),
        tag + "next_out": ((2, 4, 48, cols), bf16),
        tag + "next_in": ((2, 4, 48, cols), bf16),
        tag + "last_out": ((4, 48, cols), bf16),
        tag + "last_in": ((4, 48, cols), bf16),
        tag + "far_out": ((3, 48, cols), bf16),
        tag + "far_in": ((3, 48, cols), bf16),
        tag + "own": ((48, cols), f32),
    }


def stack_rows(rows, height=8):
    place = lax.broadcasted_iota(jnp.int32, (height, 128), 0)
    out = jnp.zeros((height, 128), f32)
    for i, row in enumerate(rows):
        out = jnp.where(place == i, jnp.broadcast_to(row, (height, 128)), out)
    return out


def lane_row(rows, base=None):
    lane = lax.broadcasted_iota(jnp.int32, (1, 128), 1)
    out = jnp.zeros((1, 128), f32) if base is None else base
    for i, row in enumerate(rows):
        out = jnp.where(lane == i, row, out)
    return out


def lane_value(row, i):
    lane = lax.broadcasted_iota(jnp.int32, (1, 128), 1)
    return jnp.sum(jnp.where(lane == i, row, 0.0), axis=1, keepdims=True)


def square_row(array):
    total = jnp.sum(jnp.sum(array * array, axis=0, keepdims=True), axis=1, keepdims=True)
    return jnp.broadcast_to(total, (1, 128))


def adam(grad, factor, moment, second, weight):
    clipped = grad * factor
    moment_new = beta_one * moment + (1.0 - beta_one) * clipped
    second_new = beta_two * second + (1.0 - beta_two) * clipped * clipped
    direction = (
        moment_new
        / (1.0 - beta_one**step_count)
        / (jnp.sqrt(second_new / (1.0 - beta_two**step_count)) + adam_eps)
        + decay_rate * weight
    )
    return clipped, moment_new, second_new, direction


PIECES = ("qkv", "out", "up", "bias", "down", "vector", "hidden", "proj")


def own_parts(own, small, mp):
    cols = (own.shape[1] - 512) // 2

    def wide(row, count):
        return jnp.concatenate([small[row + 8 * i : row + 8 * i + count, :] for i in range(3)], axis=1)

    place = lax.broadcasted_iota(jnp.int32, (8, cols), 0)

    return {
        "qkv": [own[:, 128 * i : 128 * i + 128] for i in range(3)],
        "out": [own[:, 384:512]],
        "up": [own[:, 512 : 512 + cols]],
        "bias": [jnp.sum(jnp.where(place == mp, wide(416, 8), 0.0), axis=0, keepdims=True)],
        "down": [own[:, 512 + cols : 512 + 2 * cols]],
        "vector": [wide(384, 7)],
        "hidden": [small[408:412, :]],
        "proj": [jnp.concatenate([small[128 * i : 128 * i + 128, :] for i in range(3)], axis=1)],
    }


def load(refs, kind, name):
    ref = refs[name + "_" + kind]
    if name == "qkv":
        return [ref[i] for i in range(3)]
    return [ref[...].reshape(1, -1)] if name == "bias" else [ref[...]]


def main_kernel(names, mp, clouds, width, inner, *args):
    refs = dict(zip(names, args))
    layer = Layer(refs, mp, clouds, width, inner)
    cols = inner // mp
    links = Links(layer.send_sem, layer.recv_sem)
    w = layer.w
    links.greet(True)
    share = clouds * PAD
    rows = pl.ds(pl.multiple_of(links.mp * share, 16), share)
    sources = {"feats": layer.feats_all.at[rows, :], "cotangent": layer.top_all.at[rows, :]}
    for kind in SHAPES:
        for name in PIECES:
            sources[name + "_" + kind] = refs[name + "_" + kind + "_all"]
    sources["points"] = layer.points_all
    copies = {
        name: pltpu.make_async_copy(source, refs[name], layer.load_sem.at[i])
        for i, (name, source) in enumerate(sources.items())
    }
    first = [name + "_weight" for name in ("qkv", "out", "up", "down", "bias")]
    early = ["feats", "points", "hidden_weight", "proj_weight", "vector_weight", "cotangent"]
    late = [copy for name, copy in copies.items() if name not in first + early]
    for name in first + early:
        copies[name].start()

    def flat(j, lo, hi):
        return w[j, :, :, :, lo:hi].reshape(width, hi - lo)

    layer.w_qkv = lambda j: flat(j, 0, 384)
    layer.w_out = lambda j: flat(j, 384, 512)
    layer.w_up = lambda j: flat(j, 512, 512 + cols)
    layer.w_down = lambda j: flat(j, 512 + cols, 512 + 2 * cols)
    for name in first:
        copies[name].wait()
    for i in range(3):
        w[links.mp, links.z, links.y, :, 128 * i : 128 * i + 128] = refs["qkv_weight"][i].astype(bf16)
    w[links.mp, links.z, links.y, :, 384:512] = refs["out_weight"][...].astype(bf16)
    w[links.mp, links.z, links.y, :, 512 : 512 + cols] = refs["up_weight"][...].astype(bf16)
    w[links.mp, links.z, links.y, :, 512 + cols : 512 + 2 * cols] = refs["down_weight"][...].astype(bf16)
    layer.up_bias[links.mp] = jnp.broadcast_to(refs["bias_weight"][...].reshape(1, cols), (8, cols))
    links.met(31)
    gathers = [
        Gather(links, w, 0, 256, False),
        Gather(links, w, 256, 512, True),
        Gather(links, w, 512, 512 + cols, False),
        Gather(links, w, 512 + cols, 512 + 2 * cols, True),
    ]
    near, wide = gathers[:2], gathers[2:]

    def each(group, step, *a):
        for g in group:
            getattr(g, step)(*a)

    for group in (near, wide):
        each(group, "start")
        each(group, "step", 0)
    own_bias = layer.up_bias.at[links.mp]
    bias_side = links.send(own_bias, own_bias, links.side())
    bias_core = links.send(own_bias, own_bias, links.core())
    for copy in late:
        copy.start()
    for name in early:
        copies[name].wait()
    layer.proj_low[...] = refs["proj_weight"][...].astype(bf16)
    layer.vec = jnp.concatenate([refs["vector_weight"][...], jnp.zeros((1, width), f32)], axis=0)
    layer.pos_hidden[...] = jnp.concatenate([refs["hidden_weight"][...], jnp.zeros((4, 128), f32)], axis=0)
    layer.counts = _Shifted(layer.counts_all, links.mp * clouds)
    layer.spread_rows()
    each(near, "step", 1)
    layer.entry()
    each(near, "step", 2)
    layer.masks()
    each(near, "step", 3)
    each(near, "hop", 0)
    each(near, "hop", 1)
    layer.grad_start()
    each(near, "hop", 2)
    each(wide, "step", 1)
    layer.turn(layer.grad_top, layer.turned_top)
    each(near, "hop", 3)
    each(wide, "step", 2)
    layer.turn(layer.normed_one, layer.turned_one)
    other_bias = layer.up_bias.at[links.mp + 2 - 4 * links.x]
    links.wait(bias_side, other_bias)
    bias_last = links.send(other_bias, other_bias, links.core())
    lead = (links.z * 2 + links.y == 0).astype(f32)

    def five(parts):
        out = []
        for name in ("qkv", "out", "up", "bias", "down"):
            row = sum(square_row(p) for p in parts[name])
            out.append(row * lead if name == "bias" else row)
        return out

    weights = {name: load(refs, "weight", name) for name in PIECES}
    zero = jnp.zeros((1, 1), f32)
    layer.old_rows[...] = lane_row([jnp.zeros((1, 128), f32)] + five(weights))
    each(near, "rest")
    each(wide, "step", 3)
    each(near, "corner")
    each(wide, "hop", 0)
    each(wide, "hop", 1)
    each(near, "end")
    layer.project()
    each(wide, "hop", 2)
    each(wide, "hop", 3)
    layer.attend(0, layer.blocks // 2)
    each(wide, "rest")
    layer.attend(layer.blocks // 2, layer.blocks)
    each(wide, "corner")
    layer.middle()
    layer.turn(layer.normed_two, layer.turned_two)
    each(wide, "end")
    twin = links.mp + 1 - 2 * links.c
    links.wait(bias_core, layer.up_bias.at[twin])
    links.wait(bias_last, layer.up_bias.at[twin + 2 - 4 * links.x])
    layer.feed()

    def scatter(tag, flip):
        return Scatter(links, {n[len(tag) :]: refs[n] for n in names if n.startswith(tag)}, flip)

    down, up = scatter("down__", True), scatter("up__", False)
    qk, vo = scatter("qk__", False), scatter("vo__", True)

    def weigh(product, *targets):
        for x in range(2):
            pair = product((2 * x, 2 * x + 1))
            kept = jnp.where(links.c == 0, pair[0], pair[1])
            sent = jnp.where(links.c == 0, pair[1], pair[0]).astype(bf16)
            lo = 0
            for target in targets:
                hi = lo + target.kept.shape[-1]
                target.core_out[x] = sent[:, lo:hi].reshape(4, 2, 48, hi - lo)
                target.kept[x] = kept[:, lo:hi].reshape(4, 2, 48, hi - lo)
                lo = hi

    def halves(turned, source, pair):
        both = dot(turned[...], side_by_side(lambda j: source[j], pair))
        half = both.shape[1] // 2
        return both[:, :half], both[:, half:]

    def heads_out(pair):
        heads = halves(layer.turned_one, layer.grad_proj, pair)
        mixed = halves(layer.turned_mid, layer.attn_low, pair)
        return [jnp.concatenate(parts, axis=1) for parts in zip(heads, mixed)]

    weigh(lambda pair: halves(layer.turned_top, layer.activated, pair), down)
    down.start()
    layer.feed_back()
    down.second()
    weigh(lambda pair: halves(layer.turned_two, layer.grad_pre, pair), up)
    up.start()
    layer.middle_back()
    up.second()
    layer.turn(layer.middle_low, layer.turned_mid)
    layer.attend_back()
    layer.top()
    layer.gather_rows(layer.stream, layer.stage_top)
    layer.block_low[...] = layer.stage_top[...].astype(bf16)
    out_copies = [pltpu.make_async_copy(layer.block_low, layer.block_out, layer.store_sem.at[1])]
    out_copies[0].start()
    down.third()
    weigh(heads_out, qk, vo)
    qk.start()
    vo.start()
    up.third()
    qk.second()
    vo.second()
    layer.entry_back()
    layer.proj_grad[...] = dot(layer.hidden[...], layer.pos_low[...], TN)
    layer.pos_grad[...] = dot(layer.points[...], layer.pre_grad[...], TN, highest)
    small = layer.small
    for i in range(3):
        lanes = slice(128 * i, 128 * i + 128)
        small[128 * i : 128 * i + 128, :] = layer.proj_grad[:, lanes]
        small[384 + 8 * i : 392 + 8 * i, :] = layer.vec_grad[:, lanes]
        small[416 + 8 * i : 424 + 8 * i, :] = stack_rows([layer.up_bias_grad[j, 0:1, lanes] for j in range(mp)])
    small[408:416, :] = layer.pos_grad[...]
    small[440:512, :] = jnp.zeros((72, 128), f32)
    layer.plane_out[...] = small[...].astype(bf16).reshape(8, 64, 128)
    layer.plane_in[links.plane] = layer.plane_out[links.plane]
    sums = []
    for k in range(1, 8):
        who = links.round(k)
        block = layer.plane_out.at[lax.rem(links.plane + k, 8)]
        sums.append(links.send(block, layer.plane_in.at[links.plane], who))
    down.fourth()
    layer.gather_rows(layer.middle_grad, layer.stage)
    out_copies.append(pltpu.make_async_copy(layer.stage, layer.feats_grad, layer.store_sem.at[0]))
    out_copies[1].start()
    qk.third()
    vo.third()
    up.fourth()
    for k in range(1, 8):
        links.wait(sums[k - 1], layer.plane_in.at[lax.rem(links.plane + 8 - k, 8)])
    total = layer.plane_in[0].astype(f32)
    for i in range(1, 8):
        total = total + layer.plane_in[i].astype(f32)
    layer.line_out[...] = total.astype(bf16).reshape(4, 16, 128)
    layer.line_in[links.z] = layer.line_out[links.z]
    sums = []
    for k in range(1, 4):
        block = layer.line_out.at[links.line[k]]
        sums.append(links.send(block, layer.line_in.at[links.z], links.far(k)))
    qk.fourth()
    vo.fourth()
    own = layer.own_grad
    own[:, 512 + cols :] = down.end()
    own[:, 512 : 512 + cols] = up.end()
    own[:, 256:512] = vo.end()
    for k in range(1, 4):
        links.wait(sums[k - 1], layer.line_in.at[links.line[k]])
    total = layer.line_in[0].astype(f32)
    for i in range(1, 4):
        total = total + layer.line_in[i].astype(f32)
    layer.whole[links.plane, links.z] = total.astype(bf16)
    sums = []
    for k in range(1, 4):
        block = layer.whole.at[links.plane, links.z]
        sums.append(links.send(block, block, links.far(k)))
    own[:, 0:256] = qk.end()
    def all_start(slots, row):
        slots[31] = row
        out, into = links.mark(0), links.mark(1)
        for k in range(1, 32):
            links.send(slots.at[31], slots.at[k - 1], links.any(k), out, into)
        links.sent_all(out, slots.at[0:31])
        return into

    def all_end(slots, into):
        links.wait(into, slots.at[0:31])
        total = slots[lax.rem(links.me + 31, 32)]
        for i in range(1, 32):
            total = total + slots[lax.rem(links.me + 31 - i + 32, 32)]
        return total

    mark = all_start(layer.slots_a, lane_row([square_row(own[...])], layer.old_rows[...]))
    for k in range(1, 4):
        links.wait(sums[k - 1], layer.whole.at[links.plane, links.line[k]])
    sums = []
    for k in range(1, 8):
        block = layer.whole.at[links.plane]
        sums.append(links.send(block, block, links.round(k)))
    for k in range(1, 8):
        links.wait(sums[k - 1], layer.whole.at[lax.rem(links.plane + 8 - k, 8)])
    small[...] = layer.whole[...].astype(f32).reshape(512, 128)
    first = all_end(layer.slots_a, mark)
    layer.small_out[...] = small[...]
    total = lane_value(first, 0) + square_row(small[0:440, :])[0:1, 0:1]
    factor = jnp.minimum(1.0, clip_max / (jnp.sqrt(total) + 1e-06))
    for copy in late:
        copy.wait()
    grads = own_parts(own, small, links.mp)
    ways = {}
    for name in ("qkv", "out", "up", "bias", "down"):
        ways[name] = [
            adam(g, factor, m, s, p)[3]
            for g, m, s, p in zip(grads[name], load(refs, "moment", name), load(refs, "second", name), weights[name])
        ]
    mark = all_start(layer.slots_b, lane_row(five(ways)))
    second = all_end(layer.slots_b, mark)
    rows = [total] + [lane_value(first, i) for i in range(1, 6)] + [zero, zero]
    rows += [lane_value(second, i) for i in range(5)]
    layer.sums[...] = stack_rows([jnp.broadcast_to(r, (1, 128)) for r in rows], 16)
    for copy in out_copies:
        copy.wait()
    links.finish()
    assert links.counts == [SENDS, ARRIVALS], links.counts


class _Shifted:
    def __init__(self, ref, start):
        self.ref, self.start = ref, start

    def __getitem__(self, i):
        return self.ref[self.start + i]


SHAPES = ("weight", "moment", "second")
SENDS, ARRIVALS = 89, 101


def main_call(mp, inner, counts, feats, cotangent, points, params):
    clouds = counts.shape[0] // mp
    width = feats.shape[1]
    hid = params["proj_weight"].shape[0]
    cols = inner // mp
    rows = clouds * SLOT
    smem, vmem = pl.BlockSpec(memory_space=pltpu.SMEM), pl.BlockSpec(memory_space=pltpu.VMEM)
    anywhere = pl.BlockSpec(memory_space=pl.ANY)
    inputs = {"counts_all": (counts, smem), "feats_all": (feats, anywhere), "top_all": (cotangent, anywhere)}
    inputs["points_all"] = (points, anywhere)
    scratch = layer_scratch(mp, clouds, width, inner, hid)
    scratch["points"] = (points.shape, f32)
    for name in PIECES:
        for kind in SHAPES:
            array = params[name + "_" + kind]
            inputs[name + "_" + kind + "_all"] = (array, anywhere)
            scratch[name + "_" + kind] = (array.shape, f32)
    outs = dict(
        block_out=((clouds * PAD, width), bf16),
        feats_grad=((clouds * PAD, width), f32),
        own_grad=((48, 512 + 2 * cols), f32),
        small_out=((512, 128), f32),
        sums=((16, 128), f32),
    )
    scratch.update(
        stage_top=((clouds * PAD, width), f32),
        block_low=((clouds * PAD, width), bf16),
        old_rows=((1, 128), f32),
        turned_top=((width, rows), bf16),
        turned_one=((width, rows), bf16),
        turned_two=((width, rows), bf16),
        turned_mid=((width, rows), bf16),
        feats=((clouds * PAD, width), bf16),
        cotangent=((clouds * PAD, width), bf16),
        proj_low=((hid, width), bf16),
        pos_hidden=((8, hid), f32),
        w=((mp, 4, 2, 48, 512 + 2 * cols), bf16),
        up_bias=((mp, 8, cols), f32),
        up_bias_grad=((mp, 8, cols), f32),
        vec_grad=((8, width), f32),
        pos_grad=((8, hid), f32),
        proj_grad=((hid, width), f32),
        small=((512, 128), f32),
        plane_out=((8, 64, 128), bf16),
        plane_in=((8, 64, 128), bf16),
        line_out=((4, 16, 128), bf16),
        line_in=((4, 16, 128), bf16),
        whole=((8, 4, 16, 128), bf16),
        slots_a=((32, 1, 128), f32),
        slots_b=((32, 1, 128), f32),
    )
    for tag, n in (("down__", cols), ("up__", cols), ("qk__", 256), ("vo__", 256)):
        scratch.update(scatter_scratch(tag, n))
    sems = dict(send_sem=SENDS, recv_sem=ARRIVALS, load_sem=27, store_sem=2)
    names = list(inputs) + list(outs) + list(scratch) + list(sems)
    return pl.pallas_call(
        functools.partial(main_kernel, names, mp, clouds, width, inner),
        out_shape=[jax.ShapeDtypeStruct(*v) for v in outs.values()],
        in_specs=[v[1] for v in inputs.values()],
        out_specs=[anywhere, anywhere, vmem, vmem, vmem],
        scratch_shapes=[pltpu.VMEM(*v) for v in scratch.values()]
        + [pltpu.SemaphoreType.DMA((n,)) for n in sems.values()],
        compiler_params=pltpu.CompilerParams(
            vmem_limit_bytes=60 * 1024 * 1024, collective_id=0, has_side_effects=True
        ),
    )(*[v[0] for v in inputs.values()])


def update_kernel(names, *args):
    refs = dict(zip(names, args))
    copies = [
        pltpu.make_async_copy(refs["block_in"], refs["block_out"], refs["sem"].at[0]),
        pltpu.make_async_copy(refs["feats_in"], refs["feats_out"], refs["sem"].at[1]),
    ]
    for copy in copies:
        copy.start()
    mp = lax.axis_index("mp")
    sums = refs["sums"][...]
    clip = jnp.sqrt(sums[0:1])
    factor = jnp.minimum(1.0, clip_max / (clip + 1e-06))[0:1, 0:1]
    refs["clip_out"][...] = clip
    grads = own_parts(refs["own"], refs["small"], mp)
    order, squares, steps = 0, [], []
    for name in PIECES:
        weights = load(refs, "weight", name)
        parts = [
            adam(g, factor, m, s, p)
            for g, m, s, p in zip(grads[name], load(refs, "moment", name), load(refs, "second", name), weights)
        ]
        if order < 5:
            pair = [(sums[1 + order : 2 + order, 0:1], sums[8 + order : 9 + order, 0:1])]
        else:
            kept = 1 if name == "vector" else None
            pair = []
            for a in (weights[0], parts[0][3]):
                total = jnp.sum(a * a, axis=1, keepdims=True)
                pair.append(total if kept else jnp.sum(total, axis=0, keepdims=True))
            pair = [tuple(pair)]
        order += 1
        old, way = jnp.sqrt(pair[0][0]), jnp.sqrt(pair[0][1])
        squares.append((old, way))
        ratio = old / (way + 1e-06)
        for i, (weight, part) in enumerate(zip(weights, parts)):
            new = weight - learn_rate * ratio * part[3]
            stored = {"grad": part[0], "new": new, "m": part[1], "s": part[2], "copy": new.astype(bf16)}
            for kind, value in stored.items():
                ref = refs[name + "_out_" + kind]
                if name == "qkv":
                    ref[i] = value
                else:
                    ref[...] = value.reshape(ref.shape)
    place = lax.broadcasted_iota(jnp.int32, (8, 128), 0)
    lane = lax.broadcasted_iota(jnp.int32, (8, 128), 1)
    trust = jnp.zeros((8, 128), f32)
    for side in range(2):
        column = 0
        for pair in squares:
            for r in range(pair[side].shape[0]):
                value = jnp.broadcast_to(pair[side][r : r + 1, :], (8, 128))
                trust = jnp.where((place == side) & (lane == column), value, trust)
                column += 1
    refs["trust_out"][...] = trust[0:2, 0:14]
    for copy in copies:
        copy.wait()


OUT_KINDS = (("grad", f32), ("new", f32), ("m", f32), ("s", f32), ("copy", bf16))


def update_call(block, feats, own, small, sums, params):
    vmem = pl.BlockSpec(memory_space=pltpu.VMEM)
    anywhere = pl.BlockSpec(memory_space=pl.ANY)
    inputs = {"block_in": (block, vmem), "feats_in": (feats, vmem)}
    inputs.update(own=(own, vmem), small=(small, vmem), sums=(sums, vmem))
    for name in PIECES:
        for kind in SHAPES:
            inputs[name + "_" + kind] = (params[name + "_" + kind], vmem)
    outs = {"block_out": (block.shape, bf16, anywhere), "feats_out": (feats.shape, f32, anywhere)}
    outs["clip_out"] = ((1, 128), f32, vmem)
    outs["trust_out"] = ((2, 14), f32, vmem)
    for name in PIECES:
        for kind, dtype in OUT_KINDS:
            outs[name + "_out_" + kind] = (params[name + "_weight"].shape, dtype, vmem)
    names = list(inputs) + list(outs) + ["sem"]
    result = pl.pallas_call(
        functools.partial(update_kernel, names),
        out_shape=[jax.ShapeDtypeStruct(*v[:2]) for v in outs.values()],
        in_specs=[v[1] for v in inputs.values()],
        out_specs=[v[2] for v in outs.values()],
        scratch_shapes=[pltpu.SemaphoreType.DMA((2,))],
        compiler_params=pltpu.CompilerParams(vmem_limit_bytes=60 * 1024 * 1024),
    )(*[v[0] for v in inputs.values()])
    return dict(zip(outs, result))


def close_shards(*arrays):
    feats, centres, counts, cotangent = arrays[:4]
    mp_count = lax.axis_size("mp")
    mp_index = lax.axis_index("mp")
    share = feats.shape[0] // mp_count
    clouds = share // PAD
    inner = arrays[6].shape[1] * mp_count
    params = {}
    for k, kind in enumerate(SHAPES):
        for i, name in enumerate(PIECES):
            array = arrays[4 + 8 * k + i]
            if name in ("out", "down"):
                array = array.T
            params[name + "_" + kind] = array
    mine = lax.dynamic_slice_in_dim(centres, mp_index * share, share, 1).T.reshape(clouds, PAD, 3)
    points = jnp.pad(mine, ((0, 0), (0, SLOT - PAD), (0, 0)))
    points = jnp.concatenate((points, jnp.ones((clouds, SLOT, 1), f32)), axis=2)
    points = jnp.pad(points.reshape(clouds * SLOT, 4), ((0, 0), (0, 4)))
    block, grad, own, small, sums = main_call(mp_count, inner, counts, feats, cotangent, points, params)
    out = update_call(block, grad, own, small, sums, params)
    outputs = [out["block_out"], out["feats_out"], out["clip_out"][0, 0], out["trust_out"]]
    for name in PIECES:
        for kind, _ in OUT_KINDS:
            array = out[name + "_out_" + kind]
            if name in ("out", "down"):
                array = array.T
            outputs.append(array)
    return tuple(outputs)


def solution(mesh):
    qkv, outw, upw, bias, whole = P(None, "dp", "mp"), P("mp", "dp"), P("dp", "mp"), P("mp"), P()
    params = (qkv, outw, upw, bias, outw, whole, whole, whole)
    in_specs = (P("dp", None), P(None, "dp"), P("dp"), P("dp", None)) + params * 3
    rows = P(("dp", "mp"), None)
    out_specs = (rows, rows, P(), P()) + tuple(spec for spec in params for _ in range(5))
    form = close_shards if (mesh.shape["dp"], mesh.shape["mp"]) == (8, 4) else shards
    return jax.shard_map(form, mesh=mesh, in_specs=in_specs, out_specs=out_specs, check_vma=False)
```

```python
import functools
import math

import jax
import jax.numpy as jnp
from jax import lax
from jax.experimental import pallas as pl
from jax.experimental.pallas import tpu as pltpu
from jax.sharding import PartitionSpec as P

HD = 64
PAD = 38
SLOT = 40
GROUP = 4

norm_eps = 1e-05
beta_one = 0.5
beta_two = 0.5
adam_eps = 1e-06
decay_rate = 0.01
learn_rate = 0.3
clip_max = 1.0
step_count = 3.0
neg_fill = -1e30
highest = lax.Precision.HIGHEST
f32 = jnp.float32
bf16 = jnp.bfloat16

NN = (((1,), (0,)), ((), ()))
NT = (((1,), (1,)), ((), ()))
TN = (((0,), (0,)), ((), ()))


def dot(a, b, dims=NN, precision=None):
    return lax.dot_general(a, b, dims, precision=precision, preferred_element_type=f32)


def gelu_pair(v):
    cdf = 0.5 * (1.0 + lax.erf(v * 0.7071067811865476))
    return v * cdf, cdf + v * jnp.exp(-0.5 * v * v) * 0.3989422804014327


def piece_squares(array, tensor_index):
    if tensor_index == 5:
        return jnp.sum(array * array, axis=1)
    return jnp.sum(array * array)[None]


def piece_ratio(trust_ratio, tensor_index):
    if tensor_index < 5:
        return trust_ratio[tensor_index]
    if tensor_index == 5:
        return trust_ratio[5:12][:, None]
    return trust_ratio[tensor_index + 6]


def side_by_side(take, parts):
    return jnp.concatenate([take(j) for j in parts], axis=1)


class Layer:
    def __init__(self, refs, mp, clouds, width, inner):
        self.__dict__.update(refs)
        self.mp = mp
        self.clouds = clouds
        self.width = width
        self.inner = inner
        self.rows = clouds * SLOT
        self.block = GROUP * SLOT
        self.blocks = clouds // GROUP
        self.hid = self.proj_low.shape[0]

    def live(self, j):
        return [h for h in range(2) if (2 * j + h) % 2 == 0 or j < self.mp // 2]

    def spread_rows(self):
        zeros = jnp.zeros((SLOT - PAD, self.width), f32)
        self.stage[...] = self.feats[...].astype(f32)
        for c in range(self.clouds):
            self.stream[pl.ds(SLOT * c, PAD), :] = self.stage[pl.ds(PAD * c, PAD), :]
            self.stream[pl.ds(SLOT * c + PAD, SLOT - PAD), :] = zeros
        self.stage[...] = self.cotangent[...].astype(f32)
        for c in range(self.clouds):
            self.middle_grad[pl.ds(SLOT * c, PAD), :] = self.stage[pl.ds(PAD * c, PAD), :]
            self.middle_grad[pl.ds(SLOT * c + PAD, SLOT - PAD), :] = zeros

    def keep_block(self, b, shape, dim):
        place = lax.broadcasted_iota(jnp.int32, shape, dim)
        bound = jnp.zeros(shape, jnp.int32)
        for i in range(GROUP):
            limit = self.counts[b * GROUP + i] + SLOT * i
            inside = (place >= SLOT * i) & (place < limit)
            bound = jnp.where(inside, 1, bound)
        return bound > 0

    def masks(self):
        n = self.block

        def step(b, carry):
            keys = lax.broadcasted_iota(jnp.int32, (n, n), 0)
            query = lax.broadcasted_iota(jnp.int32, (n, n), 1)
            fill = jnp.full((n, n), neg_fill, f32)
            for i in range(GROUP):
                limit = self.counts[b * GROUP + i] + SLOT * i
                inside = (keys >= SLOT * i) & (keys < limit)
                mine = (query >= SLOT * i) & (query < SLOT * (i + 1))
                fill = jnp.where(inside & mine, 0.0, fill)
            self.mask[b] = fill
            self.keep[pl.ds(b * n, n), :] = jnp.where(self.keep_block(b, (n, 128), 0), 1.0, 0.0)
            return carry

        lax.fori_loop(0, self.blocks, step, 0)

    def norm(self, x):
        centre = x - jnp.mean(x, axis=-1, keepdims=True)
        spread = jnp.mean(centre * centre, axis=-1, keepdims=True)
        rate = lax.rsqrt(spread + norm_eps)
        return centre * rate, rate

    def norm_back(self, grad, hat, rate, gain):
        scaled = grad * gain
        first = jnp.mean(scaled, axis=-1, keepdims=True)
        second = jnp.mean(scaled * hat, axis=-1, keepdims=True)
        return rate * (scaled - first - hat * second)

    def entry(self):
        value, slope = gelu_pair(dot(self.points[...], self.pos_hidden[...], NN, highest))
        hidden = value.astype(bf16)
        self.pos_slope[...] = slope
        self.hidden[...] = hidden
        x = self.stream[...] + (dot(hidden, self.proj_low[...]) + self.vec[6:7, :])
        hat, rate = self.norm(x)
        self.stream[...] = x
        self.hat_one[...] = hat
        self.rate_one[...] = jnp.broadcast_to(rate, (self.rows, 128))
        self.normed_one[...] = (hat * self.vec[0:1, :] + self.vec[2:3, :]).astype(bf16)

    def project(self):
        for j in range(0, self.mp, 2):
            both = dot(self.normed_one[...], side_by_side(self.w_qkv, (j, j + 1))).astype(bf16)
            self.qkv[j], self.qkv[j + 1] = both[:, :384], both[:, 384:]

    def lanes(self, h, n):
        lane = lax.broadcasted_iota(jnp.int32, (n, 128), 1)
        return (lane < HD) if h == 0 else (lane >= HD)

    def heads(self, rows):
        for j in range(self.mp):
            query = self.qkv[j, rows, 0:128] * jnp.asarray(1.0 / math.sqrt(HD), bf16)
            for h in self.live(j):
                own = self.lanes(h, self.block)
                alone = jnp.where(own, query, jnp.zeros_like(query))
                yield j, own, alone, self.qkv[j, rows, 128:256], self.qkv[j, rows, 256:384]

    def attend(self, start, stop):
        n = self.block

        def step(b, carry):
            rows = pl.ds(pl.multiple_of(b * n, n), n)
            mask = self.mask[b]
            live = list(self.heads(rows))
            scores = [dot(keys, query, NT) + mask for _, _, query, keys, _ in live]
            low = []
            for i, score in enumerate(scores):
                expo = jnp.exp(score - jnp.max(score, axis=0, keepdims=True))
                probs = expo * (1.0 / jnp.sum(expo, axis=0, keepdims=True))
                self.probs[i, b] = probs
                low.append(probs.astype(bf16))
            mixed = [jnp.zeros((n, 128), f32)] * self.mp
            for probs, (j, own, _, _, values) in zip(low, live):
                mixed[j] = jnp.where(own, dot(probs, values, TN), mixed[j])
            for j in range(self.mp):
                self.attn_low[j, rows, :] = mixed[j].astype(bf16)
            return carry

        lax.fori_loop(start, stop, step, 0, unroll=2)

    def middle(self):
        parts = range(self.mp)
        mixed = side_by_side(lambda j: self.attn_low[j], parts)
        x = self.stream[...] + self.vec[4:5, :] + dot(mixed, side_by_side(self.w_out, parts), NT)
        hat, rate = self.norm(x)
        self.stream[...] = x
        self.hat_two[...] = hat
        self.rate_two[...] = jnp.broadcast_to(rate, (self.rows, 128))
        self.normed_two[...] = (hat * self.vec[1:2, :] + self.vec[3:4, :]).astype(bf16)

    def feed(self):
        total = self.stream[...]
        for j in range(0, self.mp, 2):
            pair = (j, j + 1)
            bias = side_by_side(lambda i: self.up_bias[i, 0:1, :], pair)
            value, slope = gelu_pair(dot(self.normed_two[...], side_by_side(self.w_up, pair)) + bias)
            low = value.astype(bf16)
            half = low.shape[1] // 2
            for k, i in enumerate(pair):
                self.activated[i] = low[:, k * half : (k + 1) * half]
                self.slope[i] = slope[:, k * half : (k + 1) * half]
            total = total + dot(low, side_by_side(self.w_down, pair), NT)
        self.stream[...] = total

    def top(self):
        keep = jnp.concatenate([self.keep[...]] * (self.width // 128), axis=1)
        self.stream[...] = (self.stream[...] + self.vec[5:6, :]) * keep

    def grad_start(self):
        self.vec_grad[...] = jnp.zeros_like(self.vec_grad)
        keep = jnp.concatenate([self.keep[...]] * (self.width // 128), axis=1)
        grad = self.middle_grad[...] * keep
        self.middle_grad[...] = grad
        self.grad_top[...] = grad.astype(bf16)
        self.vec_grad[5:6, :] = jnp.sum(grad, axis=0, keepdims=True)

    def feed_back(self):
        total = None
        for j in range(0, self.mp, 2):
            pair = (j, j + 1)
            grad = dot(self.grad_top[...], side_by_side(self.w_down, pair))
            low = (grad * side_by_side(lambda i: self.slope[i], pair)).astype(bf16)
            bias = jnp.sum(low.astype(f32), axis=0, keepdims=True)
            half = low.shape[1] // 2
            for k, i in enumerate(pair):
                self.grad_pre[i] = low[:, k * half : (k + 1) * half]
                self.up_bias_grad[i, 0:1, :] = bias[:, k * half : (k + 1) * half]
            term = dot(low, side_by_side(self.w_up, pair), NT)
            total = term if j == 0 else total + term
        self.normed_grad[...] = total

    def middle_back(self):
        grad, hat = self.normed_grad[...], self.hat_two[...]
        rate = jnp.concatenate([self.rate_two[...]] * (self.width // 128), axis=1)
        self.vec_grad[1:2, :] = jnp.sum(grad * hat, axis=0, keepdims=True)
        self.vec_grad[3:4, :] = jnp.sum(grad, axis=0, keepdims=True)
        out = self.middle_grad[...] + self.norm_back(grad, hat, rate, self.vec[1:2, :])
        self.middle_grad[...] = out
        self.vec_grad[4:5, :] = jnp.sum(out, axis=0, keepdims=True)
        low = out.astype(bf16)
        self.middle_low[...] = low
        grads = dot(low, side_by_side(self.w_out, range(self.mp))).astype(bf16)
        for j in range(self.mp):
            self.attn_grad[j] = grads[:, 128 * j : 128 * j + 128]

    def attend_back(self):
        n = self.block
        scale = 1.0 / math.sqrt(HD)

        def step(b, carry):
            rows = pl.ds(pl.multiple_of(b * n, n), n)
            live = list(self.heads(rows))
            mine = []
            for j, own, _, _, _ in live:
                grad = self.attn_grad[j, rows, :]
                mine.append(jnp.where(own, grad, jnp.zeros_like(grad)))
            grad_probs = [dot(values, g, NT) for g, (_, _, _, _, values) in zip(mine, live)]
            scores = []
            grad_values = [jnp.zeros((n, 128), f32)] * self.mp
            for i, (j, _, _, _, _) in enumerate(live):
                probs = self.probs[i, b]
                grad_values[j] = grad_values[j] + dot(probs.astype(bf16), mine[i])
                inner = jnp.sum(probs * grad_probs[i], axis=0, keepdims=True)
                scores.append((probs * (grad_probs[i] - inner)).astype(bf16))
            grad_query = [jnp.zeros((n, 128), f32)] * self.mp
            grad_keys = [jnp.zeros((n, 128), f32)] * self.mp
            for grad, (j, own, query, keys, _) in zip(scores, live):
                grad_keys[j] = grad_keys[j] + dot(grad, query)
                grad_query[j] = jnp.where(own, dot(grad, keys, TN), grad_query[j])
            for j in range(self.mp):
                self.grad_proj[j, rows, 0:128] = (grad_query[j] * scale).astype(bf16)
                self.grad_proj[j, rows, 128:256] = grad_keys[j].astype(bf16)
                self.grad_proj[j, rows, 256:384] = grad_values[j].astype(bf16)
            return carry

        lax.fori_loop(0, self.blocks, step, 0, unroll=2)

    def entry_back(self):
        grad = None
        for j in range(0, self.mp, 2):
            pair = (j, j + 1)
            term = dot(side_by_side(lambda i: self.grad_proj[i], pair), side_by_side(self.w_qkv, pair), NT)
            grad = term if j == 0 else grad + term
        hat = self.hat_one[...]
        rate = jnp.concatenate([self.rate_one[...]] * (self.width // 128), axis=1)
        self.vec_grad[0:1, :] = jnp.sum(grad * hat, axis=0, keepdims=True)
        self.vec_grad[2:3, :] = jnp.sum(grad, axis=0, keepdims=True)
        out = self.middle_grad[...] + self.norm_back(grad, hat, rate, self.vec[0:1, :])
        self.middle_grad[...] = out
        self.vec_grad[6:7, :] = jnp.sum(out, axis=0, keepdims=True)
        low = out.astype(bf16)
        self.pos_low[...] = low
        self.pre_grad[...] = dot(low, self.proj_low[...], NT) * self.pos_slope[...]

    def turn(self, source, target):
        for i in range(self.rows // 128):
            target[:, 128 * i : 128 * i + 128] = source[128 * i : 128 * i + 128, :].T

    def gather_rows(self, source, target):
        for c in range(self.clouds):
            target[pl.ds(PAD * c, PAD), :] = source[pl.ds(SLOT * c, PAD), :]


def layer_scratch(mp, clouds, width, inner, hid):
    rows = clouds * SLOT
    block = GROUP * SLOT
    cols = inner // mp
    heads = mp + mp // 2
    shapes = dict(
        stage=((clouds * PAD, width), f32),
        stream=((rows, width), f32),
        middle_grad=((rows, width), f32),
        mask=((clouds // GROUP, block, block), f32),
        keep=((rows, 128), f32),
        pos_slope=((rows, hid), f32),
        hidden=((rows, hid), bf16),
        hat_one=((rows, width), f32),
        rate_one=((rows, 128), f32),
        normed_one=((rows, width), bf16),
        qkv=((mp, rows, 384), bf16),
        probs=((heads, clouds // GROUP, block, block), f32),
        attn_low=((mp, rows, 128), bf16),
        hat_two=((rows, width), f32),
        rate_two=((rows, 128), f32),
        normed_two=((rows, width), bf16),
        activated=((mp, rows, cols), bf16),
        slope=((mp, rows, cols), f32),
        grad_top=((rows, width), bf16),
        grad_pre=((mp, rows, cols), bf16),
        normed_grad=((rows, width), f32),
        middle_low=((rows, width), bf16),
        attn_grad=((mp, rows, 128), bf16),
        grad_proj=((mp, rows, 384), bf16),
        pos_low=((rows, width), bf16),
        pre_grad=((rows, hid), f32),
        turned=((width, rows), bf16),
    )
    return shapes


def compute_kernel(names, mp, clouds, width, inner, *args):
    refs = dict(zip(names, args))
    layer = Layer(refs, mp, clouds, width, inner)
    w = layer.w
    cols = inner // mp
    layer.w_qkv = lambda j: w[j, :, 0:384]
    layer.w_out = lambda j: w[j, :, 384:512]
    layer.w_up = lambda j: w[j, :, 512 : 512 + cols]
    layer.w_down = lambda j: w[j, :, 512 + cols : 512 + 2 * cols]
    layer.proj_low[...] = layer.pos_proj[...].astype(bf16)
    layer.spread_rows()
    layer.masks()
    layer.entry()
    layer.project()
    layer.attend(0, layer.blocks)
    layer.middle()
    layer.feed()
    layer.top()
    layer.gather_rows(layer.stream, layer.stage)
    layer.block_out[...] = layer.stage[...].astype(bf16)
    layer.grad_start()
    layer.feed_back()
    g = layer.grads
    layer.turn(layer.grad_top, layer.turned)
    for j in range(mp):
        g[j, :, 512 + cols : 512 + 2 * cols] = dot(layer.turned[...], layer.activated[j])
    layer.turn(layer.normed_two, layer.turned)
    for j in range(mp):
        g[j, :, 512 : 512 + cols] = dot(layer.turned[...], layer.grad_pre[j])
    layer.middle_back()
    layer.turn(layer.middle_low, layer.turned)
    for j in range(mp):
        g[j, :, 384:512] = dot(layer.turned[...], layer.attn_low[j])
    layer.attend_back()
    layer.turn(layer.normed_one, layer.turned)
    for j in range(mp):
        g[j, :, 0:384] = dot(layer.turned[...], layer.grad_proj[j])
    layer.entry_back()
    layer.gather_rows(layer.middle_grad, layer.feats_grad)
    layer.proj_grad[...] = dot(layer.hidden[...], layer.pos_low[...], TN)
    layer.pos_grad[...] = dot(layer.points[...], layer.pre_grad[...], TN, highest)


def compute(mp, width, inner, counts, feats, cotangent, points, w, up_bias, vec, pos_hidden, pos_proj):
    clouds = counts.shape[0]
    hid = pos_proj.shape[0]
    inputs = ["counts", "feats", "cotangent", "points", "w", "up_bias", "vec", "pos_hidden", "pos_proj"]
    outs = dict(
        block_out=((clouds * PAD, width), bf16),
        feats_grad=((clouds * PAD, width), f32),
        grads=(w.shape, f32),
        up_bias_grad=((mp, 8, inner // mp), f32),
        vec_grad=((8, width), f32),
        pos_grad=((8, hid), f32),
        proj_grad=((hid, width), f32),
    )
    scratch = layer_scratch(mp, clouds, width, inner, hid)
    scratch["proj_low"] = ((hid, width), bf16)
    names = inputs + list(outs) + list(scratch)
    vmem = pl.BlockSpec(memory_space=pltpu.VMEM)
    return pl.pallas_call(
        functools.partial(compute_kernel, names, mp, clouds, width, inner),
        out_shape=[jax.ShapeDtypeStruct(*v) for v in outs.values()],
        in_specs=[pl.BlockSpec(memory_space=pltpu.SMEM)] + [vmem] * (len(inputs) - 1),
        out_specs=[vmem] * len(outs),
        scratch_shapes=[pltpu.VMEM(*v) for v in scratch.values()],
        compiler_params=pltpu.CompilerParams(vmem_limit_bytes=60 * 1024 * 1024),
    )(counts, feats, cotangent, points, w, up_bias, vec, pos_hidden, pos_proj)


def shards(
    feats,
    centres,
    counts,
    cotangent,
    qkv_weight,
    out_weight,
    up_weight,
    up_bias,
    down_weight,
    norm_vectors,
    pos_hidden,
    pos_proj,
    qkv_moment,
    out_moment,
    up_moment,
    bias_moment,
    down_moment,
    vector_moment,
    hidden_moment,
    proj_moment,
    qkv_second,
    out_second,
    up_second,
    bias_second,
    down_second,
    vector_second,
    hidden_second,
    proj_second,
):
    mp_count = lax.axis_size("mp")
    mp_index = lax.axis_index("mp")
    dp_index = lax.axis_index("dp")
    share = feats.shape[0] // mp_count
    clouds = share // PAD
    width = feats.shape[1]
    cols = up_weight.shape[1]
    inner = cols * mp_count
    start = mp_index * share
    my_feats = lax.dynamic_slice_in_dim(feats, start, share, 0)
    my_top = lax.dynamic_slice_in_dim(cotangent, start, share, 0)
    my_counts = lax.dynamic_slice_in_dim(counts, mp_index * clouds, clouds, 0)
    my_points = lax.dynamic_slice_in_dim(centres, start, share, 1).T.reshape(clouds, PAD, 3)
    points = jnp.pad(my_points, ((0, 0), (0, SLOT - PAD), (0, 0)))
    points = jnp.concatenate((points, jnp.ones((clouds, SLOT, 1), f32)), axis=2)
    points = jnp.pad(points.reshape(clouds * SLOT, 4), ((0, 0), (0, 4)))
    packed = jnp.concatenate(
        (qkv_weight[0], qkv_weight[1], qkv_weight[2], out_weight.T, up_weight, down_weight.T), axis=1
    ).astype(bf16)
    whole = lax.all_gather(packed, "dp", axis=0, tiled=True)
    whole = lax.all_gather(whole, "mp", axis=0)
    bias = lax.all_gather(jnp.broadcast_to(up_bias[None], (8, cols)), "mp", axis=0)
    vec = jnp.pad(norm_vectors, ((0, 1), (0, 0)))
    hidden = jnp.pad(pos_hidden, ((0, 4), (0, 0)))
    block_out, feats_grad, grads, bias_grad, vec_grad, pos_grad, proj_grad = compute(
        mp_count, width, inner, my_counts, my_feats, my_top, points, whole, bias, vec, hidden, pos_proj
    )
    own = lax.psum_scatter(grads, "mp", scatter_dimension=0, tiled=True)[0]
    own = lax.psum_scatter(own, "dp", scatter_dimension=0, tiled=True)
    bias_grad, vector_grad, pos_grad, proj_grad = lax.psum(
        (bias_grad[:, 0], vec_grad[:7], pos_grad[:4], proj_grad), ("dp", "mp")
    )
    bias_grad = lax.dynamic_index_in_dim(bias_grad, mp_index, 0, keepdims=False)
    qkv_grad = jnp.stack((own[:, 0:128], own[:, 128:256], own[:, 256:384]))
    out_grad = own[:, 384:512].T
    up_grad = own[:, 512 : 512 + cols]
    down_grad = own[:, 512 + cols :].T
    leader = ((dp_index == 0) & (mp_index == 0)).astype(f32)
    first_dp = (dp_index == 0).astype(f32)
    owners = [1.0, 1.0, 1.0, first_dp, 1.0, leader, leader, leader]
    weights = [qkv_weight, out_weight, up_weight, up_bias, down_weight, norm_vectors, pos_hidden, pos_proj]
    moments = [
        qkv_moment,
        out_moment,
        up_moment,
        bias_moment,
        down_moment,
        vector_moment,
        hidden_moment,
        proj_moment,
    ]
    seconds = [
        qkv_second,
        out_second,
        up_second,
        bias_second,
        down_second,
        vector_second,
        hidden_second,
        proj_second,
    ]
    grads = [qkv_grad, out_grad, up_grad, bias_grad, down_grad, vector_grad, pos_grad, proj_grad]
    grad_square = jnp.zeros((), f32)
    weight_square = []
    for i in range(8):
        grad_square = grad_square + owners[i] * jnp.sum(grads[i] * grads[i])
        weight_square.append(owners[i] * piece_squares(weights[i], i))
    totals = lax.psum(jnp.concatenate([grad_square[None]] + weight_square), ("dp", "mp"))
    clip_norm = jnp.sqrt(totals[0])
    factor = jnp.minimum(1.0, clip_max / (clip_norm + 1e-06))
    clipped_list, moment_list, second_list, direction_list, update_square = [], [], [], [], []
    for i in range(8):
        clipped = grads[i] * factor
        moment_new = beta_one * moments[i] + (1.0 - beta_one) * clipped
        second_new = beta_two * seconds[i] + (1.0 - beta_two) * clipped * clipped
        direction = (
            moment_new
            / (1.0 - beta_one**step_count)
            / (jnp.sqrt(second_new / (1.0 - beta_two**step_count)) + adam_eps)
            + decay_rate * weights[i]
        )
        clipped_list.append(clipped)
        moment_list.append(moment_new)
        second_list.append(second_new)
        direction_list.append(direction)
        update_square.append(owners[i] * piece_squares(direction, i))
    update_total = lax.psum(jnp.concatenate(update_square), ("dp", "mp"))
    weight_norm = jnp.sqrt(totals[1:])
    update_norm = jnp.sqrt(update_total)
    trust_ratio = weight_norm / (update_norm + 1e-06)
    outputs = [block_out, feats_grad, clip_norm, jnp.stack((weight_norm, update_norm))]
    for i in range(8):
        new_weight = weights[i] - learn_rate * piece_ratio(trust_ratio, i) * direction_list[i]
        outputs.append(clipped_list[i])
        outputs.append(new_weight)
        outputs.append(moment_list[i])
        outputs.append(second_list[i])
        outputs.append(new_weight.astype(bf16))
    return tuple(outputs)


class Links:
    def __init__(self, send, recv):
        dp, mp = lax.axis_index("dp"), lax.axis_index("mp")
        self.z, self.y = dp // 2, lax.rem(dp, 2)
        self.x, self.c = mp // 2, lax.rem(mp, 2)
        self.mp = mp
        self.plane = self.y * 4 + mp
        self.me = dp * 4 + mp
        self.line = [self.z, self.z + 1 - 2 * lax.rem(self.z, 2), lax.rem(self.z + 2, 4), 3 - self.z]
        self.send_sem, self.recv_sem = send, recv
        self.counts = [0, 0]
        self.sent = []

    def at(self, z, y, x, c):
        return (z * 2 + y, x * 2 + c)

    def core(self):
        return self.at(self.z, self.y, self.x, 1 - self.c)

    def side(self):
        return self.at(self.z, self.y, 1 - self.x, self.c)

    def deep(self):
        return self.at(self.z, 1 - self.y, self.x, self.c)

    def far(self, k):
        return self.at(self.line[k], self.y, self.x, self.c)

    def round(self, k):
        other = lax.rem(self.plane + k, 8)
        return (self.z * 2 + other // 4, lax.rem(other, 4))

    def any(self, k):
        other = lax.rem(self.me + k, 32)
        return (other // 4, lax.rem(other, 4))

    def peers(self):
        return [self.far(k) for k in range(1, 4)] + [self.round(k) for k in range(1, 8)]

    def greet(self, everyone=False):
        barrier = pltpu.get_barrier_semaphore()
        for who in [self.any(k) for k in range(1, 32)] if everyone else self.peers():
            pl.semaphore_signal(barrier, inc=1, device_id=who, device_id_type=pl.DeviceIdType.MESH)

    def met(self, count):
        pl.semaphore_wait(pltpu.get_barrier_semaphore(), count)

    def copy(self, source, target, i):
        return pltpu.make_async_remote_copy(
            src_ref=source,
            dst_ref=target,
            send_sem=self.send_sem.at[i] if i < self.send_sem.shape[0] else self.send_sem.at[0],
            recv_sem=self.recv_sem.at[i] if i < self.recv_sem.shape[0] else self.recv_sem.at[0],
            device_id=self.core(),
            device_id_type=pl.DeviceIdType.MESH,
        )

    def mark(self, side):
        self.counts[side] += 1
        return self.counts[side] - 1

    def send(self, source, target, who, out=None, into=None):
        into = self.mark(1) if into is None else into
        copy = pltpu.make_async_remote_copy(
            src_ref=source,
            dst_ref=target,
            send_sem=self.send_sem.at[self.mark(0) if out is None else out],
            recv_sem=self.recv_sem.at[into],
            device_id=who,
            device_id_type=pl.DeviceIdType.MESH,
        )
        copy.start()
        if out is None:
            self.sent.append(copy)
        return into

    def wait(self, i, target):
        self.copy(target, target, i).wait_recv()

    def sent_all(self, out, source):
        self.sent.append(self.copy(source, source, out))

    def finish(self):
        for copy in self.sent:
            copy.wait_send()


class Gather:
    def __init__(self, links, w, lo, hi, flip):
        self.links, self.w, self.lo, self.hi, self.flip = links, w, lo, hi, flip

    def part(self, mp, z, y):
        return self.w.at[mp, z, y, :, self.lo : self.hi]

    def start(self):
        k = self.links
        own = self.part(k.mp, k.z, k.y)
        self.along = [k.send(own, own, k.far(i)) for i in (1, 2, 3)]
        self.out = [k.mark(0) for _ in range(5)]
        self.first = [k.mark(1) for _ in range(4)]
        self.into = [k.mark(1) for _ in range(4)]

    def step(self, i):
        k = self.links
        block = self.part(k.mp, k.line[i], k.y)
        if i:
            k.wait(self.along[i - 1], block)
        near, next_ = (k.side(), k.deep()) if self.flip else (k.deep(), k.side())
        k.send(block, block, near, self.out[0], self.first[i])
        k.send(block, block, k.core(), self.out[1], self.into[0])
        k.send(block, block, next_, self.out[2], self.into[1])

    def regions(self, mp, z):
        k = self.links
        across = mp + 2 - 4 * k.x
        side, deep = self.part(across, z, k.y), self.part(mp, z, 1 - k.y)
        return (side, deep) if self.flip else (deep, side), self.part(across, z, 1 - k.y)

    def hop(self, i):
        k = self.links
        block = self.regions(k.mp, k.line[i])[0][0]
        k.wait(self.first[i], block)
        k.send(block, block, k.deep() if self.flip else k.side(), self.out[3], self.into[2])
        k.send(block, block, k.core(), self.out[4], self.into[3])

    def rest(self):
        k = self.links
        block = self.regions(k.mp, slice(None))[0][1]
        k.wait(self.into[1], block)
        self.rest_twin = k.send(block, block, k.core())

    def corner(self):
        k = self.links
        block = self.regions(k.mp, slice(None))[1]
        k.wait(self.into[2], block)
        self.corner_twin = k.send(block, block, k.core())

    def end(self):
        k = self.links
        twin = k.mp + 1 - 2 * k.c
        near, corner = self.regions(twin, slice(None))
        k.wait(self.into[0], self.part(twin, slice(None), k.y))
        k.wait(self.into[3], near[0])
        k.wait(self.rest_twin, near[1])
        k.wait(self.corner_twin, corner)
        line = self.part(k.mp, slice(None), k.y)
        first = self.regions(k.mp, slice(None))[0][0]
        for out, block in zip(self.out, (line, line, line, first, first)):
            k.sent_all(out, block)


class Scatter:
    def __init__(self, links, refs, flip):
        self.links, self.flip = links, flip
        self.__dict__.update(refs)

    def start(self):
        k = self.links
        self.first = k.send(self.core_out, self.core_in, k.core())

    def pair(self, x, z, y):
        return self.kept[x, z, y] + self.core_in[x, z, y].astype(f32)

    def second(self):
        k = self.links
        k.wait(self.first, self.core_in)
        if self.flip:
            for x in range(2):
                for z in range(4):
                    self.next_out[x, z] = self.pair(x, z, 1 - k.y).astype(bf16)
            self.next = k.send(self.next_out, self.next_in, k.deep())
        else:
            for y in range(2):
                for z in range(4):
                    self.next_out[y, z] = self.pair(1 - k.x, z, y).astype(bf16)
            self.next = k.send(self.next_out, self.next_in, k.side())

    def third(self):
        k = self.links
        k.wait(self.next, self.next_in)
        for z in range(4):
            if self.flip:
                total = self.pair(1 - k.x, z, k.y) + self.next_in[1 - k.x, z].astype(f32)
            else:
                total = self.pair(k.x, z, 1 - k.y) + self.next_in[1 - k.y, z].astype(f32)
            self.last_out[z] = total.astype(bf16)
        self.last = k.send(self.last_out, self.last_in, k.side() if self.flip else k.deep())

    def fourth(self):
        k = self.links
        k.wait(self.last, self.last_in)
        self.along = []
        for i in range(4):
            z = k.line[i]
            mid = self.next_in[k.x, z] if self.flip else self.next_in[k.y, z]
            total = self.pair(k.x, z, k.y) + mid.astype(f32) + self.last_in[z].astype(f32)
            if i == 0:
                self.own[...] = total
            else:
                self.far_out[i - 1] = total.astype(bf16)
                self.along.append(k.send(self.far_out.at[i - 1], self.far_in.at[i - 1], k.far(i)))

    def end(self):
        k = self.links
        total = self.own[...]
        for i in range(3):
            k.wait(self.along[i], self.far_in.at[i])
            total = total + self.far_in[i].astype(f32)
        return total


def scatter_scratch(tag, cols):
    return {
        tag + "kept": ((2, 4, 2, 48, cols), f32),
        tag + "core_out": ((2, 4, 2, 48, cols), bf16),
        tag + "core_in": ((2, 4, 2, 48, cols), bf16),
        tag + "next_out": ((2, 4, 48, cols), bf16),
        tag + "next_in": ((2, 4, 48, cols), bf16),
        tag + "last_out": ((4, 48, cols), bf16),
        tag + "last_in": ((4, 48, cols), bf16),
        tag + "far_out": ((3, 48, cols), bf16),
        tag + "far_in": ((3, 48, cols), bf16),
        tag + "own": ((48, cols), f32),
    }


def stack_rows(rows, height=8):
    place = lax.broadcasted_iota(jnp.int32, (height, 128), 0)
    out = jnp.zeros((height, 128), f32)
    for i, row in enumerate(rows):
        out = jnp.where(place == i, jnp.broadcast_to(row, (height, 128)), out)
    return out


def lane_row(rows, base=None):
    lane = lax.broadcasted_iota(jnp.int32, (1, 128), 1)
    out = jnp.zeros((1, 128), f32) if base is None else base
    for i, row in enumerate(rows):
        out = jnp.where(lane == i, row, out)
    return out


def lane_value(row, i):
    lane = lax.broadcasted_iota(jnp.int32, (1, 128), 1)
    return jnp.sum(jnp.where(lane == i, row, 0.0), axis=1, keepdims=True)


def square_row(array):
    total = jnp.sum(jnp.sum(array * array, axis=0, keepdims=True), axis=1, keepdims=True)
    return jnp.broadcast_to(total, (1, 128))


def adam(grad, factor, moment, second, weight):
    clipped = grad * factor
    moment_new = beta_one * moment + (1.0 - beta_one) * clipped
    second_new = beta_two * second + (1.0 - beta_two) * clipped * clipped
    direction = (
        moment_new
        / (1.0 - beta_one**step_count)
        / (jnp.sqrt(second_new / (1.0 - beta_two**step_count)) + adam_eps)
        + decay_rate * weight
    )
    return clipped, moment_new, second_new, direction


PIECES = ("qkv", "out", "up", "bias", "down", "vector", "hidden", "proj")


def own_parts(own, small, mp):
    cols = (own.shape[1] - 512) // 2

    def wide(row, count):
        return jnp.concatenate([small[row + 8 * i : row + 8 * i + count, :] for i in range(3)], axis=1)

    place = lax.broadcasted_iota(jnp.int32, (8, cols), 0)

    return {
        "qkv": [own[:, 128 * i : 128 * i + 128] for i in range(3)],
        "out": [own[:, 384:512]],
        "up": [own[:, 512 : 512 + cols]],
        "bias": [jnp.sum(jnp.where(place == mp, wide(416, 8), 0.0), axis=0, keepdims=True)],
        "down": [own[:, 512 + cols : 512 + 2 * cols]],
        "vector": [wide(384, 7)],
        "hidden": [small[408:412, :]],
        "proj": [jnp.concatenate([small[128 * i : 128 * i + 128, :] for i in range(3)], axis=1)],
    }


def load(refs, kind, name):
    ref = refs[name + "_" + kind]
    if name == "qkv":
        return [ref[i] for i in range(3)]
    return [ref[...].reshape(1, -1)] if name == "bias" else [ref[...]]


def main_kernel(names, mp, clouds, width, inner, *args):
    refs = dict(zip(names, args))
    layer = Layer(refs, mp, clouds, width, inner)
    cols = inner // mp
    links = Links(layer.send_sem, layer.recv_sem)
    w = layer.w
    links.greet(True)
    share = clouds * PAD
    rows = pl.ds(pl.multiple_of(links.mp * share, 16), share)
    sources = {"feats": layer.feats_all.at[rows, :], "cotangent": layer.top_all.at[rows, :]}
    for kind in SHAPES:
        for name in PIECES:
            sources[name + "_" + kind] = refs[name + "_" + kind + "_all"]
    sources["points"] = layer.points_all
    copies = {
        name: pltpu.make_async_copy(source, refs[name], layer.load_sem.at[i])
        for i, (name, source) in enumerate(sources.items())
    }
    first = [name + "_weight" for name in ("qkv", "out", "up", "down", "bias")]
    early = ["feats", "points", "hidden_weight", "proj_weight", "vector_weight", "cotangent"]
    late = [copy for name, copy in copies.items() if name not in first + early]
    for name in first + early:
        copies[name].start()

    def flat(j, lo, hi):
        return w[j, :, :, :, lo:hi].reshape(width, hi - lo)

    layer.w_qkv = lambda j: flat(j, 0, 384)
    layer.w_out = lambda j: flat(j, 384, 512)
    layer.w_up = lambda j: flat(j, 512, 512 + cols)
    layer.w_down = lambda j: flat(j, 512 + cols, 512 + 2 * cols)
    for name in first:
        copies[name].wait()
    for i in range(3):
        w[links.mp, links.z, links.y, :, 128 * i : 128 * i + 128] = refs["qkv_weight"][i].astype(bf16)
    w[links.mp, links.z, links.y, :, 384:512] = refs["out_weight"][...].astype(bf16)
    w[links.mp, links.z, links.y, :, 512 : 512 + cols] = refs["up_weight"][...].astype(bf16)
    w[links.mp, links.z, links.y, :, 512 + cols : 512 + 2 * cols] = refs["down_weight"][...].astype(bf16)
    layer.up_bias[links.mp] = jnp.broadcast_to(refs["bias_weight"][...].reshape(1, cols), (8, cols))
    links.met(31)
    gathers = [
        Gather(links, w, 0, 256, False),
        Gather(links, w, 256, 512, True),
        Gather(links, w, 512, 512 + cols, False),
        Gather(links, w, 512 + cols, 512 + 2 * cols, True),
    ]
    near, wide = gathers[:2], gathers[2:]

    def each(group, step, *a):
        for g in group:
            getattr(g, step)(*a)

    for group in (near, wide):
        each(group, "start")
        each(group, "step", 0)
    own_bias = layer.up_bias.at[links.mp]
    bias_side = links.send(own_bias, own_bias, links.side())
    bias_core = links.send(own_bias, own_bias, links.core())
    for copy in late:
        copy.start()
    for name in early:
        copies[name].wait()
    layer.proj_low[...] = refs["proj_weight"][...].astype(bf16)
    layer.vec = jnp.concatenate([refs["vector_weight"][...], jnp.zeros((1, width), f32)], axis=0)
    layer.pos_hidden[...] = jnp.concatenate([refs["hidden_weight"][...], jnp.zeros((4, 128), f32)], axis=0)
    layer.counts = _Shifted(layer.counts_all, links.mp * clouds)
    layer.spread_rows()
    each(near, "step", 1)
    layer.entry()
    each(near, "step", 2)
    layer.masks()
    each(near, "step", 3)
    each(near, "hop", 0)
    each(near, "hop", 1)
    layer.grad_start()
    each(near, "hop", 2)
    each(wide, "step", 1)
    layer.turn(layer.grad_top, layer.turned_top)
    each(near, "hop", 3)
    each(wide, "step", 2)
    layer.turn(layer.normed_one, layer.turned_one)
    other_bias = layer.up_bias.at[links.mp + 2 - 4 * links.x]
    links.wait(bias_side, other_bias)
    bias_last = links.send(other_bias, other_bias, links.core())
    lead = (links.z * 2 + links.y == 0).astype(f32)

    def five(parts):
        out = []
        for name in ("qkv", "out", "up", "bias", "down"):
            row = sum(square_row(p) for p in parts[name])
            out.append(row * lead if name == "bias" else row)
        return out

    weights = {name: load(refs, "weight", name) for name in PIECES}
    zero = jnp.zeros((1, 1), f32)
    layer.old_rows[...] = lane_row([jnp.zeros((1, 128), f32)] + five(weights))
    each(near, "rest")
    each(wide, "step", 3)
    each(near, "corner")
    each(wide, "hop", 0)
    each(wide, "hop", 1)
    each(near, "end")
    layer.project()
    each(wide, "hop", 2)
    each(wide, "hop", 3)
    layer.attend(0, layer.blocks // 2)
    each(wide, "rest")
    layer.attend(layer.blocks // 2, layer.blocks)
    each(wide, "corner")
    layer.middle()
    layer.turn(layer.normed_two, layer.turned_two)
    each(wide, "end")
    twin = links.mp + 1 - 2 * links.c
    links.wait(bias_core, layer.up_bias.at[twin])
    links.wait(bias_last, layer.up_bias.at[twin + 2 - 4 * links.x])
    layer.feed()

    def scatter(tag, flip):
        return Scatter(links, {n[len(tag) :]: refs[n] for n in names if n.startswith(tag)}, flip)

    down, up = scatter("down__", True), scatter("up__", False)
    qk, vo = scatter("qk__", False), scatter("vo__", True)

    def weigh(product, *targets):
        for x in range(2):
            pair = product((2 * x, 2 * x + 1))
            kept = jnp.where(links.c == 0, pair[0], pair[1])
            sent = jnp.where(links.c == 0, pair[1], pair[0]).astype(bf16)
            lo = 0
            for target in targets:
                hi = lo + target.kept.shape[-1]
                target.core_out[x] = sent[:, lo:hi].reshape(4, 2, 48, hi - lo)
                target.kept[x] = kept[:, lo:hi].reshape(4, 2, 48, hi - lo)
                lo = hi

    def halves(turned, source, pair):
        both = dot(turned[...], side_by_side(lambda j: source[j], pair))
        half = both.shape[1] // 2
        return both[:, :half], both[:, half:]

    def heads_out(pair):
        heads = halves(layer.turned_one, layer.grad_proj, pair)
        mixed = halves(layer.turned_mid, layer.attn_low, pair)
        return [jnp.concatenate(parts, axis=1) for parts in zip(heads, mixed)]

    weigh(lambda pair: halves(layer.turned_top, layer.activated, pair), down)
    down.start()
    layer.feed_back()
    down.second()
    weigh(lambda pair: halves(layer.turned_two, layer.grad_pre, pair), up)
    up.start()
    layer.middle_back()
    up.second()
    layer.turn(layer.middle_low, layer.turned_mid)
    layer.attend_back()
    layer.top()
    layer.gather_rows(layer.stream, layer.stage_top)
    layer.block_low[...] = layer.stage_top[...].astype(bf16)
    out_copies = [pltpu.make_async_copy(layer.block_low, layer.block_out, layer.store_sem.at[1])]
    out_copies[0].start()
    down.third()
    weigh(heads_out, qk, vo)
    qk.start()
    vo.start()
    up.third()
    qk.second()
    vo.second()
    layer.entry_back()
    layer.proj_grad[...] = dot(layer.hidden[...], layer.pos_low[...], TN)
    layer.pos_grad[...] = dot(layer.points[...], layer.pre_grad[...], TN, highest)
    small = layer.small
    for i in range(3):
        lanes = slice(128 * i, 128 * i + 128)
        small[128 * i : 128 * i + 128, :] = layer.proj_grad[:, lanes]
        small[384 + 8 * i : 392 + 8 * i, :] = layer.vec_grad[:, lanes]
        small[416 + 8 * i : 424 + 8 * i, :] = stack_rows([layer.up_bias_grad[j, 0:1, lanes] for j in range(mp)])
    small[408:416, :] = layer.pos_grad[...]
    small[440:512, :] = jnp.zeros((72, 128), f32)
    layer.plane_out[...] = small[...].astype(bf16).reshape(8, 64, 128)
    layer.plane_in[links.plane] = layer.plane_out[links.plane]
    sums = []
    for k in range(1, 8):
        who = links.round(k)
        block = layer.plane_out.at[lax.rem(links.plane + k, 8)]
        sums.append(links.send(block, layer.plane_in.at[links.plane], who))
    down.fourth()
    layer.gather_rows(layer.middle_grad, layer.stage)
    out_copies.append(pltpu.make_async_copy(layer.stage, layer.feats_grad, layer.store_sem.at[0]))
    out_copies[1].start()
    qk.third()
    vo.third()
    up.fourth()
    for k in range(1, 8):
        links.wait(sums[k - 1], layer.plane_in.at[lax.rem(links.plane + 8 - k, 8)])
    total = layer.plane_in[0].astype(f32)
    for i in range(1, 8):
        total = total + layer.plane_in[i].astype(f32)
    layer.line_out[...] = total.astype(bf16).reshape(4, 16, 128)
    layer.line_in[links.z] = layer.line_out[links.z]
    sums = []
    for k in range(1, 4):
        block = layer.line_out.at[links.line[k]]
        sums.append(links.send(block, layer.line_in.at[links.z], links.far(k)))
    qk.fourth()
    vo.fourth()
    own = layer.own_grad
    own[:, 512 + cols :] = down.end()
    own[:, 512 : 512 + cols] = up.end()
    own[:, 256:512] = vo.end()
    for k in range(1, 4):
        links.wait(sums[k - 1], layer.line_in.at[links.line[k]])
    total = layer.line_in[0].astype(f32)
    for i in range(1, 4):
        total = total + layer.line_in[i].astype(f32)
    layer.whole[links.plane, links.z] = total.astype(bf16)
    sums = []
    for k in range(1, 4):
        block = layer.whole.at[links.plane, links.z]
        sums.append(links.send(block, block, links.far(k)))
    own[:, 0:256] = qk.end()
    out_copies.append(pltpu.make_async_copy(own, layer.own_out, layer.store_sem.at[2]))
    out_copies[2].start()
    def all_start(slots, row):
        slots[31] = row
        out, into = links.mark(0), links.mark(1)
        for k in range(1, 32):
            links.send(slots.at[31], slots.at[k - 1], links.any(k), out, into)
        links.sent_all(out, slots.at[0:31])
        return into

    def all_end(slots, into):
        links.wait(into, slots.at[0:31])
        total = slots[lax.rem(links.me + 31, 32)]
        for i in range(1, 32):
            total = total + slots[lax.rem(links.me + 31 - i + 32, 32)]
        return total

    mark = all_start(layer.slots_a, lane_row([square_row(own[...])], layer.old_rows[...]))
    for k in range(1, 4):
        links.wait(sums[k - 1], layer.whole.at[links.plane, links.line[k]])
    sums = []
    for k in range(1, 8):
        block = layer.whole.at[links.plane]
        sums.append(links.send(block, block, links.round(k)))
    for k in range(1, 8):
        links.wait(sums[k - 1], layer.whole.at[lax.rem(links.plane + 8 - k, 8)])
    small[...] = layer.whole[...].astype(f32).reshape(512, 128)
    first = all_end(layer.slots_a, mark)
    out_copies.append(pltpu.make_async_copy(small, layer.small_out, layer.store_sem.at[3]))
    out_copies[3].start()
    total = lane_value(first, 0) + square_row(small[0:440, :])[0:1, 0:1]
    factor = jnp.minimum(1.0, clip_max / (jnp.sqrt(total) + 1e-06))
    for copy in late:
        copy.wait()
    grads = own_parts(own, small, links.mp)
    ways = {}
    for name in ("qkv", "out", "up", "bias", "down"):
        ways[name] = [
            adam(g, factor, m, s, p)[3]
            for g, m, s, p in zip(grads[name], load(refs, "moment", name), load(refs, "second", name), weights[name])
        ]
    mark = all_start(layer.slots_b, lane_row(five(ways)))
    second = all_end(layer.slots_b, mark)
    rows = [total] + [lane_value(first, i) for i in range(1, 6)] + [zero, zero]
    rows += [lane_value(second, i) for i in range(5)]
    layer.sums[...] = stack_rows([jnp.broadcast_to(r, (1, 128)) for r in rows], 16)
    for copy in out_copies:
        copy.wait()
    links.finish()
    assert links.counts == [SENDS, ARRIVALS], links.counts


class _Shifted:
    def __init__(self, ref, start):
        self.ref, self.start = ref, start

    def __getitem__(self, i):
        return self.ref[self.start + i]


SHAPES = ("weight", "moment", "second")
SENDS, ARRIVALS = 89, 101


def main_call(mp, inner, counts, feats, cotangent, points, params):
    clouds = counts.shape[0] // mp
    width = feats.shape[1]
    hid = params["proj_weight"].shape[0]
    cols = inner // mp
    rows = clouds * SLOT
    smem, vmem = pl.BlockSpec(memory_space=pltpu.SMEM), pl.BlockSpec(memory_space=pltpu.VMEM)
    anywhere = pl.BlockSpec(memory_space=pl.ANY)
    inputs = {"counts_all": (counts, smem), "feats_all": (feats, anywhere), "top_all": (cotangent, anywhere)}
    inputs["points_all"] = (points, anywhere)
    scratch = layer_scratch(mp, clouds, width, inner, hid)
    scratch["points"] = (points.shape, f32)
    for name in PIECES:
        for kind in SHAPES:
            array = params[name + "_" + kind]
            inputs[name + "_" + kind + "_all"] = (array, anywhere)
            scratch[name + "_" + kind] = (array.shape, f32)
    outs = dict(
        block_out=((clouds * PAD, width), bf16),
        feats_grad=((clouds * PAD, width), f32),
        own_out=((48, 512 + 2 * cols), f32),
        small_out=((512, 128), f32),
        sums=((16, 128), f32),
    )
    scratch.update(
        stage_top=((clouds * PAD, width), f32),
        block_low=((clouds * PAD, width), bf16),
        old_rows=((1, 128), f32),
        own_grad=((48, 512 + 2 * cols), f32),
        turned_top=((width, rows), bf16),
        turned_one=((width, rows), bf16),
        turned_two=((width, rows), bf16),
        turned_mid=((width, rows), bf16),
        feats=((clouds * PAD, width), bf16),
        cotangent=((clouds * PAD, width), bf16),
        proj_low=((hid, width), bf16),
        pos_hidden=((8, hid), f32),
        w=((mp, 4, 2, 48, 512 + 2 * cols), bf16),
        up_bias=((mp, 8, cols), f32),
        up_bias_grad=((mp, 8, cols), f32),
        vec_grad=((8, width), f32),
        pos_grad=((8, hid), f32),
        proj_grad=((hid, width), f32),
        small=((512, 128), f32),
        plane_out=((8, 64, 128), bf16),
        plane_in=((8, 64, 128), bf16),
        line_out=((4, 16, 128), bf16),
        line_in=((4, 16, 128), bf16),
        whole=((8, 4, 16, 128), bf16),
        slots_a=((32, 1, 128), f32),
        slots_b=((32, 1, 128), f32),
    )
    for tag, n in (("down__", cols), ("up__", cols), ("qk__", 256), ("vo__", 256)):
        scratch.update(scatter_scratch(tag, n))
    sems = dict(send_sem=SENDS, recv_sem=ARRIVALS, load_sem=27, store_sem=4)
    names = list(inputs) + list(outs) + list(scratch) + list(sems)
    return pl.pallas_call(
        functools.partial(main_kernel, names, mp, clouds, width, inner),
        out_shape=[jax.ShapeDtypeStruct(*v) for v in outs.values()],
        in_specs=[v[1] for v in inputs.values()],
        out_specs=[anywhere] * 4 + [vmem],
        scratch_shapes=[pltpu.VMEM(*v) for v in scratch.values()]
        + [pltpu.SemaphoreType.DMA((n,)) for n in sems.values()],
        compiler_params=pltpu.CompilerParams(
            vmem_limit_bytes=60 * 1024 * 1024, collective_id=0, has_side_effects=True
        ),
    )(*[v[0] for v in inputs.values()])


def update_kernel(names, *args):
    refs = dict(zip(names, args))
    copies = [
        pltpu.make_async_copy(refs["block_in"], refs["block_out"], refs["sem"].at[0]),
        pltpu.make_async_copy(refs["feats_in"], refs["feats_out"], refs["sem"].at[1]),
    ]
    for copy in copies:
        copy.start()
    mp = lax.axis_index("mp")
    sums = refs["sums"][...]
    clip = jnp.sqrt(sums[0:1])
    factor = jnp.minimum(1.0, clip_max / (clip + 1e-06))[0:1, 0:1]
    refs["clip_out"][...] = clip
    grads = own_parts(refs["own"], refs["small"], mp)
    order, squares, steps = 0, [], []
    for name in PIECES:
        weights = load(refs, "weight", name)
        parts = [
            adam(g, factor, m, s, p)
            for g, m, s, p in zip(grads[name], load(refs, "moment", name), load(refs, "second", name), weights)
        ]
        if order < 5:
            pair = [(sums[1 + order : 2 + order, 0:1], sums[8 + order : 9 + order, 0:1])]
        else:
            kept = 1 if name == "vector" else None
            pair = []
            for a in (weights[0], parts[0][3]):
                total = jnp.sum(a * a, axis=1, keepdims=True)
                pair.append(total if kept else jnp.sum(total, axis=0, keepdims=True))
            pair = [tuple(pair)]
        order += 1
        old, way = jnp.sqrt(pair[0][0]), jnp.sqrt(pair[0][1])
        squares.append((old, way))
        ratio = old / (way + 1e-06)
        for i, (weight, part) in enumerate(zip(weights, parts)):
            new = weight - learn_rate * ratio * part[3]
            stored = {"grad": part[0], "new": new, "m": part[1], "s": part[2], "copy": new.astype(bf16)}
            for kind, value in stored.items():
                ref = refs[name + "_out_" + kind]
                if name == "qkv":
                    ref[i] = value
                else:
                    ref[...] = value.reshape(ref.shape)
    place = lax.broadcasted_iota(jnp.int32, (8, 128), 0)
    lane = lax.broadcasted_iota(jnp.int32, (8, 128), 1)
    trust = jnp.zeros((8, 128), f32)
    for side in range(2):
        column = 0
        for pair in squares:
            for r in range(pair[side].shape[0]):
                value = jnp.broadcast_to(pair[side][r : r + 1, :], (8, 128))
                trust = jnp.where((place == side) & (lane == column), value, trust)
                column += 1
    refs["trust_out"][...] = trust[0:2, 0:14]
    for copy in copies:
        copy.wait()


OUT_KINDS = (("grad", f32), ("new", f32), ("m", f32), ("s", f32), ("copy", bf16))


def update_call(block, feats, own, small, sums, params):
    vmem = pl.BlockSpec(memory_space=pltpu.VMEM)
    anywhere = pl.BlockSpec(memory_space=pl.ANY)
    inputs = {"block_in": (block, vmem), "feats_in": (feats, vmem)}
    inputs.update(own=(own, vmem), small=(small, vmem), sums=(sums, vmem))
    for name in PIECES:
        for kind in SHAPES:
            inputs[name + "_" + kind] = (params[name + "_" + kind], vmem)
    outs = {"block_out": (block.shape, bf16, anywhere), "feats_out": (feats.shape, f32, anywhere)}
    outs["clip_out"] = ((1, 128), f32, vmem)
    outs["trust_out"] = ((2, 14), f32, vmem)
    for name in PIECES:
        for kind, dtype in OUT_KINDS:
            outs[name + "_out_" + kind] = (params[name + "_weight"].shape, dtype, vmem)
    names = list(inputs) + list(outs) + ["sem"]
    result = pl.pallas_call(
        functools.partial(update_kernel, names),
        out_shape=[jax.ShapeDtypeStruct(*v[:2]) for v in outs.values()],
        in_specs=[v[1] for v in inputs.values()],
        out_specs=[v[2] for v in outs.values()],
        scratch_shapes=[pltpu.SemaphoreType.DMA((2,))],
        compiler_params=pltpu.CompilerParams(vmem_limit_bytes=60 * 1024 * 1024),
    )(*[v[0] for v in inputs.values()])
    return dict(zip(outs, result))


def close_shards(*arrays):
    feats, centres, counts, cotangent = arrays[:4]
    mp_count = lax.axis_size("mp")
    mp_index = lax.axis_index("mp")
    share = feats.shape[0] // mp_count
    clouds = share // PAD
    inner = arrays[6].shape[1] * mp_count
    params = {}
    for k, kind in enumerate(SHAPES):
        for i, name in enumerate(PIECES):
            array = arrays[4 + 8 * k + i]
            if name in ("out", "down"):
                array = array.T
            params[name + "_" + kind] = array
    mine = lax.dynamic_slice_in_dim(centres, mp_index * share, share, 1).T.reshape(clouds, PAD, 3)
    points = jnp.pad(mine, ((0, 0), (0, SLOT - PAD), (0, 0)))
    points = jnp.concatenate((points, jnp.ones((clouds, SLOT, 1), f32)), axis=2)
    points = jnp.pad(points.reshape(clouds * SLOT, 4), ((0, 0), (0, 4)))
    block, grad, own, small, sums = main_call(mp_count, inner, counts, feats, cotangent, points, params)
    out = update_call(block, grad, own, small, sums, params)
    outputs = [out["block_out"], out["feats_out"], out["clip_out"][0, 0], out["trust_out"]]
    for name in PIECES:
        for kind, _ in OUT_KINDS:
            array = out[name + "_out_" + kind]
            if name in ("out", "down"):
                array = array.T
            outputs.append(array)
    return tuple(outputs)


def solution(mesh):
    qkv, outw, upw, bias, whole = P(None, "dp", "mp"), P("mp", "dp"), P("dp", "mp"), P("mp"), P()
    params = (qkv, outw, upw, bias, outw, whole, whole, whole)
    in_specs = (P("dp", None), P(None, "dp"), P("dp"), P("dp", None)) + params * 3
    rows = P(("dp", "mp"), None)
    out_specs = (rows, rows, P(), P()) + tuple(spec for spec in params for _ in range(5))
    form = close_shards if (mesh.shape["dp"], mesh.shape["mp"]) == (8, 4) else shards
    return jax.shard_map(form, mesh=mesh, in_specs=in_specs, out_specs=out_specs, check_vma=False)
```
